32 devices in a mesh: groups: 2 (over y), ctx: 8 (over z, core), rows: 2 (over x).
Axes of the slice: x: 2, y: 2, z: 4, core: 2. Of those that a mesh axis runs over, the one named last changes fastest.
Arguments:
- queries: bfloat16 [64, 4, 8192], P(('groups', 'ctx'), None, 'rows'), parts along dimension 0, may hold values from -34 to 34
- selected: int32 [64, 4, 16], P(('groups', 'ctx')), parts along dimension 0, may hold values from 0 to 31, all different within a row; in each aligned block of 16 rows (0 to 15, 16 to 31, ..., all dimensions but the last counted through in order) at most 16 rows name the same one
- placement: int32 [64], P('groups'), parts along dimension 0, may hold values from 0 to 31, each once
- lengths: int32 [64], P(('groups', 'ctx')), parts along dimension 0, may hold values from 1 to 125, as said below
- cache_k: bfloat16 [64, 1024, 1024], P(('groups', 'ctx'), None, 'rows'), parts along dimension 0, may hold values from -10 to 10
- cache_v: bfloat16 [64, 1024, 1024], P(('groups', 'ctx'), None, 'rows'), parts along dimension 0, may hold values from -12 to 12
- suffix_k: bfloat16 [64, 128, 1024], P(('groups', 'ctx'), None, 'rows'), parts along dimension 0, may hold values from -12 to 12
- suffix_v: bfloat16 [64, 128, 1024], P(('groups', 'ctx'), None, 'rows'), parts along dimension 0, may hold values from -12 to 12
Outputs:
- attended: bfloat16 [64, 4, 8192], P(('groups', 'ctx'), None, 'rows'), parts along dimension 0
The draws below stay inside these ranges and needn't reach their ends.
There are 2 independent parts, one for each index of `groups`. The reference program is written for one: setup_inputs(seed, part) draws one part's arguments, and reference() takes and returns one part's arrays. A program takes and returns all parts, laid end to end along the dimension named above; each array names one. Nothing has to cross between parts.
Inputs may be any that keep to these rules, and one draw needn't show every extreme that they name: `selected`: each row and step lists 16 different block ids. Over the 4 rows of one device and all 4 steps together no block id is listed more than 16 times, and some block id is listed exactly 16 times. A permutation: block id b is stored at cache index placement[b]. At step t the first lengths[r] + t suffix slots of row r are valid; some row has exactly 125.
All inputs are finite; a program needn't handle non-finite values.
Results may differ from the reference program's by a relative error of at most 0.0041.
Values may be sent and summed in bfloat16 or wider, within the bound.
No kernel may reach another device: no remote copies, remote signals or barrier semaphores. Data moves between devices by JAX's collectives and lax.ppermute only.
A program may use at most 64 MiB of HBM per device.

```python
import math
import jax
import jax.numpy as jnp
import numpy as np
from jax import lax

H = 64
KVH = 8
HD = 128
BLOCK = 1024
TOP = 16
STEPS = 4
SUF = 128
ROWS_DEV = 4
BLOCKS = 32
ROWS = 32
MOST = 16


def draw_queries(key, part):
    key = jax.random.fold_in(key, 1)
    noise_key = jax.random.fold_in(key, 0)
    drawn = jnp.clip(1.7 * jax.random.normal(noise_key, (ROWS, STEPS, H, HD), jnp.float32), -10.0, 10.0)
    return drawn.reshape(ROWS, STEPS, H * HD).astype(jnp.bfloat16)


def draw_cache_k(key, part):
    key = jax.random.fold_in(key, 2)
    drawn = jnp.clip(1.7 * jax.random.normal(key, (BLOCKS, BLOCK, KVH, HD), jnp.float32), -10.0, 10.0)
    return drawn.reshape(BLOCKS, BLOCK, KVH * HD).astype(jnp.bfloat16)


def draw_suffix_k(key, part):
    key = jax.random.fold_in(key, 3)
    drawn = jnp.clip(2.5 * jax.random.normal(key, (ROWS, SUF, KVH, HD), jnp.float32), -12.0, 12.0)
    return drawn.reshape(ROWS, SUF, KVH * HD).astype(jnp.bfloat16)


def draw_lengths(key, part):
    key = jax.random.fold_in(key, 4)
    length_key, pick_key = jax.random.split(key)
    drawn = jax.random.randint(length_key, (ROWS,), 1, SUF - STEPS + 2, dtype=jnp.int32)
    longest = jax.random.randint(pick_key, (), 0, ROWS, dtype=jnp.int32)
    return drawn.at[longest].set(SUF - STEPS + 1).astype(jnp.int32)


def block_scale(key, dims, cuts, low, high):
    def one(dim, blocks):
        heights = jax.random.uniform(jax.random.fold_in(jax.random.fold_in(key, 6), dim), (blocks,), jnp.float32, low / len(cuts), high / len(cuts))
        return jnp.repeat(jnp.exp(heights), dims[dim] // blocks).reshape((-1,) + (1,) * (len(dims) - dim - 1))

    factor_of = one(*cuts[0])
    for cut in cuts[1:]:
        factor_of = factor_of * one(*cut)
    return factor_of


def deal_out(stream_key, own, number, rows, amount, top, reach, skew):
    order = jax.random.permutation(stream_key, amount)
    heavy_load, common = portions_of(amount, rows * top, reach, skew, True), portions_of(amount, rows * top, reach, skew, False)
    places = jnp.arange(amount)

    def named(sizes, turn):
        used = int((sizes > 0).sum())
        fixed = max(1, used // 4)
        moved = fixed + (places - fixed + turn * (used - fixed)) % max(1, amount - fixed)
        return jnp.zeros((amount,), jnp.int32).at[order[jnp.where(places < fixed, places, moved)]].set(jnp.asarray(sizes, jnp.int32))

    sizes = jnp.where(number % 4 == 0, named(heavy_load, number // 4), named(common, number - number // 4 - 1))
    mixed = jax.random.permutation(jax.random.fold_in(own, 3), amount)
    giver, receiver = mixed[0:amount // 2 * 2:2], mixed[1:amount // 2 * 2:2]
    slack = jnp.minimum(sizes[giver] - 1, reach - sizes[receiver]) // 2
    slack = jnp.where((giver == order[0]) | (receiver == order[0]) | (sizes[receiver] == 0), 0, jnp.maximum(slack, 0))
    moved = jax.random.randint(jax.random.fold_in(own, 4), (amount // 2,), 0, 1 << 20) % (slack + 1)
    sizes = sizes.at[giver].add(-moved).at[receiver].add(moved)
    labels = jnp.searchsorted(jnp.cumsum(sizes), jnp.arange(rows * top), side="right").astype(jnp.int32)
    table = labels.reshape(top, rows).T
    table = table[jax.random.permutation(jax.random.fold_in(own, 1), rows)]
    turn = jax.random.randint(jax.random.fold_in(own, 2), (rows, 1), 0, top)
    return jnp.take_along_axis(table, (jnp.arange(top)[None, :] + turn) % top, axis=1)


def portions_of(count, total, most, skew, full):
    weights = [(1 << 20) // math.isqrt(grade ** skew) + 1 for grade in range(1, count + 1)]
    largest = most if full else min(most, max(-(-total // count), total * weights[0] // sum(weights)))
    least = 1 if total - largest >= count - 1 else 0
    given, rest = [largest] + [least] * (count - 1), total - largest - least * (count - 1)
    while rest > 0:
        candidates = [i for i in range(1, count) if given[i] < largest] or [i for i in range(1, count) if given[i] < most]
        whole, budget = sum([weights[i] for i in candidates]), rest
        for i in candidates:
            extra = min(most - given[i], max(1, budget * weights[i] // whole), rest)
            given[i] = given[i] + extra
            rest = rest - extra
    return np.array(given)


def gaussian(rng, shape, width, bound, pieces=(), kind=jnp.bfloat16):
    values = width * jax.random.normal(rng, shape, jnp.float32)
    if pieces:
        values = values * block_scale(rng, shape, pieces, -0.22, 0.18)
    return jnp.clip(values, -bound, bound).astype(kind)


def setup_inputs(seed: int = 0, part: int = 0) -> dict:
    splits = jax.random.split(jax.random.key(seed), 9)
    own_keys = jax.random.split(jax.random.fold_in(splits[8], part), 9)
    queries = draw_queries(jax.random.fold_in(jax.random.fold_in(splits[8], part), 71), part)
    selected_keys = jax.random.split(jax.random.fold_in(own_keys[1], 1), ROWS * STEPS // (ROWS_DEV * STEPS))
    selected_turns = jax.random.permutation(jax.random.fold_in(own_keys[1], 3), ROWS * STEPS // (ROWS_DEV * STEPS))
    selected = jax.vmap(lambda own, number: deal_out(jax.random.fold_in(own_keys[1], 2), own, number, ROWS_DEV * STEPS, BLOCKS, TOP, MOST, 2))(selected_keys, selected_turns).reshape((ROWS, STEPS, TOP))
    placement = jax.random.permutation(own_keys[2], BLOCKS).astype(jnp.int32)
    lengths = draw_lengths(jax.random.fold_in(jax.random.fold_in(splits[8], part), 71), part)
    cache_k = draw_cache_k(jax.random.fold_in(jax.random.fold_in(splits[8], part), 71), part)
    cache_v = gaussian(own_keys[5], (BLOCKS, BLOCK, KVH * HD), 2.0, 12.0, ((0, 8), (2, 2)))
    suffix_k = draw_suffix_k(jax.random.fold_in(jax.random.fold_in(splits[8], part), 71), part)
    suffix_v = gaussian(own_keys[7], (ROWS, SUF, KVH * HD), 2.0, 12.0, ((0, 8), (2, 2)))
    return {"queries": queries, "selected": selected, "placement": placement, "lengths": lengths, "cache_k": cache_k, "cache_v": cache_v, "suffix_k": suffix_k, "suffix_v": suffix_v}


def partial_attend(query_row, key_rows, value_rows, visible):
    grouped = query_row.astype(jnp.float32).reshape(KVH, H // KVH, HD)
    key_heads = key_rows.astype(jnp.float32).reshape(-1, KVH, HD)
    value_heads = value_rows.astype(jnp.float32).reshape(-1, KVH, HD)
    scores = jnp.einsum('ghd,tgd->ght', grouped, key_heads) * (1.0 / math.sqrt(HD))
    scores = jnp.where(visible[None, None, :], scores, -jnp.inf)
    highest = lax.optimization_barrier(jnp.max(scores, axis=-1, keepdims=True))
    exponent = jnp.exp(scores - highest)
    totals = lax.optimization_barrier(jnp.sum(exponent, axis=-1, keepdims=True))
    weights = lax.optimization_barrier(exponent.astype(jnp.bfloat16)).astype(jnp.float32)
    weighted = jnp.einsum('ght,tgd->ghd', weights, value_heads) / totals
    return (weighted.reshape(H, HD), (highest + jnp.log(totals)).reshape(H))

def reference(queries, selected, placement, lengths, cache_k, cache_v, suffix_k, suffix_v):
    flat_queries = queries.reshape(ROWS * STEPS, H * HD)
    flat_selected = selected.reshape(ROWS * STEPS, TOP)
    row_owners = jnp.repeat(jnp.arange(ROWS, dtype=jnp.int32), STEPS)
    row_limits = (jnp.repeat(lengths, STEPS) + jnp.tile(jnp.arange(STEPS, dtype=jnp.int32), ROWS)).astype(jnp.int32)
    everywhere = jnp.ones((BLOCK,), dtype=jnp.bool_)

    def one_item(packed_item):
        query_row, chosen, row_owner, row_limit = packed_item
        stored = placement[chosen]
        block_keys = cache_k[stored]
        block_values = cache_v[stored]

        def one_block(key_rows, value_rows):
            return partial_attend(query_row, key_rows, value_rows, everywhere)
        block_out, block_log = jax.vmap(one_block)(block_keys, block_values)
        block_out = lax.optimization_barrier(block_out.astype(jnp.bfloat16)).astype(jnp.float32)
        visible = jnp.arange(SUF, dtype=jnp.int32) < row_limit
        suffix_out, suffix_log = partial_attend(query_row, suffix_k[row_owner], suffix_v[row_owner], visible)
        parts_out = jnp.concatenate([block_out, suffix_out[None]], axis=0)
        parts_log = jnp.concatenate([block_log, suffix_log[None]], axis=0)
        largest = lax.optimization_barrier(jnp.max(parts_log, axis=0, keepdims=True))
        factors = jnp.exp(parts_log - largest)
        merged = lax.optimization_barrier(jnp.sum(factors[..., None] * parts_out, axis=0)) / lax.optimization_barrier(jnp.sum(factors, axis=0))[..., None]
        return merged.reshape(H * HD).astype(jnp.bfloat16)
    attended = lax.map(one_item, (flat_queries, flat_selected, row_owners, row_limits))
    return attended.reshape(ROWS, STEPS, H * HD)
```

```python
import functools
import math

import jax
import jax.numpy as jnp
from jax import lax
from jax.experimental import pallas as pl
from jax.experimental.pallas import tpu as pltpu
from jax.sharding import PartitionSpec as P

HD = 128
LANES = 128
SCALE = 1.0 / math.sqrt(HD)
LOG2E = math.log2(math.e)
NONE = -1e30
VMEM = 56 * 1024 * 1024


def split3(x):
    high = x.astype(jnp.bfloat16)
    rest = x - high.astype(jnp.float32)
    middle = rest.astype(jnp.bfloat16)
    low = (rest - middle.astype(jnp.float32)).astype(jnp.bfloat16)
    return high, middle, low


def dot_nt(a, b):
    return lax.dot_general(a, b, (((1,), (1,)), ((), ())), preferred_element_type=jnp.float32)


def block_kernel(heads_step, group_size, targets, q_ref, ids_ref, k_ref, v_ref, out_ref, logs_ref, s_ref):
    kv = pl.program_id(1)
    items = q_ref.shape[0]
    blocks = k_ref.shape[0]
    rows = heads_step * items
    lane = lax.broadcasted_iota(jnp.int32, (items, LANES), 1)
    ids = ids_ref[...].astype(jnp.float32)
    listed = []
    for b in range(blocks):
        target = targets[b].astype(jnp.float32)
        hit = jnp.max(jnp.where(ids == target, 1.0, 0.0), axis=1, keepdims=True)
        listed.append(jnp.concatenate([hit] * heads_step, axis=0))
    logs = jnp.where(kv == 0, jnp.zeros((items, LANES), jnp.float32), logs_ref[...])
    for first in range(0, group_size, heads_step):
        q = jnp.concatenate(
            [q_ref[:, h * HD : (h + 1) * HD] for h in range(first, first + heads_step)], axis=0
        )
        top = jnp.full((rows, LANES), NONE, jnp.float32)
        for b in range(blocks):
            s = dot_nt(q, k_ref[b])
            s_ref[b] = s
            here = s[:, :LANES]
            for t in range(1, s.shape[1] // LANES):
                here = jnp.maximum(here, s[:, t * LANES : (t + 1) * LANES])
            top = jnp.maximum(top, jnp.where(listed[b] > 0.0, here, NONE))
        highest = jnp.max(top, axis=1, keepdims=True)
        shift = highest * (SCALE * LOG2E)
        acc = jnp.zeros((rows, HD), jnp.float32)
        total = jnp.zeros((rows, LANES), jnp.float32)
        for b in range(blocks):
            off = jnp.where(listed[b] > 0.0, shift, -NONE)
            p = jnp.exp2(s_ref[b] * (SCALE * LOG2E) - off)
            for t in range(p.shape[1] // LANES):
                total += p[:, t * LANES : (t + 1) * LANES]
            acc += jnp.dot(p.astype(jnp.bfloat16), v_ref[b], preferred_element_type=jnp.float32)
        total = jnp.sum(total, axis=1, keepdims=True)
        some = total > 0.0
        out = jnp.where(some, acc / jnp.where(some, total, 1.0), 0.0).astype(jnp.bfloat16)
        log = jnp.where(some, highest * SCALE + jnp.log(jnp.where(some, total, 1.0)), NONE)
        for n in range(heads_step):
            head = kv * group_size + first + n
            start = pl.multiple_of(head * HD, HD)
            out_ref[:, pl.ds(start, HD)] = out[n * items : (n + 1) * items]
            logs = jnp.where(lane == head, log[n * items : (n + 1) * items], logs)
    logs_ref[...] = logs

    @pl.when(kv == pl.num_programs(1) - 1)
    def _():
        heads = (out_ref.shape[1] - LANES) // HD
        high, middle, low = split3(logs)
        parts = jnp.concatenate([high[:, :heads], middle[:, :heads], low[:, :heads]], axis=1)
        pad = jnp.zeros((items, LANES - 3 * heads), jnp.bfloat16)
        out_ref[:, heads * HD :] = jnp.concatenate([parts, pad], axis=1)


def attend_blocks(targets, payload, cache_k, cache_v, width):
    items_all = payload.shape[0]
    blocks, tokens, kv_width = cache_k.shape
    kv_here = kv_width // HD
    group_size = width // kv_width
    items = min(items_all, 128)
    heads_step = 2
    return pl.pallas_call(
        functools.partial(block_kernel, heads_step, group_size),
        grid_spec=pltpu.PrefetchScalarGridSpec(
            num_scalar_prefetch=1,
            grid=(items_all // items, kv_here),
            in_specs=[
                pl.BlockSpec((items, group_size * HD), lambda i, g, t: (i, g)),
                pl.BlockSpec((items, LANES), lambda i, g, t: (i, width // LANES)),
                pl.BlockSpec((blocks, tokens, HD), lambda i, g, t: (0, 0, g)),
                pl.BlockSpec((blocks, tokens, HD), lambda i, g, t: (0, 0, g)),
            ],
            out_specs=pl.BlockSpec((items, width + LANES), lambda i, g, t: (i, 0)),
            scratch_shapes=[
                pltpu.VMEM((items, LANES), jnp.float32),
                pltpu.VMEM((blocks, heads_step * items, tokens), jnp.float32),
            ],
        ),
        out_shape=jax.ShapeDtypeStruct((items_all, width + LANES), jnp.bfloat16),
        compiler_params=pltpu.CompilerParams(vmem_limit_bytes=VMEM),
        cost_estimate=pl.CostEstimate(
            flops=4 * items_all * blocks * tokens * width,
            bytes_accessed=4 * blocks * tokens * kv_width + 4 * items_all * width,
            transcendentals=items_all * blocks * tokens * width // HD,
        ),
    )(targets, payload, payload, cache_k, cache_v)


def suffix_kernel(kv_here, group_size, steps, q_ref, limit_ref, k_ref, v_ref, out_ref, log_ref):
    items = q_ref.shape[0]
    rows_here, tokens, _ = k_ref.shape
    span = rows_here * tokens
    row = group_size * items
    lane = lax.broadcasted_iota(jnp.int32, (items, LANES), 1)
    token = lax.broadcasted_iota(jnp.int32, (items, span), 1)
    item = lax.broadcasted_iota(jnp.int32, (items, span), 0)
    offset = token - (item // steps) * tokens
    seen = jnp.where((offset >= 0) & (offset < limit_ref[...]), 1.0, 0.0)
    seen = jnp.concatenate([seen] * group_size, axis=0)
    logs = jnp.zeros((items, LANES), jnp.float32)
    for g in range(kv_here):
        first = g * group_size
        q = jnp.concatenate(
            [q_ref[:, h * HD : (h + 1) * HD] for h in range(first, first + group_size)], axis=0
        )
        keys = k_ref[:, :, g * HD : (g + 1) * HD].reshape(span, HD)
        values = v_ref[:, :, g * HD : (g + 1) * HD].reshape(span, HD)
        s = jnp.where(seen > 0.0, dot_nt(q, keys), NONE)
        highest = jnp.max(s, axis=1, keepdims=True)
        p = jnp.exp2((s - highest) * (SCALE * LOG2E))
        p = jnp.where(seen > 0.0, p, 0.0)
        total = jnp.sum(p, axis=1, keepdims=True)
        out = jnp.dot(p.astype(jnp.bfloat16), values, preferred_element_type=jnp.float32) / total
        log = highest * SCALE + jnp.log(total)
        for n in range(group_size):
            h = first + n
            out_ref[:, h * HD : (h + 1) * HD] = out[n * items : (n + 1) * items]
            logs = jnp.where(lane == h, log[n * items : (n + 1) * items], logs)
    log_ref[...] = logs


def attend_suffix(queries, limits, suffix_k, suffix_v, steps):
    items, width = queries.shape
    kv_width = suffix_k.shape[2]
    return pl.pallas_call(
        functools.partial(suffix_kernel, kv_width // HD, width // kv_width, steps),
        out_shape=(
            jax.ShapeDtypeStruct((items, width), jnp.float32),
            jax.ShapeDtypeStruct((items, LANES), jnp.float32),
        ),
        compiler_params=pltpu.CompilerParams(vmem_limit_bytes=VMEM),
    )(queries, limits, suffix_k, suffix_v)


def merge_kernel(parts, items, back_ref, out_s_ref, log_s_ref, out_ref):
    heads = out_s_ref.shape[1] // HD
    width = heads * HD

    def log_of(part):
        return back_ref[pl.ds(pl.multiple_of(part * items, items), items), width:].astype(jnp.float32)

    def whole(x):
        x = x[:, : 3 * heads]
        return x[:, :heads] + x[:, heads : 2 * heads] + x[:, 2 * heads :]

    logs = [whole(log_of(part)) for part in range(parts)]
    log_s = log_s_ref[:, :heads]
    top = log_s
    for log in logs:
        top = jnp.maximum(top, log)
    factor_s = jnp.exp(log_s - top)
    factors = [jnp.exp(log - top) for log in logs]
    total = factor_s
    for factor in factors:
        total += factor
    inverse = 1.0 / total
    factor_s = factor_s * inverse
    factors = [factor * inverse for factor in factors]
    for h in range(heads):
        columns = slice(h * HD, (h + 1) * HD)
        acc = factor_s[:, h : h + 1] * out_s_ref[:, columns]
        for part in range(parts):
            value = back_ref[part * items : (part + 1) * items, columns].astype(jnp.float32)
            acc += factors[part][:, h : h + 1] * value
        out_ref[:, columns] = acc.astype(jnp.bfloat16)


def merge(back, out_s, log_s, parts):
    items, width = out_s.shape
    return pl.pallas_call(
        functools.partial(merge_kernel, parts, items),
        out_shape=jax.ShapeDtypeStruct((items, width), jnp.bfloat16),
        compiler_params=pltpu.CompilerParams(vmem_limit_bytes=VMEM),
    )(back, out_s, log_s)


def local(queries, selected, placement, lengths, cache_k, cache_v, suffix_k, suffix_v):
    rows_here, steps, width = queries.shape
    listed = selected.shape[2]
    parts = lax.axis_size("ctx")
    blocks_here = cache_k.shape[0]
    items = rows_here * steps
    own = lax.axis_index("ctx")
    flat_queries = queries.reshape(items, width)
    ids = jnp.pad(
        selected.reshape(items, listed).astype(jnp.bfloat16),
        ((0, 0), (0, LANES - listed)),
        constant_values=-1,
    )
    payload = lax.all_gather(
        jnp.concatenate([flat_queries, ids], axis=1), "ctx", axis=0, tiled=True
    )
    cache_index = own * blocks_here + jnp.arange(blocks_here, dtype=jnp.int32)
    block_ids = jnp.arange(placement.shape[0], dtype=jnp.int32)
    targets = jnp.sum(
        jnp.where(placement[None, :] == cache_index[:, None], block_ids[None, :], 0), axis=1
    )
    limits = (lengths[:, None] + jnp.arange(steps, dtype=jnp.int32)[None, :]).reshape(items, 1)
    out_s, log_s = attend_suffix(flat_queries, limits, suffix_k, suffix_v, steps)
    partial = attend_blocks(targets, payload, cache_k, cache_v, width)
    back = lax.all_to_all(partial, "ctx", split_axis=0, concat_axis=0, tiled=True)
    merged = merge(back, out_s, log_s, parts)
    return merged.reshape(rows_here, steps, width)


def solution(mesh):
    rows = P(("groups", "ctx"), None, "rows")
    in_specs = (
        rows,
        P(("groups", "ctx"), None, None),
        P("groups"),
        P(("groups", "ctx")),
        rows,
        rows,
        rows,
        rows,
    )
    return jax.shard_map(local, mesh=mesh, in_specs=in_specs, out_specs=rows, check_vma=False)
```

```python
import functools
import math

import jax
import jax.numpy as jnp
from jax import lax
from jax.experimental import pallas as pl
from jax.experimental.pallas import tpu as pltpu
from jax.sharding import PartitionSpec as P

HD = 128
LANES = 128
SCALE = 1.0 / math.sqrt(HD)
LOG2E = math.log2(math.e)
NONE = -1e30
LOW, HIGH = 2.0**-80, 2.0**100
VMEM = 56 * 1024 * 1024


def split3(x):
    high = x.astype(jnp.bfloat16)
    rest = x - high.astype(jnp.float32)
    middle = rest.astype(jnp.bfloat16)
    low = (rest - middle.astype(jnp.float32)).astype(jnp.bfloat16)
    return high, middle, low


def dot_nt(a, b):
    return lax.dot_general(a, b, (((1,), (1,)), ((), ())), preferred_element_type=jnp.float32)


def stack(arrays):
    return arrays[0] if len(arrays) == 1 else jnp.concatenate(arrays, axis=0)


def params():
    return pltpu.CompilerParams(vmem_limit_bytes=VMEM)


def pack_kernel(chunks, q_ref, selected_ref, *out_refs):
    rows, steps, width = q_ref.shape
    items = rows * steps
    columns = width // chunks
    for c in range(chunks):
        part = q_ref[:, :, c * columns : (c + 1) * columns].astype(jnp.float32)
        out_refs[c][:, :columns] = part.reshape(items, columns).astype(jnp.bfloat16)
    ids = selected_ref[...].astype(jnp.float32).reshape(items, -1)
    pad = jnp.full((items, LANES - ids.shape[1]), -1.0, jnp.float32)
    out_refs[0][:, columns:] = jnp.concatenate([ids, pad], axis=1).astype(jnp.bfloat16)


def pack(queries, selected, chunks):
    rows, steps, width = queries.shape
    columns = width // chunks
    return pl.pallas_call(
        functools.partial(pack_kernel, chunks),
        out_shape=[
            jax.ShapeDtypeStruct((rows * steps, columns + (LANES if c == 0 else 0)), jnp.bfloat16)
            for c in range(chunks)
        ],
        compiler_params=params(),
    )(queries, selected)


def block_kernel(pieces, group_size, base_ref, place_ref, *refs):
    q_refs = refs[:pieces]
    id_refs = refs[pieces : 2 * pieces]
    k_ref, v_ref = refs[2 * pieces : 2 * pieces + 2]
    out_refs = refs[2 * pieces + 2 : 3 * pieces + 2]
    logs_ref, s_ref = refs[3 * pieces + 2 :]
    kv = pl.program_id(1)
    share = q_refs[0].shape[0]
    items = share * pieces
    blocks = k_ref.shape[0]
    tokens = k_ref.shape[1]
    lane = lax.broadcasted_iota(jnp.int32, (items, LANES), 1)
    first_head = kv * group_size
    mine = (lane >= first_head) & (lane < first_head + group_size)
    ids = stack([ref[...].astype(jnp.float32) for ref in id_refs])
    place = place_ref[...]
    block_ids = lax.broadcasted_iota(jnp.int32, place.shape, 1)
    hits = []
    for b in range(blocks):
        target = jnp.sum(
            jnp.where(place == base_ref[0] + b, block_ids, 0).astype(jnp.float32), axis=1, keepdims=True
        )
        hits.append(jnp.max(jnp.where(ids == target, 1.0, 0.0), axis=1, keepdims=True))
    some = hits[0]
    for hit in hits[1:]:
        some = jnp.maximum(some, hit)

    def write(head, out):
        start = pl.multiple_of((first_head + head) * HD, HD)
        out = out.astype(jnp.bfloat16)
        for n, ref in enumerate(out_refs):
            ref[:, pl.ds(start, HD)] = out[n * share : (n + 1) * share]

    step = 2
    ones = jnp.ones((tokens, LANES), jnp.bfloat16)
    totals = jnp.ones((items, LANES), jnp.float32)
    for first in range(0, group_size, step):
        q = stack(
            [ref[:, h * HD : (h + 1) * HD] for h in range(first, first + step) for ref in q_refs]
        )
        acc = jnp.zeros((step * items, HD + LANES), jnp.float32)
        for b in range(blocks):
            p = jnp.exp2(dot_nt(q, k_ref[b]) * (SCALE * LOG2E)).astype(jnp.bfloat16)
            values = jnp.concatenate([v_ref[b], ones], axis=1)
            here = jnp.dot(p, values, preferred_element_type=jnp.float32)
            hit = stack([hits[b]] * step)
            acc = jnp.where(hit > 0.0, acc + here, acc)
        for n in range(step):
            total = acc[n * items : (n + 1) * items, HD:]
            out = acc[n * items : (n + 1) * items, :HD]
            write(first + n, jnp.where(some > 0.0, out / jnp.where(some > 0.0, total, 1.0), 0.0))
            totals = jnp.where(lane == first_head + first + n, total, totals)
    good = (totals > LOW) & (totals < HIGH)
    bad = jnp.max(jnp.where(good | (some == 0.0), 0.0, 1.0))
    logs = jnp.where((some > 0.0) & good, jnp.log(jnp.where(good, totals, 1.0)), NONE)
    logs_ref[...] = jnp.where(mine, logs, logs_ref[...])

    @pl.when(bad > 0.0)
    def _():
        @pl.loop(0, group_size)
        def _(head):
            start = pl.multiple_of(head * HD, HD)
            q = stack([ref[:, pl.ds(start, HD)] for ref in q_refs])
            top = jnp.full((items, 1), NONE, jnp.float32)
            for b in range(blocks):
                s = dot_nt(q, k_ref[b])
                s_ref[b] = s
                here = jnp.max(s, axis=1, keepdims=True)
                top = jnp.where(hits[b] > 0.0, jnp.maximum(top, here), top)
            acc = jnp.zeros((items, HD), jnp.float32)
            total = jnp.zeros((items, 1), jnp.float32)
            for b in range(blocks):
                p = jnp.exp2((s_ref[b] - top) * (SCALE * LOG2E))
                p = jnp.where(hits[b] > 0.0, p, 0.0)
                total += jnp.sum(p, axis=1, keepdims=True)
                acc += jnp.dot(p.astype(jnp.bfloat16), v_ref[b], preferred_element_type=jnp.float32)
            safe = jnp.where(some > 0.0, total, 1.0)
            write(head, jnp.where(some > 0.0, acc / safe, 0.0))
            log = jnp.where(some > 0.0, top * SCALE + jnp.log(safe), NONE)
            logs_ref[...] = jnp.where(lane == first_head + head, log, logs_ref[...])

    @pl.when(kv == pl.num_programs(1) - 1)
    def _():
        heads = (out_refs[0].shape[1] - LANES) // HD
        parts = jnp.concatenate([x[:, :heads] for x in split3(logs_ref[...])], axis=1)
        pad = jnp.zeros((items, LANES - 3 * heads), jnp.bfloat16)
        both = jnp.concatenate([parts, pad], axis=1)
        for n, ref in enumerate(out_refs):
            ref[:, heads * HD :] = both[n * share : (n + 1) * share]


def attend_blocks(chunk, base, place, queries, ids, cache_k, cache_v, group_size, kv_chunk):
    pieces = len(queries)
    rows = queries[0].shape[0]
    blocks, tokens, _ = cache_k.shape
    columns = kv_chunk * group_size * HD
    id_block = ids[0].shape[1] // LANES - 1
    share = min(rows, 128)
    items = share * pieces
    out_columns = columns + LANES
    return pl.pallas_call(
        functools.partial(block_kernel, pieces, group_size),
        grid_spec=pltpu.PrefetchScalarGridSpec(
            num_scalar_prefetch=1,
            grid=(rows // share, kv_chunk),
            in_specs=[pl.BlockSpec(place.shape, lambda i, g, t: (0, 0))]
            + [pl.BlockSpec((share, group_size * HD), lambda i, g, t: (i, g))] * pieces
            + [pl.BlockSpec((share, LANES), lambda i, g, t: (i, id_block))] * pieces
            + [pl.BlockSpec((blocks, tokens, HD), lambda i, g, t: (0, 0, chunk * kv_chunk + g))] * 2,
            out_specs=[pl.BlockSpec((share, out_columns), lambda i, g, t: (i, 0))] * pieces,
            scratch_shapes=[
                pltpu.VMEM((items, LANES), jnp.float32),
                pltpu.VMEM((blocks, items, tokens), jnp.float32),
            ],
        ),
        out_shape=[jax.ShapeDtypeStruct((rows, out_columns), jnp.bfloat16)] * pieces,
        compiler_params=params(),
        cost_estimate=pl.CostEstimate(
            flops=8 * rows * pieces * blocks * tokens * columns,
            bytes_accessed=4 * blocks * tokens * kv_chunk * HD + 4 * rows * pieces * columns,
            transcendentals=rows * pieces * blocks * tokens * columns // HD,
        ),
    )(base, place, *queries, *ids, cache_k, cache_v)


def suffix_kernel(kv_here, group_size, steps, *refs):
    chunks = len(refs) - 5
    q_refs = refs[:chunks]
    limit_ref, k_ref, v_ref, out_ref, log_ref = refs[chunks:]
    items = limit_ref.shape[0]
    rows_here, tokens, _ = k_ref.shape
    span = rows_here * tokens
    lane = lax.broadcasted_iota(jnp.int32, (items, LANES), 1)
    token = lax.broadcasted_iota(jnp.int32, (items, span), 1)
    item = lax.broadcasted_iota(jnp.int32, (items, span), 0)
    offset = token - (item // steps) * tokens
    seen = jnp.where((offset >= 0) & (offset < limit_ref[...]), 1.0, 0.0)
    seen = jnp.concatenate([seen] * group_size, axis=0)
    logs = jnp.zeros((items, LANES), jnp.float32)
    kv_chunk = kv_here // chunks
    for g in range(kv_here):
        q_ref = q_refs[g // kv_chunk]
        first = (g % kv_chunk) * group_size
        q = stack([q_ref[:, h * HD : (h + 1) * HD] for h in range(first, first + group_size)])
        keys = k_ref[:, :, g * HD : (g + 1) * HD].reshape(span, HD)
        values = v_ref[:, :, g * HD : (g + 1) * HD].reshape(span, HD)
        s = jnp.where(seen > 0.0, dot_nt(q, keys), NONE)
        highest = jnp.max(s, axis=1, keepdims=True)
        p = jnp.exp2((s - highest) * (SCALE * LOG2E))
        p = jnp.where(seen > 0.0, p, 0.0)
        total = jnp.sum(p, axis=1, keepdims=True)
        out = jnp.dot(p.astype(jnp.bfloat16), values, preferred_element_type=jnp.float32) / total
        log = highest * SCALE + jnp.log(total)
        for n in range(group_size):
            h = g * group_size + n
            out_ref[:, h * HD : (h + 1) * HD] = out[n * items : (n + 1) * items]
            logs = jnp.where(lane == h, log[n * items : (n + 1) * items], logs)
    log_ref[...] = logs


def attend_suffix(queries, limits, suffix_k, suffix_v, steps, group_size):
    items = queries[0].shape[0]
    rows, tokens, kv_width = suffix_k.shape
    width = kv_width * group_size
    return pl.pallas_call(
        functools.partial(suffix_kernel, kv_width // HD, group_size, steps),
        out_shape=(
            jax.ShapeDtypeStruct((items, width), jnp.float32),
            jax.ShapeDtypeStruct((items, LANES), jnp.float32),
        ),
        compiler_params=params(),
        cost_estimate=pl.CostEstimate(
            flops=16 * items * rows * tokens * width,
            bytes_accessed=4 * suffix_k.size + 6 * items * width,
            transcendentals=items * rows * tokens * width // HD,
        ),
    )(*queries, limits, suffix_k, suffix_v)


def merge_kernel(steps, chunk, arrays, *refs):
    back_refs = refs[:arrays]
    out_s_ref, log_s_ref = refs[arrays : arrays + 2]
    out_ref = refs[-1]
    items, columns = out_s_ref.shape
    heads = columns // HD
    first = chunk * heads
    parts = [(ref, start) for ref in back_refs for start in range(0, ref.shape[0], items)]
    logs = []
    for ref, start in parts:
        x = ref[start : start + items, columns:].astype(jnp.float32)
        logs.append(x[:, :heads] + x[:, heads : 2 * heads] + x[:, 2 * heads : 3 * heads])
    log_s = log_s_ref[:, first : first + heads]
    top = log_s
    for log in logs:
        top = jnp.maximum(top, log)
    factor_s = jnp.exp(log_s - top)
    factors = [jnp.exp(log - top) for log in logs]
    total = factor_s
    for factor in factors:
        total += factor
    inverse = 1.0 / total
    factor_s = factor_s * inverse
    factors = [factor * inverse for factor in factors]
    for h in range(heads):
        span = slice(h * HD, (h + 1) * HD)
        acc = factor_s[:, h : h + 1] * out_s_ref[:, span]
        for factor, (ref, start) in zip(factors, parts):
            acc += factor[:, h : h + 1] * ref[start : start + items, span].astype(jnp.float32)
        for row in range(items // steps):
            out_ref[row, :, span] = acc[row * steps : (row + 1) * steps].astype(jnp.bfloat16)


def merge(chunk, steps, back, out_s, log_s, so_far):
    items, width = out_s.shape
    columns = back[0].shape[1] - LANES
    shape = (items // steps, steps, width)
    others = [] if so_far is None else [so_far]
    return pl.pallas_call(
        functools.partial(merge_kernel, steps, chunk, len(back)),
        grid=(1,),
        in_specs=[pl.BlockSpec(x.shape, lambda i: (0, 0)) for x in back]
        + [pl.BlockSpec((items, columns), lambda i: (0, chunk)), pl.BlockSpec(log_s.shape, lambda i: (0, 0))]
        + [pl.BlockSpec(memory_space=pl.ANY)] * len(others),
        out_specs=pl.BlockSpec((shape[0], steps, columns), lambda i: (0, 0, chunk)),
        out_shape=jax.ShapeDtypeStruct(shape, jnp.bfloat16),
        input_output_aliases={len(back) + 2: 0} if others else {},
        compiler_params=params(),
    )(*back, out_s, log_s, *others)


def swap(x, bits, size):
    return lax.ppermute(x, "ctx", [(i, i ^ bits) for i in range(size)])


def gather(x, size, few):
    if not few:
        return [lax.all_gather(x, "ctx", axis=0, tiled=True)]
    same = {0: x}
    for n in range(2, size, 2):
        same[n] = swap(x, n, size)
    every = dict(same)
    for n in range(0, size, 2):
        every[n ^ 1] = swap(same[n], 1, size)
    return [every[n] for n in range(size)]


def give_back(arrays, size, few):
    if not few:
        return [lax.all_to_all(arrays[0], "ctx", split_axis=0, concat_axis=0, tiled=True)]
    return [x if n == 0 else swap(x, n, size) for n, x in enumerate(arrays)]


def local(queries, selected, placement, lengths, cache_k, cache_v, suffix_k, suffix_v):
    rows_here, steps, width = queries.shape
    size = lax.axis_size("ctx")
    blocks_here, _, kv_width = cache_k.shape
    kv_here = kv_width // HD
    group_size = width // kv_width
    items = rows_here * steps
    few = size <= 8
    chunks = 2
    kv_chunk = kv_here // chunks
    base = (lax.axis_index("ctx") * blocks_here).astype(jnp.int32).reshape(1)
    place = placement.reshape(1, -1)
    limits = (lengths[:, None] + jnp.arange(steps, dtype=jnp.int32)[None, :]).reshape(items, 1)
    packed = pack(queries, selected, chunks)
    gathered = [gather(x, size, few) for x in packed]
    out_s, log_s = attend_suffix(packed, limits, suffix_k, suffix_v, steps, group_size)
    merged = None
    returned = []
    for c in range(chunks):
        partial = attend_blocks(
            c, base, place, gathered[c], gathered[0], cache_k, cache_v, group_size, kv_chunk
        )
        returned.append(give_back(partial, size, few))
    for c in range(chunks):
        merged = merge(c, steps, returned[c], out_s, log_s, merged)
    return merged


def solution(mesh):
    rows = P(("groups", "ctx"), None, "rows")
    in_specs = (
        rows,
        P(("groups", "ctx"), None, None),
        P("groups"),
        P(("groups", "ctx")),
        rows,
        rows,
        rows,
        rows,
    )
    return jax.shard_map(local, mesh=mesh, in_specs=in_specs, out_specs=rows, check_vma=False)
```

```python
import functools
import math

import jax
import jax.numpy as jnp
from jax import lax
from jax.experimental import pallas as pl
from jax.experimental.pallas import tpu as pltpu
from jax.sharding import PartitionSpec as P

HD = 128
LANES = 128
SCALE = 1.0 / math.sqrt(HD)
LOG2E = math.log2(math.e)
NONE = -1e30
LOW, HIGH = 2.0**-80, 2.0**100
VMEM = 56 * 1024 * 1024
ROWS_STEP = 256


def split3(x):
    high = x.astype(jnp.bfloat16)
    rest = x - high.astype(jnp.float32)
    middle = rest.astype(jnp.bfloat16)
    low = (rest - middle.astype(jnp.float32)).astype(jnp.bfloat16)
    return high, middle, low


def dot_nt(a, b):
    return lax.dot_general(a, b, (((1,), (1,)), ((), ())), preferred_element_type=jnp.float32)


def stack(arrays):
    return arrays[0] if len(arrays) == 1 else jnp.concatenate(arrays, axis=0)


def params():
    return pltpu.CompilerParams(vmem_limit_bytes=VMEM)


def flat(x):
    return x.astype(jnp.float32).reshape(x.shape[0] * x.shape[1], x.shape[2])


def pack_kernel(where_ref, q_ref, selected_ref, mine_ref, other_ref):
    half = q_ref.shape[2] // 2
    core = where_ref[2]
    ids = flat(selected_ref[...])
    pad = jnp.full((ids.shape[0], LANES - ids.shape[1]), -1.0, jnp.float32)
    ids = jnp.concatenate([ids, pad], axis=1).astype(jnp.bfloat16)
    for ref, which in ((mine_ref, core), (other_ref, 1 - core)):
        start = pl.multiple_of(which * half, LANES)
        ref[:, :half] = flat(q_ref[:, :, pl.ds(start, half)]).astype(jnp.bfloat16)
        ref[:, half:] = ids


def pack(where, queries, selected):
    rows, steps, width = queries.shape
    shape = jax.ShapeDtypeStruct((rows * steps, width // 2 + LANES), jnp.bfloat16)
    whole = lambda i, w: (0, 0, 0)
    return pl.pallas_call(
        pack_kernel,
        grid_spec=pltpu.PrefetchScalarGridSpec(
            num_scalar_prefetch=1,
            grid=(1,),
            in_specs=[pl.BlockSpec(queries.shape, whole), pl.BlockSpec(selected.shape, whole)],
            out_specs=[pl.BlockSpec(shape.shape, lambda i, w: (0, 0))] * 2,
        ),
        out_shape=[shape, shape],
        compiler_params=params(),
    )(where, queries, selected)


def halve_kernel(blocks, where_ref, k_ref, v_ref, out_ref):
    @pl.when(pl.program_id(0) < blocks)
    def _():
        out_ref[...] = k_ref[...]

    @pl.when(pl.program_id(0) >= blocks)
    def _():
        out_ref[...] = v_ref[...]


def halve(where, cache_k, cache_v):
    blocks, tokens, columns = cache_k.shape
    block = (1, tokens, columns // 2)
    return pl.pallas_call(
        functools.partial(halve_kernel, blocks),
        grid_spec=pltpu.PrefetchScalarGridSpec(
            num_scalar_prefetch=1,
            grid=(2 * blocks,),
            in_specs=[
                pl.BlockSpec(block, lambda i, w: (jnp.minimum(i, blocks - 1), 0, 1 - w[2])),
                pl.BlockSpec(block, lambda i, w: (jnp.maximum(i - blocks, 0), 0, 1 - w[2])),
            ],
            out_specs=pl.BlockSpec(block, lambda i, w: (i, 0, 0)),
        ),
        out_shape=jax.ShapeDtypeStruct((2 * blocks, tokens, columns // 2), jnp.bfloat16),
        compiler_params=params(),
    )(where, cache_k, cache_v)


def block_kernel(pieces, group_size, step, where_ref, place_ref, *refs):
    q_refs = refs[:pieces]
    id_refs = refs[pieces : 2 * pieces]
    own_k, own_v, next_k, next_v = refs[2 * pieces : 2 * pieces + 4]
    out_ref, logs_ref, s_ref = refs[-3:]
    kv = pl.program_id(1)
    share = q_refs[0].shape[0]
    items = share * pieces
    blocks, tokens, _ = own_k.shape
    lane = lax.broadcasted_iota(jnp.int32, (items, LANES), 1)
    first_head = kv * group_size
    mine = (lane >= first_head) & (lane < first_head + group_size)
    ids = stack([ref[...].astype(jnp.float32) for ref in id_refs])
    place = place_ref[...]
    block_ids = lax.broadcasted_iota(jnp.int32, place.shape, 1)
    keys = [ref.at[b] for ref in (own_k, next_k) for b in range(blocks)]
    values = [ref.at[b] for ref in (own_v, next_v) for b in range(blocks)]
    hits = []
    for base in (where_ref[0], where_ref[1]):
        for b in range(blocks):
            target = jnp.sum(
                jnp.where(place == base + b, block_ids, 0).astype(jnp.float32), axis=1, keepdims=True
            )
            hits.append(jnp.max(jnp.where(ids == target, 1.0, 0.0), axis=1, keepdims=True))
    some = hits[0]
    for hit in hits[1:]:
        some = jnp.maximum(some, hit)

    def write(head, out):
        start = pl.multiple_of((first_head + head) * HD, HD)
        out_ref[:, pl.ds(start, HD)] = out.astype(jnp.bfloat16)

    ones = jnp.ones((tokens, LANES), jnp.bfloat16)
    totals = jnp.ones((items, LANES), jnp.float32)
    for first in range(0, group_size, step):
        q = stack(
            [ref[:, h * HD : (h + 1) * HD] for h in range(first, first + step) for ref in q_refs]
        )
        acc = jnp.zeros((step * items, HD + LANES), jnp.float32)
        for hit, key, value in zip(hits, keys, values):
            p = jnp.exp2(dot_nt(q, key[...]) * (SCALE * LOG2E)).astype(jnp.bfloat16)
            both = jnp.concatenate([value[...], ones], axis=1)
            here = jnp.dot(p, both, preferred_element_type=jnp.float32)
            acc = jnp.where(stack([hit] * step) > 0.0, acc + here, acc)
        for n in range(step):
            total = acc[n * items : (n + 1) * items, HD:]
            out = acc[n * items : (n + 1) * items, :HD]
            write(first + n, jnp.where(some > 0.0, out / jnp.where(some > 0.0, total, 1.0), 0.0))
            totals = jnp.where(lane == first_head + first + n, total, totals)
    good = (totals > LOW) & (totals < HIGH)
    bad = jnp.max(jnp.where(good | (some == 0.0), 0.0, 1.0))
    logs = jnp.where((some > 0.0) & good, jnp.log(jnp.where(good, totals, 1.0)), NONE)
    logs_ref[...] = jnp.where(mine, logs, logs_ref[...])

    @pl.when(bad > 0.0)
    def _():
        @pl.loop(0, group_size)
        def _(head):
            start = pl.multiple_of(head * HD, HD)
            q = stack([ref[:, pl.ds(start, HD)] for ref in q_refs])
            top = jnp.full((items, 1), NONE, jnp.float32)
            for n, (hit, key) in enumerate(zip(hits, keys)):
                s = dot_nt(q, key[...])
                s_ref[n] = s
                here = jnp.max(s, axis=1, keepdims=True)
                top = jnp.where(hit > 0.0, jnp.maximum(top, here), top)
            acc = jnp.zeros((items, HD), jnp.float32)
            total = jnp.zeros((items, 1), jnp.float32)
            for n, (hit, value) in enumerate(zip(hits, values)):
                p = jnp.exp2((s_ref[n] - top) * (SCALE * LOG2E))
                p = jnp.where(hit > 0.0, p, 0.0)
                total += jnp.sum(p, axis=1, keepdims=True)
                acc += jnp.dot(p.astype(jnp.bfloat16), value[...], preferred_element_type=jnp.float32)
            safe = jnp.where(some > 0.0, total, 1.0)
            write(head, jnp.where(some > 0.0, acc / safe, 0.0))
            log = jnp.where(some > 0.0, top * SCALE + jnp.log(safe), NONE)
            logs_ref[...] = jnp.where(lane == first_head + head, log, logs_ref[...])

    @pl.when(kv == pl.num_programs(1) - 1)
    def _():
        heads = (out_ref.shape[1] - LANES) // HD
        parts = jnp.concatenate([x[:, :heads] for x in split3(logs_ref[...])], axis=1)
        pad = jnp.zeros((items, LANES - 3 * heads), jnp.bfloat16)
        out_ref[:, heads * HD :] = jnp.concatenate([parts, pad], axis=1)


def attend_blocks(where, place, queries, cache_k, cache_v, halves, group_size, after):
    pieces = len(queries)
    rows, columns = queries[0].shape
    blocks, tokens, kv_width = cache_k.shape
    kv_half = kv_width // HD // 2
    share = min(rows, 128)
    items = share * pieces
    own = pl.BlockSpec((blocks, tokens, HD), lambda i, g, w: (0, 0, w[2] * kv_half + g))
    queries_block = pl.BlockSpec((share, group_size * HD), lambda i, g, w: (i, g))
    ids_block = pl.BlockSpec((share, LANES), lambda i, g, w: (i, columns // LANES - 1))
    return pl.pallas_call(
        functools.partial(block_kernel, pieces, group_size, max(1, ROWS_STEP // items)),
        grid_spec=pltpu.PrefetchScalarGridSpec(
            num_scalar_prefetch=1,
            grid=(rows // share, kv_half),
            in_specs=[pl.BlockSpec(place.shape, lambda i, g, w: (0, 0))]
            + [queries_block] * pieces
            + [ids_block] * pieces
            + [own, own]
            + [
                pl.BlockSpec((blocks, tokens, HD), lambda i, g, w: (0, 0, g)),
                pl.BlockSpec((blocks, tokens, HD), lambda i, g, w: (1, 0, g)),
            ]
            + [pl.BlockSpec(memory_space=pl.ANY)] * len(after),
            out_specs=pl.BlockSpec((items, columns), lambda i, g, w: (i, 0)),
            scratch_shapes=[
                pltpu.VMEM((items, LANES), jnp.float32),
                pltpu.VMEM((2 * blocks, items, tokens), jnp.float32),
            ],
        ),
        out_shape=jax.ShapeDtypeStruct((rows * pieces, columns), jnp.bfloat16),
        compiler_params=params(),
        cost_estimate=pl.CostEstimate(
            flops=16 * rows * pieces * blocks * tokens * columns,
            bytes_accessed=8 * blocks * tokens * kv_half * HD + 4 * rows * pieces * columns,
            transcendentals=2 * rows * pieces * blocks * tokens * columns // HD,
        ),
    )(where, place, *queries, *queries, cache_k, cache_v, halves, halves, *after)


def suffix_kernel(group_size, lengths_ref, q_ref, k_ref, v_ref, out_ref, log_ref):
    rows_here, steps, width = q_ref.shape
    tokens = k_ref.shape[1]
    kv_here = k_ref.shape[2] // HD
    items = rows_here * steps
    span = rows_here * tokens
    half = width // HD // 2
    lane = lax.broadcasted_iota(jnp.int32, (items, LANES), 1)
    token = lax.broadcasted_iota(jnp.int32, (items, span), 1)
    item = lax.broadcasted_iota(jnp.int32, (items, span), 0)
    seen = jnp.zeros((items, span), jnp.float32)
    for r in range(rows_here):
        offset = token - r * tokens
        inside = (item // steps == r) & (offset >= 0) & (offset < lengths_ref[r] + item % steps)
        seen = jnp.where(inside, 1.0, seen)
    seen = jnp.concatenate([seen] * group_size, axis=0)
    logs = [jnp.zeros((items, LANES), jnp.float32)] * 2
    for g in range(kv_here):
        columns = slice(g * group_size * HD, (g + 1) * group_size * HD)
        q_all = flat(q_ref[:, :, columns]).astype(jnp.bfloat16)
        q = stack([q_all[:, n * HD : (n + 1) * HD] for n in range(group_size)])
        keys = k_ref[:, :, g * HD : (g + 1) * HD].reshape(span, HD)
        values = v_ref[:, :, g * HD : (g + 1) * HD].reshape(span, HD)
        s = jnp.where(seen > 0.0, dot_nt(q, keys), NONE)
        highest = jnp.max(s, axis=1, keepdims=True)
        p = jnp.exp2((s - highest) * (SCALE * LOG2E))
        p = jnp.where(seen > 0.0, p, 0.0)
        total = jnp.sum(p, axis=1, keepdims=True)
        out = jnp.dot(p.astype(jnp.bfloat16), values, preferred_element_type=jnp.float32) / total
        log = highest * SCALE + jnp.log(total)
        for n in range(group_size):
            h = g * group_size + n
            out_ref[:, h * HD : (h + 1) * HD] = out[n * items : (n + 1) * items]
            side = h // half
            logs[side] = jnp.where(lane == h % half, log[n * items : (n + 1) * items], logs[side])
    for side in range(2):
        log_ref[side] = logs[side]


def attend_suffix(lengths, queries, suffix_k, suffix_v):
    rows, steps, width = queries.shape
    _, tokens, kv_width = suffix_k.shape
    items = rows * steps
    whole = lambda i, n: (0, 0, 0)
    return pl.pallas_call(
        functools.partial(suffix_kernel, width // kv_width),
        grid_spec=pltpu.PrefetchScalarGridSpec(
            num_scalar_prefetch=1,
            grid=(1,),
            in_specs=[pl.BlockSpec(x.shape, whole) for x in (queries, suffix_k, suffix_v)],
            out_specs=[
                pl.BlockSpec((items, width), lambda i, n: (0, 0)),
                pl.BlockSpec((2, items, LANES), whole),
            ],
        ),
        out_shape=(
            jax.ShapeDtypeStruct((items, width), jnp.float32),
            jax.ShapeDtypeStruct((2, items, LANES), jnp.float32),
        ),
        compiler_params=params(),
        cost_estimate=pl.CostEstimate(
            flops=16 * items * rows * tokens * width,
            bytes_accessed=4 * suffix_k.size + 6 * items * width,
            transcendentals=items * rows * tokens * width // HD,
        ),
    )(lengths, queries, suffix_k, suffix_v)


def merge_kernel(arrays, *refs):
    back_refs = refs[:arrays]
    out_refs = refs[arrays:]
    items = out_refs[0].shape[0]
    columns = out_refs[0].shape[1] - LANES
    heads = columns // HD
    for side, out_ref in enumerate(out_refs):
        parts = [
            (ref, start + side * items)
            for ref in back_refs
            for start in range(0, ref.shape[0], 2 * items)
        ]
        logs = []
        for ref, start in parts:
            x = ref[start : start + items, columns:].astype(jnp.float32)
            logs.append(x[:, :heads] + x[:, heads : 2 * heads] + x[:, 2 * heads : 3 * heads])
        top = logs[0]
        for log in logs[1:]:
            top = jnp.maximum(top, log)
        factors = [jnp.exp(log - top) for log in logs]
        total = factors[0]
        for factor in factors[1:]:
            total += factor
        inverse = 1.0 / total
        factors = [factor * inverse for factor in factors]
        for h in range(heads):
            span = slice(h * HD, (h + 1) * HD)
            acc = jnp.zeros((items, HD), jnp.float32)
            for factor, (ref, start) in zip(factors, parts):
                acc += factor[:, h : h + 1] * ref[start : start + items, span].astype(jnp.float32)
            out_ref[:, span] = acc
        log = top + jnp.log(total)
        pad = jnp.zeros((items, LANES - heads), jnp.float32)
        out_ref[:, columns:] = jnp.concatenate([log, pad], axis=1)


def merge(back, items):
    shape = jax.ShapeDtypeStruct((items, back[0].shape[1]), jnp.float32)
    return pl.pallas_call(
        functools.partial(merge_kernel, len(back)),
        out_shape=[shape, shape],
        compiler_params=params(),
    )(*back)


def finish_kernel(where_ref, mine_ref, other_ref, out_s_ref, log_s_ref, out_ref):
    items = mine_ref.shape[0]
    columns = mine_ref.shape[1] - LANES
    heads = columns // HD
    rows, steps, _ = out_ref.shape
    core = where_ref[2]
    for ref, which in ((mine_ref, core), (other_ref, 1 - core)):
        log = ref[:, columns:]
        log_s = log_s_ref[which]
        top = jnp.maximum(log, log_s)
        factor = jnp.exp(log - top)
        factor_s = jnp.exp(log_s - top)
        inverse = 1.0 / (factor + factor_s)
        factor, factor_s = factor * inverse, factor_s * inverse
        for h in range(heads):
            start = pl.multiple_of(which * columns + h * HD, HD)
            out = factor[:, h : h + 1] * ref[:, h * HD : (h + 1) * HD]
            out += factor_s[:, h : h + 1] * out_s_ref[:, pl.ds(start, HD)]
            for row in range(rows):
                part = out[row * steps : (row + 1) * steps]
                out_ref[row, :, pl.ds(start, HD)] = part.astype(jnp.bfloat16)


def finish(where, mine, other, out_s, log_s, shape):
    flat_map = lambda i, w: (0, 0)
    return pl.pallas_call(
        finish_kernel,
        grid_spec=pltpu.PrefetchScalarGridSpec(
            num_scalar_prefetch=1,
            grid=(1,),
            in_specs=[pl.BlockSpec(x.shape, flat_map) for x in (mine, other, out_s)]
            + [pl.BlockSpec(log_s.shape, lambda i, w: (0, 0, 0))],
            out_specs=pl.BlockSpec(shape, lambda i, w: (0, 0, 0)),
        ),
        out_shape=jax.ShapeDtypeStruct(shape, jnp.bfloat16),
        compiler_params=params(),
    )(where, mine, other, out_s, log_s)


def local(queries, selected, placement, lengths, cache_k, cache_v, suffix_k, suffix_v):
    rows_here, steps, width = queries.shape
    size = lax.axis_size("ctx")
    blocks_here, _, kv_width = cache_k.shape
    group_size = width // kv_width
    items = rows_here * steps
    chips = size // 2

    def swap(x, bits):
        return lax.ppermute(x, "ctx", [(i, i ^ bits) for i in range(size)])

    own = lax.axis_index("ctx")
    where = jnp.stack([own * blocks_here, (own ^ 1) * blocks_here, own & 1]).astype(jnp.int32)
    place = placement.reshape(1, -1)
    halves = swap(halve(where, cache_k, cache_v), 1)
    mine, other = pack(where, queries, selected)
    out_s, log_s = attend_suffix(lengths, queries, suffix_k, suffix_v)
    attend = functools.partial(attend_blocks, where, place)
    if chips <= 4:
        order = [2, 3, 1, 0] if chips == 4 else list(range(chips - 1, -1, -1))
        arrived = {k: [swap(mine, 2 * k) if k else mine, swap(other, 2 * k + 1)] for k in order}
        back = []
        after = [log_s]
        for k in order:
            partial = attend(arrived[k], cache_k, cache_v, halves, group_size, after)
            after = [partial]
            back.append(swap(partial, 2 * k) if k else partial)
    else:
        same = [[2 * z + core for z in range(chips)] for core in range(2)]
        chip = jnp.concatenate([mine, swap(other, 1)], axis=0)
        every = lax.all_gather(chip, "ctx", axis=0, tiled=True, axis_index_groups=same)
        partial = attend([every], cache_k, cache_v, halves, group_size, [log_s])
        back = [
            lax.all_to_all(
                partial, "ctx", split_axis=0, concat_axis=0, tiled=True, axis_index_groups=same
            )
        ]
    keep, send = merge(back, items)
    return finish(where, keep, swap(send, 1), out_s, log_s, queries.shape)


def solution(mesh):
    rows = P(("groups", "ctx"), None, "rows")
    in_specs = (
        rows,
        P(("groups", "ctx"), None, None),
        P("groups"),
        P(("groups", "ctx")),
        rows,
        rows,
        rows,
        rows,
    )
    return jax.shard_map(local, mesh=mesh, in_specs=in_specs, out_specs=rows, check_vma=False)
```

```python
import functools
import math

import jax
import jax.numpy as jnp
from jax import lax
from jax.experimental import pallas as pl
from jax.experimental.pallas import tpu as pltpu
from jax.sharding import PartitionSpec as P

HD = 128
LANES = 128
SCALE = 1.0 / math.sqrt(HD)
LOG2E = math.log2(math.e)
NONE = -1e30
LOW, HIGH = 2.0**-80, 2.0**100
VMEM = 60 * 1024 * 1024
ROWS_STEP = 512


def split3(x):
    high = x.astype(jnp.bfloat16)
    rest = x - high.astype(jnp.float32)
    middle = rest.astype(jnp.bfloat16)
    low = (rest - middle.astype(jnp.float32)).astype(jnp.bfloat16)
    return high, middle, low


def dot_nt(a, b):
    return lax.dot_general(a, b, (((1,), (1,)), ((), ())), preferred_element_type=jnp.float32)


def stack(arrays):
    return arrays[0] if len(arrays) == 1 else jnp.concatenate(arrays, axis=0)


def params():
    return pltpu.CompilerParams(vmem_limit_bytes=VMEM)


def flat(x):
    return x.astype(jnp.float32).reshape(x.shape[0] * x.shape[1], x.shape[2])


ANY = pl.BlockSpec(memory_space=pl.ANY)


def pack_kernel(q_ref, selected_ref, mine_ref, other_ref):
    half = q_ref.shape[2] // 2
    core = lax.axis_index("ctx") % 2
    ids = flat(selected_ref[...])
    pad = jnp.full((ids.shape[0], LANES - ids.shape[1]), -1.0, jnp.float32)
    ids = jnp.concatenate([ids, pad], axis=1).astype(jnp.bfloat16)
    for ref, which in ((mine_ref, core), (other_ref, 1 - core)):
        start = pl.multiple_of(which * half, LANES)
        ref[:, :half] = flat(q_ref[:, :, pl.ds(start, half)]).astype(jnp.bfloat16)
        ref[:, half:] = ids


def pack(queries, selected):
    rows, steps, width = queries.shape
    shape = jax.ShapeDtypeStruct((rows * steps, width // 2 + LANES), jnp.bfloat16)
    return pl.pallas_call(pack_kernel, out_shape=[shape, shape], compiler_params=params())(
        queries, selected
    )


def halve_kernel(k_ref, v_ref, out_ref, sems):
    blocks, _, columns = k_ref.shape
    half = columns // 2
    start = pl.multiple_of((1 - lax.axis_index("ctx") % 2) * half, LANES)
    copies = [
        pltpu.make_async_copy(
            ref.at[b, :, pl.ds(start, half)], out_ref.at[n * blocks + b], sems.at[n * blocks + b]
        )
        for n, ref in enumerate((k_ref, v_ref))
        for b in range(blocks)
    ]
    for copy in copies:
        copy.start()
    for copy in copies:
        copy.wait()


def halve(cache_k, cache_v):
    blocks, tokens, columns = cache_k.shape
    return pl.pallas_call(
        halve_kernel,
        in_specs=[ANY, ANY],
        out_specs=ANY,
        out_shape=jax.ShapeDtypeStruct((2 * blocks, tokens, columns // 2), jnp.bfloat16),
        scratch_shapes=[pltpu.SemaphoreType.DMA((2 * blocks,))],
        compiler_params=params(),
    )(cache_k, cache_v)


def block_kernel(pieces, group_size, step, tiles, place_ref, *refs):
    q_refs = refs[:pieces]
    own_k, own_v, next_kv = refs[pieces : pieces + 3]
    out_refs = refs[-pieces - 7 : -7]
    q_ref, k_ref, v_ref, logs_ref, s_ref, sems, q_sems = refs[-7:]
    share = out_refs[0].shape[0]
    items, width = q_ref.shape
    columns = width - LANES
    kv_half, both_blocks, tokens, _ = k_ref.shape
    blocks = both_blocks // 2
    own = lax.axis_index("ctx")
    core = own % 2
    tile = pl.program_id(0)

    copies = {}
    for g in range(kv_half):
        mine = pl.ds(pl.multiple_of((core * kv_half + g) * HD, HD), HD)
        other = slice(g * HD, (g + 1) * HD)
        for b in range(both_blocks):
            if b < blocks:
                sources = own_k.at[b, :, mine], own_v.at[b, :, mine]
            else:
                sources = next_kv.at[b - blocks, :, other], next_kv.at[b, :, other]
            for n, (source, held) in enumerate(zip(sources, (k_ref, v_ref))):
                copies[g, b, n] = pltpu.make_async_copy(source, held.at[g, b], sems.at[g, b, n])
    q_copies = [
        pltpu.make_async_copy(
            ref.at[pl.ds(pl.multiple_of(tile * share, share), share)],
            q_ref.at[n * share : (n + 1) * share],
            q_sems.at[n],
        )
        for n, ref in enumerate(q_refs)
    ]

    def first_time(action):
        if tiles == 1:
            action()
        else:
            pl.when(tile == 0)(action)

    for copy in q_copies:
        copy.start()

    def start_all():
        for g in range(kv_half):
            for b in range(both_blocks):
                for n in range(2):
                    copies[g, b, n].start()

    first_time(start_all)
    for copy in q_copies:
        copy.wait()

    lane = lax.broadcasted_iota(jnp.int32, (items, LANES), 1)
    ids = q_ref[:, columns:].astype(jnp.float32)
    place = place_ref[...]
    block_ids = lax.broadcasted_iota(jnp.int32, place.shape, 1)
    hits = []
    for owner in (own, own + 1 - 2 * core):
        for b in range(blocks):
            target = jnp.sum(
                jnp.where(place == owner * blocks + b, block_ids, 0).astype(jnp.float32),
                axis=1,
                keepdims=True,
            )
            hits.append(jnp.max(jnp.where(ids == target, 1.0, 0.0), axis=1, keepdims=True))
    some = hits[0]
    for hit in hits[1:]:
        some = jnp.maximum(some, hit)

    def write(head, out):
        start = pl.multiple_of(head * HD, HD) if not isinstance(head, int) else head * HD
        out = out.astype(jnp.bfloat16)
        for n, ref in enumerate(out_refs):
            ref[:, pl.ds(start, HD)] = out[n * share : (n + 1) * share]

    ones = jnp.ones((tokens, LANES), jnp.bfloat16)
    totals = jnp.ones((items, LANES), jnp.float32)
    units = [
        (g, first, b)
        for g in range(kv_half)
        for first in range(0, group_size, step)
        for b in range(both_blocks)
    ]

    def scores(g, first, b):
        if first == 0:

            def ready():
                copies[g, b, 0].wait()
                copies[g, b, 1].wait()

            first_time(ready)
        heads = range(g * group_size + first, g * group_size + first + step)
        q = stack([q_ref[:, h * HD : (h + 1) * HD] for h in heads])
        return dot_nt(q, k_ref[g, b])

    s = scores(*units[0])
    acc = None
    for n, (g, first, b) in enumerate(units):
        following = scores(*units[n + 1]) if n + 1 < len(units) else None
        p = jnp.exp2(s * (SCALE * LOG2E)).astype(jnp.bfloat16)
        values = jnp.concatenate([v_ref[g, b], ones], axis=1)
        here = jnp.dot(p, values, preferred_element_type=jnp.float32)
        hit = stack([hits[b]] * step) > 0.0
        acc = jnp.where(hit, here if b == 0 else acc + here, 0.0 if b == 0 else acc)
        s = following
        if b == both_blocks - 1:
            for m in range(step):
                head = g * group_size + first + m
                total = acc[m * items : (m + 1) * items, HD:]
                out = acc[m * items : (m + 1) * items, :HD]
                write(head, jnp.where(some > 0.0, out / jnp.where(some > 0.0, total, 1.0), 0.0))
                totals = jnp.where(lane == head, total, totals)
    good = (totals > LOW) & (totals < HIGH)
    bad = jnp.max(jnp.where(good | (some == 0.0), 0.0, 1.0))
    logs = jnp.where((some > 0.0) & good, jnp.log(jnp.where(good, totals, 1.0)), NONE)
    logs_ref[...] = logs

    @pl.when(bad > 0.0)
    def _():
        @pl.loop(0, kv_half * group_size)
        def _(head):
            g = head // group_size
            q = q_ref[:, pl.ds(pl.multiple_of(head * HD, HD), HD)]
            top = jnp.full((items, 1), NONE, jnp.float32)
            for n, hit in enumerate(hits):
                s = dot_nt(q, k_ref[g, n])
                s_ref[n] = s
                here = jnp.max(s, axis=1, keepdims=True)
                top = jnp.where(hit > 0.0, jnp.maximum(top, here), top)
            acc = jnp.zeros((items, HD), jnp.float32)
            total = jnp.zeros((items, 1), jnp.float32)
            for n, hit in enumerate(hits):
                p = jnp.exp2((s_ref[n] - top) * (SCALE * LOG2E))
                p = jnp.where(hit > 0.0, p, 0.0)
                total += jnp.sum(p, axis=1, keepdims=True)
                acc += jnp.dot(p.astype(jnp.bfloat16), v_ref[g, n], preferred_element_type=jnp.float32)
            safe = jnp.where(some > 0.0, total, 1.0)
            write(head, jnp.where(some > 0.0, acc / safe, 0.0))
            log = jnp.where(some > 0.0, top * SCALE + jnp.log(safe), NONE)
            logs_ref[...] = jnp.where(lane == head, log, logs_ref[...])

    heads = columns // HD
    parts = jnp.concatenate([x[:, :heads] for x in split3(logs_ref[...])], axis=1)
    pad = jnp.zeros((items, LANES - 3 * heads), jnp.bfloat16)
    parts = jnp.concatenate([parts, pad], axis=1)
    for n, ref in enumerate(out_refs):
        ref[:, columns:] = parts[n * share : (n + 1) * share]


def attend_blocks(place, queries, cache_k, cache_v, halves, group_size, after):
    pieces = len(queries)
    rows, columns = queries[0].shape
    blocks, tokens, kv_width = cache_k.shape
    kv_half = kv_width // HD // 2
    share = min(rows, 64)
    items = share * pieces
    tiles = rows // share
    step = min(group_size, max(1, ROWS_STEP // items))
    return pl.pallas_call(
        functools.partial(block_kernel, pieces, group_size, step, tiles),
        grid=(tiles,),
        in_specs=[pl.BlockSpec(place.shape, lambda i: (0, 0))] + [ANY] * (pieces + 3 + len(after)),
        out_specs=[pl.BlockSpec((share, columns), lambda i: (i, 0))] * pieces,
        out_shape=[jax.ShapeDtypeStruct((rows, columns), jnp.bfloat16)] * pieces,
        scratch_shapes=[
            pltpu.VMEM((items, columns), jnp.bfloat16),
            pltpu.VMEM((kv_half, 2 * blocks, tokens, HD), jnp.bfloat16),
            pltpu.VMEM((kv_half, 2 * blocks, tokens, HD), jnp.bfloat16),
            pltpu.VMEM((items, LANES), jnp.float32),
            pltpu.VMEM((2 * blocks, items, tokens), jnp.float32),
            pltpu.SemaphoreType.DMA((kv_half, 2 * blocks, 2)),
            pltpu.SemaphoreType.DMA((pieces,)),
        ],
        compiler_params=params(),
        cost_estimate=pl.CostEstimate(
            flops=16 * rows * pieces * blocks * tokens * columns,
            bytes_accessed=8 * blocks * tokens * kv_half * HD + 4 * rows * pieces * columns,
            transcendentals=2 * rows * pieces * blocks * tokens * columns // HD,
        ),
    )(place, *queries, cache_k, cache_v, halves, *after)


def suffix_kernel(group_size, lengths_ref, q_ref, k_ref, v_ref, out_ref, log_ref):
    rows_here, steps, width = q_ref.shape
    tokens = k_ref.shape[1]
    kv_here = k_ref.shape[2] // HD
    items = rows_here * steps
    span = rows_here * tokens
    half = width // HD // 2
    lane = lax.broadcasted_iota(jnp.int32, (items, LANES), 1)
    token = lax.broadcasted_iota(jnp.int32, (items, span), 1)
    item = lax.broadcasted_iota(jnp.int32, (items, span), 0)
    seen = jnp.zeros((items, span), jnp.float32)
    for r in range(rows_here):
        offset = token - r * tokens
        inside = (item // steps == r) & (offset >= 0) & (offset < lengths_ref[r] + item % steps)
        seen = jnp.where(inside, 1.0, seen)
    seen = jnp.concatenate([seen] * group_size, axis=0)
    logs = [jnp.zeros((items, LANES), jnp.float32)] * 2
    for g in range(kv_here):
        columns = slice(g * group_size * HD, (g + 1) * group_size * HD)
        q_all = flat(q_ref[:, :, columns]).astype(jnp.bfloat16)
        q = stack([q_all[:, n * HD : (n + 1) * HD] for n in range(group_size)])
        keys = k_ref[:, :, g * HD : (g + 1) * HD].reshape(span, HD)
        values = v_ref[:, :, g * HD : (g + 1) * HD].reshape(span, HD)
        s = jnp.where(seen > 0.0, dot_nt(q, keys), NONE)
        highest = jnp.max(s, axis=1, keepdims=True)
        p = jnp.exp2((s - highest) * (SCALE * LOG2E))
        p = jnp.where(seen > 0.0, p, 0.0)
        total = jnp.sum(p, axis=1, keepdims=True)
        out = jnp.dot(p.astype(jnp.bfloat16), values, preferred_element_type=jnp.float32) / total
        log = highest * SCALE + jnp.log(total)
        for n in range(group_size):
            h = g * group_size + n
            out_ref[:, h * HD : (h + 1) * HD] = out[n * items : (n + 1) * items]
            side = h // half
            logs[side] = jnp.where(lane == h % half, log[n * items : (n + 1) * items], logs[side])
    for side in range(2):
        log_ref[side] = logs[side]


def attend_suffix(lengths, queries, suffix_k, suffix_v):
    rows, steps, width = queries.shape
    _, tokens, kv_width = suffix_k.shape
    items = rows * steps
    whole = lambda i, n: (0, 0, 0)
    return pl.pallas_call(
        functools.partial(suffix_kernel, width // kv_width),
        grid_spec=pltpu.PrefetchScalarGridSpec(
            num_scalar_prefetch=1,
            grid=(1,),
            in_specs=[pl.BlockSpec(x.shape, whole) for x in (queries, suffix_k, suffix_v)],
            out_specs=[
                pl.BlockSpec((items, width), lambda i, n: (0, 0)),
                pl.BlockSpec((2, items, LANES), whole),
            ],
        ),
        out_shape=(
            jax.ShapeDtypeStruct((items, width), jnp.float32),
            jax.ShapeDtypeStruct((2, items, LANES), jnp.float32),
        ),
        compiler_params=params(),
        cost_estimate=pl.CostEstimate(
            flops=16 * items * rows * tokens * width,
            bytes_accessed=4 * suffix_k.size + 6 * items * width,
            transcendentals=items * rows * tokens * width // HD,
        ),
    )(lengths, queries, suffix_k, suffix_v)


def merge_kernel(even, odd, *refs):
    sides = refs[:even], refs[even : even + odd]
    out_s_ref, log_s_ref, out_ref = refs[even + odd :]
    items, width = out_s_ref.shape
    columns = width // 2
    heads = columns // HD
    rows, steps, _ = out_ref.shape
    core = lax.axis_index("ctx") % 2
    for which, back in ((core, sides[0]), (1 - core, sides[1])):
        parts = [(ref, start) for ref in back for start in range(0, ref.shape[0], items)]
        logs = [log_s_ref[which][:, :heads]]
        for ref, start in parts:
            x = ref[start : start + items, columns:].astype(jnp.float32)
            logs.append(x[:, :heads] + x[:, heads : 2 * heads] + x[:, 2 * heads : 3 * heads])
        top = logs[0]
        for log in logs[1:]:
            top = jnp.maximum(top, log)
        factors = [jnp.exp(log - top) for log in logs]
        total = factors[0]
        for factor in factors[1:]:
            total += factor
        inverse = 1.0 / total
        factors = [factor * inverse for factor in factors]
        for h in range(heads):
            span = pl.ds(pl.multiple_of(which * columns + h * HD, HD), HD)
            acc = factors[0][:, h : h + 1] * out_s_ref[:, span]
            for factor, (ref, start) in zip(factors[1:], parts):
                value = ref[start : start + items, h * HD : (h + 1) * HD]
                acc += factor[:, h : h + 1] * value.astype(jnp.float32)
            for row in range(rows):
                out_ref[row, :, span] = acc[row * steps : (row + 1) * steps].astype(jnp.bfloat16)


def merge(even, odd, out_s, log_s, shape):
    return pl.pallas_call(
        functools.partial(merge_kernel, len(even), len(odd)),
        out_shape=jax.ShapeDtypeStruct(shape, jnp.bfloat16),
        compiler_params=params(),
    )(*even, *odd, out_s, log_s)


def local(queries, selected, placement, lengths, cache_k, cache_v, suffix_k, suffix_v):
    rows_here, steps, width = queries.shape
    size = lax.axis_size("ctx")
    kv_width = cache_k.shape[2]
    group_size = width // kv_width
    items = rows_here * steps
    chips = size // 2

    def swap(x, bits):
        return lax.ppermute(x, "ctx", [(i, i ^ bits) for i in range(size)]) if bits else x

    place = placement.reshape(1, -1)
    halves = swap(halve(cache_k, cache_v), 1)
    packed = pack(queries, selected)
    out_s, log_s = attend_suffix(lengths, queries, suffix_k, suffix_v)
    if chips <= 4:
        far = list(range(chips, size)) if chips > 1 else []
        arrived = {n: swap(packed[n % 2], n) for n in far + list(range(chips))}
        back = {}
        after = [log_s]
        for call in (far, list(range(chips))) if far else (list(range(size)),):
            partial = attend_blocks(
                place, [arrived[n] for n in call], cache_k, cache_v, halves, group_size, after
            )
            after = [partial[0]]
            for n, piece in zip(call, partial):
                back[n] = swap(piece, n)
        even = [back[n] for n in range(0, size, 2)]
        odd = [back[n] for n in range(1, size, 2)]
    else:
        same = [[2 * z + core for z in range(chips)] for core in range(2)]
        chip = jnp.concatenate([packed[0], swap(packed[1], 1)], axis=0)
        every = lax.all_gather(chip, "ctx", axis=0, tiled=True, axis_index_groups=same)
        (partial,) = attend_blocks(place, [every], cache_k, cache_v, halves, group_size, [log_s])
        back = lax.all_to_all(
            partial, "ctx", split_axis=0, concat_axis=0, tiled=True, axis_index_groups=same
        ).reshape(chips, 2, items, -1)
        even = [back[:, 0].reshape(chips * items, -1)]
        odd = [swap(back[:, 1].reshape(chips * items, -1), 1)]
    return merge(even, odd, out_s, log_s, queries.shape)


def solution(mesh):
    rows = P(("groups", "ctx"), None, "rows")
    in_specs = (
        rows,
        P(("groups", "ctx"), None, None),
        P("groups"),
        P(("groups", "ctx")),
        rows,
        rows,
        rows,
        rows,
    )
    return jax.shard_map(local, mesh=mesh, in_specs=in_specs, out_specs=rows, check_vma=False)
```

```python
import functools
import math

import jax
import jax.numpy as jnp
from jax import lax
from jax.experimental import pallas as pl
from jax.experimental.pallas import tpu as pltpu
from jax.sharding import PartitionSpec as P

HD = 128
LANES = 128
SCALE = 1.0 / math.sqrt(HD)
LOG2E = math.log2(math.e)
NONE = -1e30
LOW, HIGH = 2.0**-80, 2.0**100
VMEM = 60 * 1024 * 1024
ROWS_STEP = 512


def split3(x):
    high = x.astype(jnp.bfloat16)
    rest = x - high.astype(jnp.float32)
    middle = rest.astype(jnp.bfloat16)
    low = (rest - middle.astype(jnp.float32)).astype(jnp.bfloat16)
    return high, middle, low


def dot_nt(a, b):
    return lax.dot_general(a, b, (((1,), (1,)), ((), ())), preferred_element_type=jnp.float32)


def stack(arrays):
    return arrays[0] if len(arrays) == 1 else jnp.concatenate(arrays, axis=0)


def params():
    return pltpu.CompilerParams(vmem_limit_bytes=VMEM)


def flat(x):
    return x.astype(jnp.float32).reshape(x.shape[0] * x.shape[1], x.shape[2])


ANY = pl.BlockSpec(memory_space=pl.ANY)


def pack_kernel(q_ref, selected_ref, k_ref, v_ref, mine_ref, other_ref, out_ref, held, in_sems, out_sems):
    blocks, _, kv_columns = k_ref.shape
    kv_half = kv_columns // 2
    half = q_ref.shape[2] // 2
    core = lax.axis_index("ctx") % 2
    kv_start = pl.multiple_of((1 - core) * kv_half, LANES)
    reads, writes = [], []
    for n, ref in enumerate((k_ref, v_ref)):
        for b in range(blocks):
            m = n * blocks + b
            source = ref.at[b, :, pl.ds(kv_start, kv_half)]
            reads.append(pltpu.make_async_copy(source, held.at[m], in_sems.at[m]))
            writes.append(pltpu.make_async_copy(held.at[m], out_ref.at[m], out_sems.at[m]))
    for read in reads:
        read.start()
    ids = flat(selected_ref[...])
    pad = jnp.full((ids.shape[0], LANES - ids.shape[1]), -1.0, jnp.float32)
    ids = jnp.concatenate([ids, pad], axis=1).astype(jnp.bfloat16)
    for ref, which in ((mine_ref, core), (other_ref, 1 - core)):
        start = pl.multiple_of(which * half, LANES)
        ref[:, :half] = flat(q_ref[:, :, pl.ds(start, half)]).astype(jnp.bfloat16)
        ref[:, half:] = ids
    for read, write in zip(reads, writes):
        read.wait()
        write.start()
    for write in writes:
        write.wait()


def pack(queries, selected, cache_k, cache_v):
    rows, steps, width = queries.shape
    blocks, tokens, columns = cache_k.shape
    shape = jax.ShapeDtypeStruct((rows * steps, width // 2 + LANES), jnp.bfloat16)
    kv_shape = (2 * blocks, tokens, columns // 2)
    whole = pl.BlockSpec(memory_space=pltpu.VMEM)
    return pl.pallas_call(
        pack_kernel,
        in_specs=[whole, whole, ANY, ANY],
        out_specs=[whole, whole, ANY],
        out_shape=[shape, shape, jax.ShapeDtypeStruct(kv_shape, jnp.bfloat16)],
        scratch_shapes=[
            pltpu.VMEM(kv_shape, jnp.bfloat16),
            pltpu.SemaphoreType.DMA((2 * blocks,)),
            pltpu.SemaphoreType.DMA((2 * blocks,)),
        ],
        compiler_params=params(),
    )(queries, selected, cache_k, cache_v)


def block_kernel(pieces, group_size, step, where_ref, place_ref, *refs):
    q_refs = refs[:pieces]
    id_refs = refs[pieces : 2 * pieces]
    own_k, own_v, next_k, next_v = refs[2 * pieces : 2 * pieces + 4]
    outs = max(1, pieces // 2)
    out_refs = refs[-2 - outs : -2]
    logs_ref, s_ref = refs[-2:]
    kv = pl.program_id(1)
    share = q_refs[0].shape[0]
    items = share * pieces
    kept = items // outs
    blocks, tokens, _ = own_k.shape
    lane = lax.broadcasted_iota(jnp.int32, (items, LANES), 1)
    first_head = kv * group_size
    mine = (lane >= first_head) & (lane < first_head + group_size)
    ids = stack([ref[...].astype(jnp.float32) for ref in id_refs])
    place = place_ref[...]
    block_ids = lax.broadcasted_iota(jnp.int32, place.shape, 1)
    keys = [ref.at[b] for ref in (own_k, next_k) for b in range(blocks)]
    values = [ref.at[b] for ref in (own_v, next_v) for b in range(blocks)]
    hits = []
    for base in (where_ref[0], where_ref[1]):
        for b in range(blocks):
            target = jnp.sum(
                jnp.where(place == base + b, block_ids, 0).astype(jnp.float32), axis=1, keepdims=True
            )
            hits.append(jnp.max(jnp.where(ids == target, 1.0, 0.0), axis=1, keepdims=True))
    some = hits[0]
    for hit in hits[1:]:
        some = jnp.maximum(some, hit)

    def write(head, out):
        start = pl.multiple_of((first_head + head) * HD, HD)
        out = out.astype(jnp.bfloat16)
        for n, ref in enumerate(out_refs):
            ref[:, pl.ds(start, HD)] = out[n * kept : (n + 1) * kept]

    ones = jnp.ones((tokens, LANES), jnp.bfloat16)
    totals = jnp.ones((items, LANES), jnp.float32)
    for first in range(0, group_size, step):
        q = stack(
            [ref[:, h * HD : (h + 1) * HD] for h in range(first, first + step) for ref in q_refs]
        )
        acc = jnp.zeros((step * items, HD + LANES), jnp.float32)
        for hit, key, value in zip(hits, keys, values):
            p = jnp.exp2(dot_nt(q, key[...]) * (SCALE * LOG2E)).astype(jnp.bfloat16)
            both = jnp.concatenate([value[...], ones], axis=1)
            here = jnp.dot(p, both, preferred_element_type=jnp.float32)
            acc = jnp.where(stack([hit] * step) > 0.0, acc + here, acc)
        for n in range(step):
            total = acc[n * items : (n + 1) * items, HD:]
            out = acc[n * items : (n + 1) * items, :HD]
            write(first + n, jnp.where(some > 0.0, out / jnp.where(some > 0.0, total, 1.0), 0.0))
            totals = jnp.where(lane == first_head + first + n, total, totals)
    good = (totals > LOW) & (totals < HIGH)
    bad = jnp.max(jnp.where(good | (some == 0.0), 0.0, 1.0))
    logs = jnp.where((some > 0.0) & good, jnp.log(jnp.where(good, totals, 1.0)), NONE)
    logs_ref[...] = jnp.where(mine, logs, logs_ref[...])

    @pl.when(bad > 0.0)
    def _():
        @pl.loop(0, group_size)
        def _(head):
            start = pl.multiple_of(head * HD, HD)
            q = stack([ref[:, pl.ds(start, HD)] for ref in q_refs])
            top = jnp.full((items, 1), NONE, jnp.float32)
            for n, (hit, key) in enumerate(zip(hits, keys)):
                s = dot_nt(q, key[...])
                s_ref[n] = s
                here = jnp.max(s, axis=1, keepdims=True)
                top = jnp.where(hit > 0.0, jnp.maximum(top, here), top)
            acc = jnp.zeros((items, HD), jnp.float32)
            total = jnp.zeros((items, 1), jnp.float32)
            for n, (hit, value) in enumerate(zip(hits, values)):
                p = jnp.exp2((s_ref[n] - top) * (SCALE * LOG2E))
                p = jnp.where(hit > 0.0, p, 0.0)
                total += jnp.sum(p, axis=1, keepdims=True)
                acc += jnp.dot(p.astype(jnp.bfloat16), value[...], preferred_element_type=jnp.float32)
            safe = jnp.where(some > 0.0, total, 1.0)
            write(head, jnp.where(some > 0.0, acc / safe, 0.0))
            log = jnp.where(some > 0.0, top * SCALE + jnp.log(safe), NONE)
            logs_ref[...] = jnp.where(lane == first_head + head, log, logs_ref[...])

    @pl.when(kv == pl.num_programs(1) - 1)
    def _():
        heads = (out_refs[0].shape[1] - LANES) // HD
        parts = jnp.concatenate([x[:, :heads] for x in split3(logs_ref[...])], axis=1)
        pad = jnp.zeros((items, LANES - 3 * heads), jnp.bfloat16)
        parts = jnp.concatenate([parts, pad], axis=1)
        for n, ref in enumerate(out_refs):
            ref[:, heads * HD :] = parts[n * kept : (n + 1) * kept]


def attend_blocks(where, place, queries, cache_k, cache_v, halves, group_size, after):
    pieces = len(queries)
    rows, columns = queries[0].shape
    blocks, tokens, kv_width = cache_k.shape
    kv_half = kv_width // HD // 2
    share = min(rows, 64)
    items = share * pieces
    outs = max(1, pieces // 2)
    own = pl.BlockSpec((blocks, tokens, HD), lambda i, g, w: (0, 0, w[2] * kv_half + g))
    queries_block = pl.BlockSpec((share, group_size * HD), lambda i, g, w: (i, g))
    ids_block = pl.BlockSpec((share, LANES), lambda i, g, w: (i, columns // LANES - 1))
    return pl.pallas_call(
        functools.partial(block_kernel, pieces, group_size, min(group_size, max(1, ROWS_STEP // items))),
        grid_spec=pltpu.PrefetchScalarGridSpec(
            num_scalar_prefetch=1,
            grid=(rows // share, kv_half),
            in_specs=[pl.BlockSpec(place.shape, lambda i, g, w: (0, 0))]
            + [queries_block] * pieces
            + [ids_block] * pieces
            + [own, own]
            + [
                pl.BlockSpec((blocks, tokens, HD), lambda i, g, w: (0, 0, g)),
                pl.BlockSpec((blocks, tokens, HD), lambda i, g, w: (1, 0, g)),
            ]
            + [pl.BlockSpec(memory_space=pl.ANY)] * len(after),
            out_specs=[pl.BlockSpec((items // outs, columns), lambda i, g, w: (i, 0))] * outs,
            scratch_shapes=[
                pltpu.VMEM((items, LANES), jnp.float32),
                pltpu.VMEM((2 * blocks, items, tokens), jnp.float32),
            ],
        ),
        out_shape=[jax.ShapeDtypeStruct((rows * pieces // outs, columns), jnp.bfloat16)] * outs,
        compiler_params=params(),
        cost_estimate=pl.CostEstimate(
            flops=rows * pieces * tokens * columns,
            bytes_accessed=4 * rows * pieces * columns,
            transcendentals=rows * pieces * columns,
        ),
    )(where, place, *queries, *queries, cache_k, cache_v, halves, halves, *after)


def suffix_kernel(group_size, lengths_ref, q_ref, k_ref, v_ref, out_ref, log_ref):
    rows_here, steps, width = q_ref.shape
    tokens = k_ref.shape[1]
    kv_here = k_ref.shape[2] // HD
    items = rows_here * steps
    span = rows_here * tokens
    half = width // HD // 2
    lane = lax.broadcasted_iota(jnp.int32, (items, LANES), 1)
    token = lax.broadcasted_iota(jnp.int32, (items, span), 1)
    item = lax.broadcasted_iota(jnp.int32, (items, span), 0)
    seen = jnp.zeros((items, span), jnp.float32)
    for r in range(rows_here):
        offset = token - r * tokens
        inside = (item // steps == r) & (offset >= 0) & (offset < lengths_ref[r] + item % steps)
        seen = jnp.where(inside, 1.0, seen)
    seen = jnp.concatenate([seen] * group_size, axis=0)
    logs = [jnp.zeros((items, LANES), jnp.float32)] * 2
    for g in range(kv_here):
        columns = slice(g * group_size * HD, (g + 1) * group_size * HD)
        q_all = flat(q_ref[:, :, columns]).astype(jnp.bfloat16)
        q = stack([q_all[:, n * HD : (n + 1) * HD] for n in range(group_size)])
        keys = k_ref[:, :, g * HD : (g + 1) * HD].reshape(span, HD)
        values = v_ref[:, :, g * HD : (g + 1) * HD].reshape(span, HD)
        s = jnp.where(seen > 0.0, dot_nt(q, keys), NONE)
        highest = jnp.max(s, axis=1, keepdims=True)
        p = jnp.exp2((s - highest) * (SCALE * LOG2E))
        p = jnp.where(seen > 0.0, p, 0.0)
        total = jnp.sum(p, axis=1, keepdims=True)
        out = jnp.dot(p.astype(jnp.bfloat16), values, preferred_element_type=jnp.float32) / total
        log = highest * SCALE + jnp.log(total)
        for n in range(group_size):
            h = g * group_size + n
            out_ref[:, h * HD : (h + 1) * HD] = out[n * items : (n + 1) * items]
            side = h // half
            logs[side] = jnp.where(lane == h % half, log[n * items : (n + 1) * items], logs[side])
    for side in range(2):
        log_ref[side] = logs[side]


def attend_suffix(lengths, queries, suffix_k, suffix_v):
    rows, steps, width = queries.shape
    _, tokens, kv_width = suffix_k.shape
    items = rows * steps
    whole = lambda i, n: (0, 0, 0)
    return pl.pallas_call(
        functools.partial(suffix_kernel, width // kv_width),
        grid_spec=pltpu.PrefetchScalarGridSpec(
            num_scalar_prefetch=1,
            grid=(1,),
            in_specs=[pl.BlockSpec(x.shape, whole) for x in (queries, suffix_k, suffix_v)],
            out_specs=[
                pl.BlockSpec((items, width), lambda i, n: (0, 0)),
                pl.BlockSpec((2, items, LANES), whole),
            ],
        ),
        out_shape=(
            jax.ShapeDtypeStruct((items, width), jnp.float32),
            jax.ShapeDtypeStruct((2, items, LANES), jnp.float32),
        ),
        compiler_params=params(),
        cost_estimate=pl.CostEstimate(
            flops=16 * items * rows * tokens * width,
            bytes_accessed=4 * suffix_k.size + 6 * items * width,
            transcendentals=items * rows * tokens * width // HD,
        ),
    )(lengths, queries, suffix_k, suffix_v)


def weigh(parts, items, heads):
    columns = heads * HD
    logs = []
    for ref, start in parts:
        x = ref[start : start + items, columns:].astype(jnp.float32)
        logs.append(x[:, :heads] + x[:, heads : 2 * heads] + x[:, 2 * heads : 3 * heads])
    return logs


def shares(logs):
    top = logs[0]
    for log in logs[1:]:
        top = jnp.maximum(top, log)
    factors = [jnp.exp(log - top) for log in logs]
    total = factors[0]
    for factor in factors[1:]:
        total += factor
    inverse = 1.0 / total
    return [factor * inverse for factor in factors], top + jnp.log(total)


def parts_of(refs, items, side):
    return [(ref, start + side * items) for ref in refs for start in range(0, ref.shape[0], 2 * items)]


def other_kernel(*refs):
    out_ref = refs[-1]
    items = out_ref.shape[0]
    columns = out_ref.shape[1] - LANES
    heads = columns // HD
    parts = parts_of(refs[:-1], items, 1)
    factors, log = shares(weigh(parts, items, heads))
    for h in range(heads):
        span = slice(h * HD, (h + 1) * HD)
        acc = jnp.zeros((items, HD), jnp.float32)
        for factor, (ref, start) in zip(factors, parts):
            acc += factor[:, h : h + 1] * ref[start : start + items, span].astype(jnp.float32)
        out_ref[:, span] = acc
    pad = jnp.zeros((items, LANES - heads), jnp.float32)
    out_ref[:, columns:] = jnp.concatenate([log, pad], axis=1)


def merge_other(back, items):
    return pl.pallas_call(
        other_kernel,
        out_shape=jax.ShapeDtypeStruct((items, back[0].shape[1]), jnp.float32),
        compiler_params=params(),
    )(*back)


def finish_kernel(arrays, own, where_ref, *refs):
    back_refs = refs[:arrays]
    out_s_ref, log_s_ref = refs[arrays : arrays + 2]
    out_ref = refs[-1]
    rows, steps, columns = out_ref.shape
    items = rows * steps
    heads = columns // HD
    log_s = log_s_ref[0][:, :heads]
    if own:
        parts = parts_of(back_refs, items, 0)
        logs = weigh(parts, items, heads)
    else:
        parts = [(back_refs[0], 0)]
        logs = [back_refs[0][:, columns : columns + heads]]
    factors, _ = shares([log_s] + logs)
    for h in range(heads):
        span = slice(h * HD, (h + 1) * HD)
        acc = factors[0][:, h : h + 1] * out_s_ref[:, span]
        for factor, (ref, start) in zip(factors[1:], parts):
            acc += factor[:, h : h + 1] * ref[start : start + items, span].astype(jnp.float32)
        for row in range(rows):
            out_ref[row, :, span] = acc[row * steps : (row + 1) * steps].astype(jnp.bfloat16)


def finish(where, back, out_s, log_s, shape, so_far):
    rows, steps, width = shape
    items = rows * steps
    own = so_far is None
    others = [] if own else [so_far]

    def side(w):
        return w[2] if own else 1 - w[2]

    return pl.pallas_call(
        functools.partial(finish_kernel, len(back), own),
        grid_spec=pltpu.PrefetchScalarGridSpec(
            num_scalar_prefetch=1,
            grid=(1,),
            in_specs=[pl.BlockSpec(x.shape, lambda i, w: (0, 0)) for x in back]
            + [
                pl.BlockSpec((items, width // 2), lambda i, w: (0, side(w))),
                pl.BlockSpec((1,) + log_s.shape[1:], lambda i, w: (side(w), 0, 0)),
            ]
            + [ANY] * len(others),
            out_specs=pl.BlockSpec((rows, steps, width // 2), lambda i, w: (0, 0, side(w))),
        ),
        out_shape=jax.ShapeDtypeStruct(shape, jnp.bfloat16),
        input_output_aliases={} if own else {len(back) + 3: 0},
        compiler_params=params(),
    )(where, *back, out_s, log_s, *others)


def local(queries, selected, placement, lengths, cache_k, cache_v, suffix_k, suffix_v):
    rows_here, steps, width = queries.shape
    size = lax.axis_size("ctx")
    blocks_here, _, kv_width = cache_k.shape
    group_size = width // kv_width
    items = rows_here * steps
    chips = size // 2

    def swap(x, bits):
        return lax.ppermute(x, "ctx", [(i, i ^ bits) for i in range(size)]) if bits else x

    own = lax.axis_index("ctx")
    where = jnp.stack([own * blocks_here, (own ^ 1) * blocks_here, own & 1]).astype(jnp.int32)
    place = placement.reshape(1, -1)
    *packed, halves = pack(queries, selected, cache_k, cache_v)
    halves = swap(halves, 1)
    out_s, log_s = attend_suffix(lengths, queries, suffix_k, suffix_v)
    attend = functools.partial(attend_blocks, where, place)
    if chips <= 4:
        calls = [[2, 3], [1], [0]] if chips == 4 else [[k] for k in range(chips - 1, -1, -1)]
        arrived = {
            k: [swap(packed[0], 2 * k), swap(packed[1], 2 * k + 1)] for call in calls for k in call
        }
        back = []
        after = [log_s]
        for call in calls:
            pieces = [piece for k in call for piece in arrived[k]]
            partial = attend(pieces, cache_k, cache_v, halves, group_size, after)
            after = [partial[0], arrived[0][1]]
            back += [swap(x, 2 * k) for k, x in zip(call, partial)]
    else:
        same = [[2 * z + core for z in range(chips)] for core in range(2)]
        chip = jnp.concatenate([packed[0], swap(packed[1], 1)], axis=0)
        every = lax.all_gather(chip, "ctx", axis=0, tiled=True, axis_index_groups=same)
        (partial,) = attend([every], cache_k, cache_v, halves, group_size, [log_s])
        back = [
            lax.all_to_all(
                partial, "ctx", split_axis=0, concat_axis=0, tiled=True, axis_index_groups=same
            )
        ]
    other = swap(merge_other(back, items), 1)
    half = finish(where, back, out_s, log_s, queries.shape, None)
    return finish(where, [other], out_s, log_s, queries.shape, half)


def solution(mesh):
    rows = P(("groups", "ctx"), None, "rows")
    in_specs = (
        rows,
        P(("groups", "ctx"), None, None),
        P("groups"),
        P(("groups", "ctx")),
        rows,
        rows,
        rows,
        rows,
    )
    return jax.shard_map(local, mesh=mesh, in_specs=in_specs, out_specs=rows, check_vma=False)
```

```python
import functools
import math

import jax
import jax.numpy as jnp
from jax import lax
from jax.experimental import pallas as pl
from jax.experimental.pallas import tpu as pltpu
from jax.sharding import PartitionSpec as P

HD = 128
LANES = 128
SCALE = 1.0 / math.sqrt(HD)
LOG2E = math.log2(math.e)
NONE = -1e30
LOW, HIGH = 2.0**-80, 2.0**100
VMEM = 36 * 1024 * 1024
ROWS_STEP = 512


def split3(x):
    high = x.astype(jnp.bfloat16)
    rest = x - high.astype(jnp.float32)
    middle = rest.astype(jnp.bfloat16)
    low = (rest - middle.astype(jnp.float32)).astype(jnp.bfloat16)
    return high, middle, low


def dot_nt(a, b):
    return lax.dot_general(a, b, (((1,), (1,)), ((), ())), preferred_element_type=jnp.float32)


def dot_tn(a, b):
    return lax.dot_general(a, b, (((0,), (0,)), ((), ())), preferred_element_type=jnp.float32)


def stack(arrays):
    return arrays[0] if len(arrays) == 1 else jnp.concatenate(arrays, axis=0)


def params():
    return pltpu.CompilerParams(vmem_limit_bytes=VMEM)


def flat(x):
    return x.astype(jnp.float32).reshape(x.shape[0] * x.shape[1], x.shape[2])


ANY = pl.BlockSpec(memory_space=pl.ANY)


def pack_kernel(q_ref, selected_ref, k_ref, v_ref, mine_ref, other_ref, out_ref, held, in_sems, out_sems):
    blocks, _, kv_columns = k_ref.shape
    kv_half = kv_columns // 2
    half = q_ref.shape[2] // 2
    core = lax.axis_index("ctx") % 2
    kv_start = pl.multiple_of((1 - core) * kv_half, LANES)
    reads, writes = [], []
    for n, ref in enumerate((k_ref, v_ref)):
        for b in range(blocks):
            m = n * blocks + b
            source = ref.at[b, :, pl.ds(kv_start, kv_half)]
            reads.append(pltpu.make_async_copy(source, held.at[m], in_sems.at[m]))
            writes.append(pltpu.make_async_copy(held.at[m], out_ref.at[m], out_sems.at[m]))
    for read in reads:
        read.start()
    ids = flat(selected_ref[...])
    pad = jnp.full((ids.shape[0], LANES - ids.shape[1]), -1.0, jnp.float32)
    ids = jnp.concatenate([ids, pad], axis=1).astype(jnp.bfloat16)
    for ref, which in ((mine_ref, core), (other_ref, 1 - core)):
        start = pl.multiple_of(which * half, LANES)
        ref[:, :half] = flat(q_ref[:, :, pl.ds(start, half)]).astype(jnp.bfloat16)
        ref[:, half:] = ids
    for read, write in zip(reads, writes):
        read.wait()
        write.start()
    for write in writes:
        write.wait()


def pack(queries, selected, cache_k, cache_v):
    rows, steps, width = queries.shape
    blocks, tokens, columns = cache_k.shape
    shape = jax.ShapeDtypeStruct((rows * steps, width // 2 + LANES), jnp.bfloat16)
    kv_shape = (2 * blocks, tokens, columns // 2)
    whole = pl.BlockSpec(memory_space=pltpu.VMEM)
    return pl.pallas_call(
        pack_kernel,
        in_specs=[whole, whole, ANY, ANY],
        out_specs=[whole, whole, ANY],
        out_shape=[shape, shape, jax.ShapeDtypeStruct(kv_shape, jnp.bfloat16)],
        scratch_shapes=[
            pltpu.VMEM(kv_shape, jnp.bfloat16),
            pltpu.SemaphoreType.DMA((2 * blocks,)),
            pltpu.SemaphoreType.DMA((2 * blocks,)),
        ],
        compiler_params=params(),
    )(queries, selected, cache_k, cache_v)


def block_kernel(pieces, group_size, step, where_ref, place_ref, *refs):
    q_refs = refs[:pieces]
    id_refs = refs[pieces : 2 * pieces]
    own_k, own_v, next_k, next_v = refs[2 * pieces : 2 * pieces + 4]
    outs = max(1, pieces // 2)
    out_refs = refs[-2 - outs : -2]
    logs_ref, s_ref = refs[-2:]
    kv = pl.program_id(1)
    share = q_refs[0].shape[0]
    items = share * pieces
    kept = items // outs
    blocks, tokens, _ = own_k.shape
    lane = lax.broadcasted_iota(jnp.int32, (items, LANES), 1)
    first_head = kv * group_size
    mine = (lane >= first_head) & (lane < first_head + group_size)
    ids = stack([ref[...].astype(jnp.float32) for ref in id_refs])
    place = place_ref[...]
    block_ids = lax.broadcasted_iota(jnp.int32, place.shape, 1)
    keys = [ref.at[b] for ref in (own_k, next_k) for b in range(blocks)]
    values = [ref.at[b] for ref in (own_v, next_v) for b in range(blocks)]
    hits = []
    for base in (where_ref[0], where_ref[1]):
        for b in range(blocks):
            target = jnp.sum(
                jnp.where(place == base + b, block_ids, 0).astype(jnp.float32), axis=1, keepdims=True
            )
            hits.append(jnp.max(jnp.where(ids == target, 1.0, 0.0), axis=1, keepdims=True))
    some = hits[0]
    for hit in hits[1:]:
        some = jnp.maximum(some, hit)

    def write(head, out):
        start = pl.multiple_of((first_head + head) * HD, HD)
        out = out.astype(jnp.bfloat16)
        for n, ref in enumerate(out_refs):
            ref[:, pl.ds(start, HD)] = out[n * kept : (n + 1) * kept]

    listed = jnp.zeros((items, LANES), jnp.float32)
    for n, hit in enumerate(hits):
        listed = jnp.where(lane == n, hit, listed)
    wide = (items, step * items)
    column = lax.broadcasted_iota(jnp.int32, wide, 1) % items
    spread = jnp.where(column == lax.broadcasted_iota(jnp.int32, wide, 0), 1.0, 0.0)
    listed = dot_tn(listed, spread)
    totals = jnp.ones((items, LANES), jnp.float32)
    for first in range(0, group_size, step):
        q = stack(
            [ref[:, h * HD : (h + 1) * HD] for h in range(first, first + step) for ref in q_refs]
        )
        acc = jnp.zeros((HD, step * items), jnp.float32)
        total = jnp.zeros((1, step * items), jnp.float32)
        for n, (key, value) in enumerate(zip(keys, values)):
            p = jnp.exp2(dot_nt(key[...], q) * (SCALE * LOG2E))
            here = dot_tn(value[...], p.astype(jnp.bfloat16))
            hit = listed[n : n + 1] > 0.0
            acc = jnp.where(hit, acc + here, acc)
            total = jnp.where(hit, total + jnp.sum(p, axis=0, keepdims=True), total)
        out = (acc / jnp.where(total > 0.0, total, 1.0)).T
        total = jnp.broadcast_to(total, (8, step * items)).T
        for n in range(step):
            rows = slice(n * items, (n + 1) * items)
            write(first + n, out[rows])
            totals = jnp.where(lane == first_head + first + n, total[rows, :1], totals)
    good = (totals > LOW) & (totals < HIGH)
    bad = jnp.max(jnp.where(good | (some == 0.0), 0.0, 1.0))
    logs = jnp.where((some > 0.0) & good, jnp.log(jnp.where(good, totals, 1.0)), NONE)
    logs_ref[...] = jnp.where(mine, logs, logs_ref[...])

    @pl.when(bad > 0.0)
    def _():
        @pl.loop(0, group_size)
        def _(head):
            start = pl.multiple_of(head * HD, HD)
            q = stack([ref[:, pl.ds(start, HD)] for ref in q_refs])
            top = jnp.full((items, 1), NONE, jnp.float32)
            for n, (hit, key) in enumerate(zip(hits, keys)):
                s = dot_nt(q, key[...])
                s_ref[n] = s
                here = jnp.max(s, axis=1, keepdims=True)
                top = jnp.where(hit > 0.0, jnp.maximum(top, here), top)
            acc = jnp.zeros((items, HD), jnp.float32)
            total = jnp.zeros((items, 1), jnp.float32)
            for n, (hit, value) in enumerate(zip(hits, values)):
                p = jnp.exp2((s_ref[n] - top) * (SCALE * LOG2E))
                p = jnp.where(hit > 0.0, p, 0.0)
                total += jnp.sum(p, axis=1, keepdims=True)
                acc += jnp.dot(p.astype(jnp.bfloat16), value[...], preferred_element_type=jnp.float32)
            safe = jnp.where(some > 0.0, total, 1.0)
            write(head, jnp.where(some > 0.0, acc / safe, 0.0))
            log = jnp.where(some > 0.0, top * SCALE + jnp.log(safe), NONE)
            logs_ref[...] = jnp.where(lane == first_head + head, log, logs_ref[...])

    @pl.when(kv == pl.num_programs(1) - 1)
    def _():
        heads = (out_refs[0].shape[1] - LANES) // HD
        parts = jnp.concatenate([x[:, :heads] for x in split3(logs_ref[...])], axis=1)
        pad = jnp.zeros((items, LANES - 3 * heads), jnp.bfloat16)
        parts = jnp.concatenate([parts, pad], axis=1)
        for n, ref in enumerate(out_refs):
            ref[:, heads * HD :] = parts[n * kept : (n + 1) * kept]


def attend_blocks(where, place, queries, cache_k, cache_v, halves, group_size, after):
    pieces = len(queries)
    rows, columns = queries[0].shape
    blocks, tokens, kv_width = cache_k.shape
    kv_half = kv_width // HD // 2
    share = min(rows, 64)
    items = share * pieces
    outs = max(1, pieces // 2)
    own = pl.BlockSpec((blocks, tokens, HD), lambda i, g, w: (0, 0, w[2] * kv_half + g))
    queries_block = pl.BlockSpec((share, group_size * HD), lambda i, g, w: (i, g))
    ids_block = pl.BlockSpec((share, LANES), lambda i, g, w: (i, columns // LANES - 1))
    return pl.pallas_call(
        functools.partial(block_kernel, pieces, group_size, min(group_size, max(1, ROWS_STEP // items))),
        grid_spec=pltpu.PrefetchScalarGridSpec(
            num_scalar_prefetch=1,
            grid=(rows // share, kv_half),
            in_specs=[pl.BlockSpec(place.shape, lambda i, g, w: (0, 0))]
            + [queries_block] * pieces
            + [ids_block] * pieces
            + [own, own]
            + [
                pl.BlockSpec((blocks, tokens, HD), lambda i, g, w: (0, 0, g)),
                pl.BlockSpec((blocks, tokens, HD), lambda i, g, w: (1, 0, g)),
            ]
            + [pl.BlockSpec(memory_space=pl.ANY)] * len(after),
            out_specs=[pl.BlockSpec((items // outs, columns), lambda i, g, w: (i, 0))] * outs,
            scratch_shapes=[
                pltpu.VMEM((items, LANES), jnp.float32),
                pltpu.VMEM((2 * blocks, items, tokens), jnp.float32),
            ],
        ),
        out_shape=[jax.ShapeDtypeStruct((rows * pieces // outs, columns), jnp.bfloat16)] * outs,
        compiler_params=params(),
        cost_estimate=pl.CostEstimate(
            flops=rows * pieces * tokens * columns,
            bytes_accessed=4 * rows * pieces * columns,
            transcendentals=rows * pieces * columns,
        ),
    )(where, place, *queries, *queries, cache_k, cache_v, halves, halves, *after)


def suffix_kernel(group_size, lengths_ref, q_ref, k_ref, v_ref, pass_ref, out_ref, log_ref, passed_ref):
    passed_ref[...] = pass_ref[...]
    rows_here, steps, width = q_ref.shape
    tokens = k_ref.shape[1]
    kv_here = k_ref.shape[2] // HD
    items = rows_here * steps
    span = rows_here * tokens
    half = width // HD // 2
    lane = lax.broadcasted_iota(jnp.int32, (items, LANES), 1)
    token = lax.broadcasted_iota(jnp.int32, (items, span), 1)
    item = lax.broadcasted_iota(jnp.int32, (items, span), 0)
    seen = jnp.zeros((items, span), jnp.float32)
    for r in range(rows_here):
        offset = token - r * tokens
        inside = (item // steps == r) & (offset >= 0) & (offset < lengths_ref[r] + item % steps)
        seen = jnp.where(inside, 1.0, seen)
    seen = jnp.concatenate([seen] * group_size, axis=0)
    logs = [jnp.zeros((items, LANES), jnp.float32)] * 2
    for g in range(kv_here):
        columns = slice(g * group_size * HD, (g + 1) * group_size * HD)
        q_all = flat(q_ref[:, :, columns]).astype(jnp.bfloat16)
        q = stack([q_all[:, n * HD : (n + 1) * HD] for n in range(group_size)])
        keys = k_ref[:, :, g * HD : (g + 1) * HD].reshape(span, HD)
        values = v_ref[:, :, g * HD : (g + 1) * HD].reshape(span, HD)
        s = jnp.where(seen > 0.0, dot_nt(q, keys), NONE)
        highest = jnp.max(s, axis=1, keepdims=True)
        p = jnp.exp2((s - highest) * (SCALE * LOG2E))
        p = jnp.where(seen > 0.0, p, 0.0)
        total = jnp.sum(p, axis=1, keepdims=True)
        out = jnp.dot(p.astype(jnp.bfloat16), values, preferred_element_type=jnp.float32) / total
        log = highest * SCALE + jnp.log(total)
        for n in range(group_size):
            h = g * group_size + n
            out_ref[:, h * HD : (h + 1) * HD] = out[n * items : (n + 1) * items]
            side = h // half
            logs[side] = jnp.where(lane == h % half, log[n * items : (n + 1) * items], logs[side])
    for side in range(2):
        log_ref[side] = logs[side]


def attend_suffix(lengths, queries, suffix_k, suffix_v, passing):
    rows, steps, width = queries.shape
    _, tokens, kv_width = suffix_k.shape
    items = rows * steps
    whole = lambda i, n: (0, 0, 0)
    return pl.pallas_call(
        functools.partial(suffix_kernel, width // kv_width),
        grid_spec=pltpu.PrefetchScalarGridSpec(
            num_scalar_prefetch=1,
            grid=(1,),
            in_specs=[pl.BlockSpec(x.shape, whole) for x in (queries, suffix_k, suffix_v)]
            + [pl.BlockSpec(passing.shape, lambda i, n: (0, 0))],
            out_specs=[
                pl.BlockSpec((items, width), lambda i, n: (0, 0)),
                pl.BlockSpec((2, items, LANES), whole),
                pl.BlockSpec(passing.shape, lambda i, n: (0, 0)),
            ],
        ),
        out_shape=(
            jax.ShapeDtypeStruct((items, width), jnp.float32),
            jax.ShapeDtypeStruct((2, items, LANES), jnp.float32),
            jax.ShapeDtypeStruct(passing.shape, passing.dtype),
        ),
        compiler_params=params(),
        cost_estimate=pl.CostEstimate(
            flops=16 * items * rows * tokens * width,
            bytes_accessed=4 * suffix_k.size + 6 * items * width,
            transcendentals=items * rows * tokens * width // HD,
        ),
    )(lengths, queries, suffix_k, suffix_v, passing)


def weigh(parts, items, heads):
    columns = heads * HD
    logs = []
    for ref, start in parts:
        x = ref[start : start + items, columns:].astype(jnp.float32)
        logs.append(x[:, :heads] + x[:, heads : 2 * heads] + x[:, 2 * heads : 3 * heads])
    return logs


def shares(logs):
    top = logs[0]
    for log in logs[1:]:
        top = jnp.maximum(top, log)
    factors = [jnp.exp(log - top) for log in logs]
    total = factors[0]
    for factor in factors[1:]:
        total += factor
    inverse = 1.0 / total
    return [factor * inverse for factor in factors], top + jnp.log(total)


def parts_of(refs, items, side):
    return [(ref, start + side * items) for ref in refs for start in range(0, ref.shape[0], 2 * items)]


def other_kernel(*refs):
    out_ref = refs[-1]
    items = out_ref.shape[0]
    columns = out_ref.shape[1] - LANES
    heads = columns // HD
    parts = parts_of(refs[:-1], items, 1)
    factors, log = shares(weigh(parts, items, heads))
    for h in range(heads):
        span = slice(h * HD, (h + 1) * HD)
        acc = jnp.zeros((items, HD), jnp.float32)
        for factor, (ref, start) in zip(factors, parts):
            acc += factor[:, h : h + 1] * ref[start : start + items, span].astype(jnp.float32)
        out_ref[:, span] = acc
    pad = jnp.zeros((items, LANES - heads), jnp.float32)
    out_ref[:, columns:] = jnp.concatenate([log, pad], axis=1)


def merge_other(back, items):
    return pl.pallas_call(
        other_kernel,
        out_shape=jax.ShapeDtypeStruct((items, back[0].shape[1]), jnp.float32),
        compiler_params=params(),
    )(*back)


def finish_kernel(arrays, own, where_ref, *refs):
    back_refs = refs[:arrays]
    out_s_ref, log_s_ref = refs[arrays : arrays + 2]
    out_ref = refs[-1]
    rows, steps, columns = out_ref.shape
    items = rows * steps
    heads = columns // HD
    log_s = log_s_ref[0][:, :heads]
    if own:
        parts = parts_of(back_refs, items, 0)
        logs = weigh(parts, items, heads)
    else:
        parts = [(back_refs[0], 0)]
        logs = [back_refs[0][:, columns : columns + heads]]
    factors, _ = shares([log_s] + logs)
    for h in range(heads):
        span = slice(h * HD, (h + 1) * HD)
        acc = factors[0][:, h : h + 1] * out_s_ref[:, span]
        for factor, (ref, start) in zip(factors[1:], parts):
            acc += factor[:, h : h + 1] * ref[start : start + items, span].astype(jnp.float32)
        for row in range(rows):
            out_ref[row, :, span] = acc[row * steps : (row + 1) * steps].astype(jnp.bfloat16)


def finish(where, back, out_s, log_s, shape, so_far):
    rows, steps, width = shape
    items = rows * steps
    own = so_far is None
    others = [] if own else [so_far]

    def side(w):
        return w[2] if own else 1 - w[2]

    return pl.pallas_call(
        functools.partial(finish_kernel, len(back), own),
        grid_spec=pltpu.PrefetchScalarGridSpec(
            num_scalar_prefetch=1,
            grid=(1,),
            in_specs=[pl.BlockSpec(x.shape, lambda i, w: (0, 0)) for x in back]
            + [
                pl.BlockSpec((items, width // 2), lambda i, w: (0, side(w))),
                pl.BlockSpec((1,) + log_s.shape[1:], lambda i, w: (side(w), 0, 0)),
            ]
            + [ANY] * len(others),
            out_specs=pl.BlockSpec((rows, steps, width // 2), lambda i, w: (0, 0, side(w))),
        ),
        out_shape=jax.ShapeDtypeStruct(shape, jnp.bfloat16),
        input_output_aliases={} if own else {len(back) + 3: 0},
        compiler_params=params(),
    )(where, *back, out_s, log_s, *others)


def local(queries, selected, placement, lengths, cache_k, cache_v, suffix_k, suffix_v):
    rows_here, steps, width = queries.shape
    size = lax.axis_size("ctx")
    blocks_here, _, kv_width = cache_k.shape
    group_size = width // kv_width
    items = rows_here * steps
    chips = size // 2

    def swap(x, bits):
        return lax.ppermute(x, "ctx", [(i, i ^ bits) for i in range(size)]) if bits else x

    own = lax.axis_index("ctx")
    where = jnp.stack([own * blocks_here, (own ^ 1) * blocks_here, own & 1]).astype(jnp.int32)
    place = placement.reshape(1, -1)
    *packed, halves = pack(queries, selected, cache_k, cache_v)
    halves = swap(halves, 1)
    out_s, log_s, passed = attend_suffix(lengths, queries, suffix_k, suffix_v, packed[1])
    attend = functools.partial(attend_blocks, where, place)
    if chips <= 4:
        calls = [[2, 1], [3], [0]] if chips == 4 else [[k] for k in range(chips - 1, -1, -1)]
        arrived = {0: [packed[0], swap(passed, 1)]}
        for k in range(1, chips):
            if k == 3:
                arrived[k] = [swap(x, 2) for x in arrived[2]]
            else:
                arrived[k] = [swap(packed[0], 2 * k), swap(packed[1], 2 * k + 1)]
        back = []
        after = [log_s]
        for call in calls:
            pieces = [piece for k in call for piece in arrived[k]]
            partial = attend(pieces, cache_k, cache_v, halves, group_size, after)
            after = [partial[0], arrived[0][1]]
            back += [swap(x, 2 * k) for k, x in zip(call, partial)]
    else:
        same = [[2 * z + core for z in range(chips)] for core in range(2)]
        chip = jnp.concatenate([packed[0], swap(passed, 1)], axis=0)
        every = lax.all_gather(chip, "ctx", axis=0, tiled=True, axis_index_groups=same)
        (partial,) = attend([every], cache_k, cache_v, halves, group_size, [log_s])
        back = [
            lax.all_to_all(
                partial, "ctx", split_axis=0, concat_axis=0, tiled=True, axis_index_groups=same
            )
        ]
    other = swap(merge_other(back, items), 1)
    half = finish(where, back, out_s, log_s, queries.shape, None)
    return finish(where, [other], out_s, log_s, queries.shape, half)


def solution(mesh):
    rows = P(("groups", "ctx"), None, "rows")
    in_specs = (
        rows,
        P(("groups", "ctx"), None, None),
        P("groups"),
        P(("groups", "ctx")),
        rows,
        rows,
        rows,
        rows,
    )
    return jax.shard_map(local, mesh=mesh, in_specs=in_specs, out_specs=rows, check_vma=False)
```

```python
import functools
import math

import jax
import jax.numpy as jnp
from jax import lax
from jax.experimental import pallas as pl
from jax.experimental.pallas import tpu as pltpu
from jax.sharding import PartitionSpec as P

HD = 128
LANES = 128
SCALE = 1.0 / math.sqrt(HD)
LOG2E = math.log2(math.e)
NONE = -1e30
LOW, HIGH = 2.0**-80, 2.0**100
VMEM = 121 * 1024 * 1024 // 2
SMALL = 16 * 1024 * 1024
ROWS_STEP = 512


def split3(x):
    high = x.astype(jnp.bfloat16)
    rest = x - high.astype(jnp.float32)
    middle = rest.astype(jnp.bfloat16)
    low = (rest - middle.astype(jnp.float32)).astype(jnp.bfloat16)
    return high, middle, low


def dot_nt(a, b):
    return lax.dot_general(a, b, (((1,), (1,)), ((), ())), preferred_element_type=jnp.float32)


def dot_tn(a, b):
    return lax.dot_general(a, b, (((0,), (0,)), ((), ())), preferred_element_type=jnp.float32)


def stack(arrays):
    return arrays[0] if len(arrays) == 1 else jnp.concatenate(arrays, axis=0)


def params(limit=VMEM):
    return pltpu.CompilerParams(vmem_limit_bytes=limit)


def flat(x):
    return x.astype(jnp.float32).reshape(x.shape[0] * x.shape[1], x.shape[2])


ANY = pl.BlockSpec(memory_space=pl.ANY)


def pack_kernel(q_ref, selected_ref, mine_ref, other_ref):
    half = q_ref.shape[2] // 2
    core = lax.axis_index("ctx") % 2
    ids = flat(selected_ref[...])
    pad = jnp.full((ids.shape[0], LANES - ids.shape[1]), -1.0, jnp.float32)
    ids = jnp.concatenate([ids, pad], axis=1).astype(jnp.bfloat16)
    for ref, which in ((mine_ref, core), (other_ref, 1 - core)):
        start = pl.multiple_of(which * half, LANES)
        ref[:, :half] = flat(q_ref[:, :, pl.ds(start, half)]).astype(jnp.bfloat16)
        ref[:, half:] = ids


def pack(queries, selected):
    rows, steps, width = queries.shape
    shape = jax.ShapeDtypeStruct((rows * steps, width // 2 + LANES), jnp.bfloat16)
    return pl.pallas_call(pack_kernel, out_shape=[shape, shape], compiler_params=params())(
        queries, selected
    )


def block_kernel(pieces, outs, group_size, step, where_ref, place_ref, *refs):
    q_refs = refs[:pieces]
    id_refs = refs[pieces : 2 * pieces]
    own_k, own_v, next_k, next_v = refs[2 * pieces : 2 * pieces + 4]
    out_refs = refs[-2 - outs : -2]
    logs_ref, s_ref = refs[-2:]
    kv = pl.program_id(1)
    share = q_refs[0].shape[0]
    items = share * pieces
    kept = items // outs
    blocks, tokens, _ = own_k.shape
    lane = lax.broadcasted_iota(jnp.int32, (items, LANES), 1)
    first_head = kv * group_size
    mine = (lane >= first_head) & (lane < first_head + group_size)
    ids = stack([ref[...].astype(jnp.float32) for ref in id_refs])
    place = place_ref[...]
    block_ids = lax.broadcasted_iota(jnp.int32, place.shape, 1)
    keys = [ref.at[b] for ref in (own_k, next_k) for b in range(blocks)]
    values = [ref.at[b] for ref in (own_v, next_v) for b in range(blocks)]
    hits = []
    for base in (where_ref[0], where_ref[1]):
        for b in range(blocks):
            target = jnp.sum(
                jnp.where(place == base + b, block_ids, 0).astype(jnp.float32), axis=1, keepdims=True
            )
            hits.append(jnp.max(jnp.where(ids == target, 1.0, 0.0), axis=1, keepdims=True))
    some = hits[0]
    for hit in hits[1:]:
        some = jnp.maximum(some, hit)

    def write(head, out):
        start = pl.multiple_of((first_head + head) * HD, HD)
        out = out.astype(jnp.bfloat16)
        for n, ref in enumerate(out_refs):
            ref[:, pl.ds(start, HD)] = out[n * kept : (n + 1) * kept]

    listed = jnp.zeros((items, LANES), jnp.float32)
    for n, hit in enumerate(hits):
        listed = jnp.where(lane == n, hit, listed)
    wide = (items, step * items)
    column = lax.broadcasted_iota(jnp.int32, wide, 1) % items
    spread = jnp.where(column == lax.broadcasted_iota(jnp.int32, wide, 0), 1.0, 0.0)
    listed = dot_tn(listed, spread)
    totals = jnp.ones((items, LANES), jnp.float32)
    for first in range(0, group_size, step):
        q = stack(
            [ref[:, h * HD : (h + 1) * HD] for h in range(first, first + step) for ref in q_refs]
        )
        acc = jnp.zeros((HD, step * items), jnp.float32)
        total = jnp.zeros((1, step * items), jnp.float32)
        for n, (key, value) in enumerate(zip(keys, values)):
            p = jnp.exp2(dot_nt(key[...], q) * (SCALE * LOG2E))
            here = dot_tn(value[...], p.astype(jnp.bfloat16))
            hit = listed[n : n + 1] > 0.0
            acc = jnp.where(hit, acc + here, acc)
            total = jnp.where(hit, total + jnp.sum(p, axis=0, keepdims=True), total)
        out = (acc / jnp.where(total > 0.0, total, 1.0)).T
        total = jnp.broadcast_to(total, (8, step * items)).T
        for n in range(step):
            rows = slice(n * items, (n + 1) * items)
            write(first + n, out[rows])
            totals = jnp.where(lane == first_head + first + n, total[rows, :1], totals)
    good = (totals > LOW) & (totals < HIGH)
    bad = jnp.max(jnp.where(good | (some == 0.0), 0.0, 1.0))
    logs = jnp.where((some > 0.0) & good, jnp.log(jnp.where(good, totals, 1.0)), NONE)
    logs_ref[...] = jnp.where(mine, logs, logs_ref[...])

    @pl.when(bad > 0.0)
    def _():
        @pl.loop(0, group_size)
        def _(head):
            start = pl.multiple_of(head * HD, HD)
            q = stack([ref[:, pl.ds(start, HD)] for ref in q_refs])
            top = jnp.full((items, 1), NONE, jnp.float32)
            for n, (hit, key) in enumerate(zip(hits, keys)):
                s = dot_nt(q, key[...])
                s_ref[n] = s
                here = jnp.max(s, axis=1, keepdims=True)
                top = jnp.where(hit > 0.0, jnp.maximum(top, here), top)
            acc = jnp.zeros((items, HD), jnp.float32)
            total = jnp.zeros((items, 1), jnp.float32)
            for n, (hit, value) in enumerate(zip(hits, values)):
                p = jnp.exp2((s_ref[n] - top) * (SCALE * LOG2E))
                p = jnp.where(hit > 0.0, p, 0.0)
                total += jnp.sum(p, axis=1, keepdims=True)
                acc += jnp.dot(p.astype(jnp.bfloat16), value[...], preferred_element_type=jnp.float32)
            safe = jnp.where(some > 0.0, total, 1.0)
            write(head, jnp.where(some > 0.0, acc / safe, 0.0))
            log = jnp.where(some > 0.0, top * SCALE + jnp.log(safe), NONE)
            logs_ref[...] = jnp.where(lane == first_head + head, log, logs_ref[...])

    @pl.when(kv == pl.num_programs(1) - 1)
    def _():
        heads = (out_refs[0].shape[1] - LANES) // HD
        parts = jnp.concatenate([x[:, :heads] for x in split3(logs_ref[...])], axis=1)
        pad = jnp.zeros((items, LANES - 3 * heads), jnp.bfloat16)
        parts = jnp.concatenate([parts, pad], axis=1)
        for n, ref in enumerate(out_refs):
            ref[:, heads * HD :] = parts[n * kept : (n + 1) * kept]


def attend_blocks(where, place, caches, group_size, queries, outs, after):
    pieces = len(queries)
    rows, columns = queries[0].shape
    blocks, tokens, kv_width = caches[0].shape
    kv_half = kv_width // HD // 2
    share = min(rows, 64)
    items = share * pieces
    cache_block = pl.BlockSpec((blocks, tokens, HD), lambda i, g, w: (0, 0, w[2] * kv_half + g))
    queries_block = pl.BlockSpec((share, group_size * HD), lambda i, g, w: (i, g))
    ids_block = pl.BlockSpec((share, LANES), lambda i, g, w: (i, columns // LANES - 1))
    return pl.pallas_call(
        functools.partial(block_kernel, pieces, outs, group_size, min(group_size, max(1, ROWS_STEP // items))),
        grid_spec=pltpu.PrefetchScalarGridSpec(
            num_scalar_prefetch=1,
            grid=(rows // share, kv_half),
            in_specs=[pl.BlockSpec(place.shape, lambda i, g, w: (0, 0))]
            + [queries_block] * pieces
            + [ids_block] * pieces
            + [cache_block] * 4
            + [pl.BlockSpec(memory_space=pl.ANY)] * len(after),
            out_specs=[pl.BlockSpec((items // outs, columns), lambda i, g, w: (i, 0))] * outs,
            scratch_shapes=[
                pltpu.VMEM((items, LANES), jnp.float32),
                pltpu.VMEM((2 * blocks, items, tokens), jnp.float32),
            ],
        ),
        out_shape=[jax.ShapeDtypeStruct((rows * pieces // outs, columns), jnp.bfloat16)] * outs,
        compiler_params=params(),
        cost_estimate=pl.CostEstimate(
            flops=rows * pieces * tokens * columns,
            bytes_accessed=4 * rows * pieces * columns,
            transcendentals=rows * pieces * columns,
        ),
    )(where, place, *queries, *queries, *caches, *after)


def suffix_kernel(group_size, lengths_ref, q_ref, k_ref, v_ref, out_ref, log_ref):
    rows_here, steps, width = q_ref.shape
    tokens = k_ref.shape[1]
    kv_here = k_ref.shape[2] // HD
    items = rows_here * steps
    span = rows_here * tokens
    half = width // HD // 2
    lane = lax.broadcasted_iota(jnp.int32, (items, LANES), 1)
    token = lax.broadcasted_iota(jnp.int32, (items, span), 1)
    item = lax.broadcasted_iota(jnp.int32, (items, span), 0)
    seen = jnp.zeros((items, span), jnp.float32)
    for r in range(rows_here):
        offset = token - r * tokens
        inside = (item // steps == r) & (offset >= 0) & (offset < lengths_ref[r] + item % steps)
        seen = jnp.where(inside, 1.0, seen)
    seen = jnp.concatenate([seen] * group_size, axis=0)
    logs = [jnp.zeros((items, LANES), jnp.float32)] * 2
    for g in range(kv_here):
        columns = slice(g * group_size * HD, (g + 1) * group_size * HD)
        q_all = flat(q_ref[:, :, columns]).astype(jnp.bfloat16)
        q = stack([q_all[:, n * HD : (n + 1) * HD] for n in range(group_size)])
        keys = k_ref[:, :, g * HD : (g + 1) * HD].reshape(span, HD)
        values = v_ref[:, :, g * HD : (g + 1) * HD].reshape(span, HD)
        s = jnp.where(seen > 0.0, dot_nt(q, keys), NONE)
        highest = jnp.max(s, axis=1, keepdims=True)
        p = jnp.exp2((s - highest) * (SCALE * LOG2E))
        p = jnp.where(seen > 0.0, p, 0.0)
        total = jnp.sum(p, axis=1, keepdims=True)
        out = jnp.dot(p.astype(jnp.bfloat16), values, preferred_element_type=jnp.float32) / total
        log = highest * SCALE + jnp.log(total)
        for n in range(group_size):
            h = g * group_size + n
            out_ref[:, h * HD : (h + 1) * HD] = out[n * items : (n + 1) * items]
            side = h // half
            logs[side] = jnp.where(lane == h % half, log[n * items : (n + 1) * items], logs[side])
    for side in range(2):
        log_ref[side] = logs[side]


def attend_suffix(lengths, queries, suffix_k, suffix_v):
    rows, steps, width = queries.shape
    _, tokens, kv_width = suffix_k.shape
    items = rows * steps
    whole = lambda i, n: (0, 0, 0)
    return pl.pallas_call(
        functools.partial(suffix_kernel, width // kv_width),
        grid_spec=pltpu.PrefetchScalarGridSpec(
            num_scalar_prefetch=1,
            grid=(1,),
            in_specs=[pl.BlockSpec(x.shape, whole) for x in (queries, suffix_k, suffix_v)],
            out_specs=[
                pl.BlockSpec((items, width), lambda i, n: (0, 0)),
                pl.BlockSpec((2, items, LANES), whole),
            ],
        ),
        out_shape=(
            jax.ShapeDtypeStruct((items, width), jnp.float32),
            jax.ShapeDtypeStruct((2, items, LANES), jnp.float32),
        ),
        compiler_params=params(),
        cost_estimate=pl.CostEstimate(
            flops=16 * items * rows * tokens * width,
            bytes_accessed=4 * suffix_k.size + 6 * items * width,
            transcendentals=items * rows * tokens * width // HD,
        ),
    )(lengths, queries, suffix_k, suffix_v)


def weigh(parts, items, heads):
    columns = heads * HD
    logs = []
    for ref, start in parts:
        x = ref[start : start + items, columns:].astype(jnp.float32)
        logs.append(x[:, :heads] + x[:, heads : 2 * heads] + x[:, 2 * heads : 3 * heads])
    return logs


def shares(logs):
    top = logs[0]
    for log in logs[1:]:
        top = jnp.maximum(top, log)
    factors = [jnp.exp(log - top) for log in logs]
    total = factors[0]
    for factor in factors[1:]:
        total += factor
    inverse = 1.0 / total
    return [factor * inverse for factor in factors], top + jnp.log(total)


def merge_kernel(sides, *refs):
    out_refs = refs[-len(sides) :]
    items, columns = out_refs[0].shape
    columns -= LANES
    heads = columns // HD
    pad = jnp.zeros((items, LANES - heads), jnp.float32)
    taken = 0
    for count, out_ref in zip(sides, out_refs):
        back_refs = refs[taken : taken + count]
        taken += count
        parts = [(ref, start) for ref in back_refs for start in range(0, ref.shape[0], items)]
        factors, log = shares(weigh(parts, items, heads))
        for h in range(heads):
            span = slice(h * HD, (h + 1) * HD)
            acc = jnp.zeros((items, HD), jnp.float32)
            for factor, (ref, start) in zip(factors, parts):
                acc += factor[:, h : h + 1] * ref[start : start + items, span].astype(jnp.float32)
            out_ref[:, span] = acc
        out_ref[:, columns:] = jnp.concatenate([log, pad], axis=1)


def merge(sides, items, after):
    arrays = [x for side in sides for x in side]
    shape = jax.ShapeDtypeStruct((items, arrays[0].shape[1]), jnp.float32)
    return pl.pallas_call(
        functools.partial(merge_kernel, [len(side) for side in sides]),
        in_specs=[pl.BlockSpec(memory_space=pltpu.VMEM)] * len(arrays) + [ANY] * len(after),
        out_shape=[shape, shape],
        compiler_params=params(SMALL),
        cost_estimate=pl.CostEstimate(
            flops=1 << 30, bytes_accessed=8 * shape.size, transcendentals=items
        ),
    )(*arrays, *after)


def finish_kernel(late, *refs):
    out_s_ref, log_s_ref, out_ref = refs[-3:]
    rows, steps, width = out_ref.shape
    items = rows * steps
    columns = width // 2
    heads = columns // HD
    core = lax.axis_index("ctx") % 2
    for side, which in ((0, core), (1, 1 - core)):
        merged_ref, *late_refs = refs[side * (late + 1) : (side + 1) * (late + 1)]
        parts = [(ref, 0) for ref in late_refs]
        logs = [log_s_ref[which][:, :heads], merged_ref[:, columns : columns + heads]]
        factors, _ = shares(logs + weigh(parts, items, heads))
        for h in range(heads):
            here = slice(h * HD, (h + 1) * HD)
            span = pl.ds(pl.multiple_of(which * columns + h * HD, HD), HD)
            acc = factors[0][:, h : h + 1] * out_s_ref[:, span]
            acc += factors[1][:, h : h + 1] * merged_ref[:, here]
            for factor, (ref, _) in zip(factors[2:], parts):
                acc += factor[:, h : h + 1] * ref[:, here].astype(jnp.float32)
            for row in range(rows):
                out_ref[row, :, span] = acc[row * steps : (row + 1) * steps].astype(jnp.bfloat16)


def finish(own, other, out_s, log_s, shape):
    return pl.pallas_call(
        functools.partial(finish_kernel, len(own) - 1),
        out_shape=jax.ShapeDtypeStruct(shape, jnp.bfloat16),
        compiler_params=params(SMALL),
    )(*own, *other, out_s, log_s)


def local(queries, selected, placement, lengths, cache_k, cache_v, suffix_k, suffix_v):
    rows_here, steps, width = queries.shape
    size = lax.axis_size("ctx")
    blocks_here, _, kv_width = cache_k.shape
    group_size = width // kv_width
    items = rows_here * steps
    chips = size // 2

    def swap(x, bits):
        return lax.ppermute(x, "ctx", [(i, i ^ bits) for i in range(size)]) if bits else x

    own = lax.axis_index("ctx")
    where = jnp.stack([own * blocks_here, (own ^ 1) * blocks_here, own & 1]).astype(jnp.int32)
    place = placement.reshape(1, -1)
    caches = [cache_k, cache_v, swap(cache_k, 1), swap(cache_v, 1)]
    packed = pack(queries, selected)
    chip = jnp.concatenate([packed[0], swap(packed[1], 1)], axis=0)
    out_s, log_s = attend_suffix(lengths, queries, suffix_k, suffix_v)
    attend = functools.partial(attend_blocks, where, place, caches, group_size)
    if chips == 4:
        far, near = swap(chip, 4), swap(chip, 2)
        farthest = swap(far, 2)
        first = attend([far, near], 4, [log_s])
        sides = [[swap(first[n], 4 + n), swap(first[2 + n], 2 + n)] for n in range(2)]
        last = attend([farthest, chip], 4, [first[0]])
        late = [[swap(last[n], 6 + n), swap(last[2 + n], n)] for n in range(2)]
        after = [last[2]]
    else:
        same = [[2 * z + core for z in range(chips)] for core in range(2)]
        every = lax.all_gather(chip, "ctx", axis=0, tiled=True, axis_index_groups=same)
        (partial,) = attend([every], 1, [log_s])
        back = lax.all_to_all(
            partial, "ctx", split_axis=0, concat_axis=0, tiled=True, axis_index_groups=same
        ).reshape(chips, 2, items, -1)
        sides = [[swap(back[:, n].reshape(chips * items, -1), n)] for n in range(2)]
        late, after = [[], []], []
    merged = merge(sides, items, after)
    own, other = ([x] + y for x, y in zip(merged, late))
    return finish(own, other, out_s, log_s, queries.shape)


def solution(mesh):
    rows = P(("groups", "ctx"), None, "rows")
    in_specs = (
        rows,
        P(("groups", "ctx"), None, None),
        P("groups"),
        P(("groups", "ctx")),
        rows,
        rows,
        rows,
        rows,
    )
    return jax.shard_map(local, mesh=mesh, in_specs=in_specs, out_specs=rows, check_vma=False)
```

```python
import functools
import math

import jax
import jax.numpy as jnp
from jax import lax
from jax.experimental import pallas as pl
from jax.experimental.pallas import tpu as pltpu
from jax.sharding import PartitionSpec as P

HD = 128
LANES = 128
SCALE = 1.0 / math.sqrt(HD)
LOG2E = math.log2(math.e)
NONE = -1e30
LOW, HIGH = 2.0**-80, 2.0**100
VMEM = 121 * 1024 * 1024 // 2
SMALL = 16 * 1024 * 1024
ROWS_STEP = 1024


def split3(x):
    high = x.astype(jnp.bfloat16)
    rest = x - high.astype(jnp.float32)
    middle = rest.astype(jnp.bfloat16)
    low = (rest - middle.astype(jnp.float32)).astype(jnp.bfloat16)
    return high, middle, low


def dot_nt(a, b):
    return lax.dot_general(a, b, (((1,), (1,)), ((), ())), preferred_element_type=jnp.float32)


def dot_tn(a, b):
    return lax.dot_general(a, b, (((0,), (0,)), ((), ())), preferred_element_type=jnp.float32)


def stack(arrays):
    return arrays[0] if len(arrays) == 1 else jnp.concatenate(arrays, axis=0)


def params(limit=VMEM):
    return pltpu.CompilerParams(vmem_limit_bytes=limit)


def flat(x):
    return x.astype(jnp.float32).reshape(x.shape[0] * x.shape[1], x.shape[2])


ANY = pl.BlockSpec(memory_space=pl.ANY)


def pack_kernel(q_ref, selected_ref, mine_ref, other_ref):
    half = q_ref.shape[2] // 2
    core = lax.axis_index("ctx") % 2
    ids = flat(selected_ref[...])
    pad = jnp.full((ids.shape[0], LANES - ids.shape[1]), -1.0, jnp.float32)
    ids = jnp.concatenate([ids, pad], axis=1).astype(jnp.bfloat16)
    for ref, which in ((mine_ref, core), (other_ref, 1 - core)):
        start = pl.multiple_of(which * half, LANES)
        ref[:, :half] = flat(q_ref[:, :, pl.ds(start, half)]).astype(jnp.bfloat16)
        ref[:, half:] = ids


def pack(queries, selected):
    rows, steps, width = queries.shape
    shape = jax.ShapeDtypeStruct((rows * steps, width // 2 + LANES), jnp.bfloat16)
    return pl.pallas_call(pack_kernel, out_shape=[shape, shape], compiler_params=params())(
        queries, selected
    )


def block_kernel(pieces, outs, group_size, step, where_ref, place_ref, *refs):
    q_refs = refs[:pieces]
    id_refs = refs[pieces : 2 * pieces]
    own_k, own_v, next_k, next_v = refs[2 * pieces : 2 * pieces + 4]
    out_refs = refs[-2 - outs : -2]
    logs_ref, s_ref = refs[-2:]
    kv = pl.program_id(1)
    share = q_refs[0].shape[0]
    items = share * pieces
    kept = items // outs
    blocks, tokens, _ = own_k.shape
    lane = lax.broadcasted_iota(jnp.int32, (items, LANES), 1)
    first_head = kv * group_size
    mine = (lane >= first_head) & (lane < first_head + group_size)
    ids = stack([ref[...].astype(jnp.float32) for ref in id_refs])
    place = place_ref[...]
    block_ids = lax.broadcasted_iota(jnp.int32, place.shape, 1)
    keys = [ref.at[b] for ref in (own_k, next_k) for b in range(blocks)]
    values = [ref.at[b] for ref in (own_v, next_v) for b in range(blocks)]
    hits = []
    for base in (where_ref[0], where_ref[1]):
        for b in range(blocks):
            target = jnp.sum(
                jnp.where(place == base + b, block_ids, 0).astype(jnp.float32), axis=1, keepdims=True
            )
            hits.append(jnp.max(jnp.where(ids == target, 1.0, 0.0), axis=1, keepdims=True))
    some = hits[0]
    for hit in hits[1:]:
        some = jnp.maximum(some, hit)

    def write(head, out):
        start = pl.multiple_of((first_head + head) * HD, HD)
        out = out.astype(jnp.bfloat16)
        for n, ref in enumerate(out_refs):
            ref[:, pl.ds(start, HD)] = out[n * kept : (n + 1) * kept]

    listed = jnp.zeros((items, LANES), jnp.float32)
    for n, hit in enumerate(hits):
        listed = jnp.where(lane == n, hit, listed)
    wide = (items, step * items)
    column = lax.broadcasted_iota(jnp.int32, wide, 1) % items
    spread = jnp.where(column == lax.broadcasted_iota(jnp.int32, wide, 0), 1.0, 0.0)
    listed = dot_tn(listed, spread)
    totals = jnp.ones((items, LANES), jnp.float32)
    for first in range(0, group_size, step):
        q = stack(
            [ref[:, h * HD : (h + 1) * HD] for h in range(first, first + step) for ref in q_refs]
        )
        acc = jnp.zeros((HD, step * items), jnp.float32)
        total = jnp.zeros((1, step * items), jnp.float32)
        for n, (key, value) in enumerate(zip(keys, values)):
            p = jnp.exp2(dot_nt(key[...], q) * (SCALE * LOG2E))
            here = dot_tn(value[...], p.astype(jnp.bfloat16))
            hit = listed[n : n + 1] > 0.0
            acc = jnp.where(hit, acc + here, acc)
            total = jnp.where(hit, total + jnp.sum(p, axis=0, keepdims=True), total)
        out = (acc / jnp.where(total > 0.0, total, 1.0)).T
        total = jnp.broadcast_to(total, (8, step * items)).T
        for n in range(step):
            rows = slice(n * items, (n + 1) * items)
            write(first + n, out[rows])
            totals = jnp.where(lane == first_head + first + n, total[rows, :1], totals)
    good = (totals > LOW) & (totals < HIGH)
    bad = jnp.max(jnp.where(good | (some == 0.0), 0.0, 1.0))
    logs = jnp.where((some > 0.0) & good, jnp.log(jnp.where(good, totals, 1.0)), NONE)
    logs_ref[...] = jnp.where(mine, logs, logs_ref[...])

    @pl.when(bad > 0.0)
    def _():
        @pl.loop(0, group_size)
        def _(head):
            start = pl.multiple_of(head * HD, HD)
            q = stack([ref[:, pl.ds(start, HD)] for ref in q_refs])
            top = jnp.full((items, 1), NONE, jnp.float32)
            for n, (hit, key) in enumerate(zip(hits, keys)):
                s = dot_nt(q, key[...])
                s_ref[n] = s
                here = jnp.max(s, axis=1, keepdims=True)
                top = jnp.where(hit > 0.0, jnp.maximum(top, here), top)
            acc = jnp.zeros((items, HD), jnp.float32)
            total = jnp.zeros((items, 1), jnp.float32)
            for n, (hit, value) in enumerate(zip(hits, values)):
                p = jnp.exp2((s_ref[n] - top) * (SCALE * LOG2E))
                p = jnp.where(hit > 0.0, p, 0.0)
                total += jnp.sum(p, axis=1, keepdims=True)
                acc += jnp.dot(p.astype(jnp.bfloat16), value[...], preferred_element_type=jnp.float32)
            safe = jnp.where(some > 0.0, total, 1.0)
            write(head, jnp.where(some > 0.0, acc / safe, 0.0))
            log = jnp.where(some > 0.0, top * SCALE + jnp.log(safe), NONE)
            logs_ref[...] = jnp.where(lane == first_head + head, log, logs_ref[...])

    @pl.when(kv == pl.num_programs(1) - 1)
    def _():
        heads = (out_refs[0].shape[1] - LANES) // HD
        parts = jnp.concatenate([x[:, :heads] for x in split3(logs_ref[...])], axis=1)
        pad = jnp.zeros((items, LANES - 3 * heads), jnp.bfloat16)
        parts = jnp.concatenate([parts, pad], axis=1)
        for n, ref in enumerate(out_refs):
            ref[:, heads * HD :] = parts[n * kept : (n + 1) * kept]


def attend_blocks(where, place, caches, group_size, queries, outs, after):
    pieces = len(queries)
    rows, columns = queries[0].shape
    blocks, tokens, kv_width = caches[0].shape
    kv_half = kv_width // HD // 2
    share = min(rows, 64)
    items = share * pieces
    cache_block = pl.BlockSpec((blocks, tokens, HD), lambda i, g, w: (0, 0, w[2] * kv_half + g))
    queries_block = pl.BlockSpec((share, group_size * HD), lambda i, g, w: (i, g))
    ids_block = pl.BlockSpec((share, LANES), lambda i, g, w: (i, columns // LANES - 1))
    return pl.pallas_call(
        functools.partial(block_kernel, pieces, outs, group_size, min(group_size, max(1, ROWS_STEP // items))),
        grid_spec=pltpu.PrefetchScalarGridSpec(
            num_scalar_prefetch=1,
            grid=(rows // share, kv_half),
            in_specs=[pl.BlockSpec(place.shape, lambda i, g, w: (0, 0))]
            + [queries_block] * pieces
            + [ids_block] * pieces
            + [cache_block] * 4
            + [pl.BlockSpec(memory_space=pl.ANY)] * len(after),
            out_specs=[pl.BlockSpec((items // outs, columns), lambda i, g, w: (i, 0))] * outs,
            scratch_shapes=[
                pltpu.VMEM((items, LANES), jnp.float32),
                pltpu.VMEM((2 * blocks, items, tokens), jnp.float32),
            ],
        ),
        out_shape=[jax.ShapeDtypeStruct((rows * pieces // outs, columns), jnp.bfloat16)] * outs,
        compiler_params=params(),
        cost_estimate=pl.CostEstimate(
            flops=rows * pieces * tokens * columns,
            bytes_accessed=4 * rows * pieces * columns,
            transcendentals=rows * pieces * columns,
        ),
    )(where, place, *queries, *queries, *caches, *after)


def suffix_kernel(group_size, lengths_ref, q_ref, k_ref, v_ref, out_ref, log_ref):
    rows_here, steps, width = q_ref.shape
    tokens = k_ref.shape[1]
    kv_here = k_ref.shape[2] // HD
    items = rows_here * steps
    span = rows_here * tokens
    half = width // HD // 2
    lane = lax.broadcasted_iota(jnp.int32, (items, LANES), 1)
    token = lax.broadcasted_iota(jnp.int32, (items, span), 1)
    item = lax.broadcasted_iota(jnp.int32, (items, span), 0)
    seen = jnp.zeros((items, span), jnp.float32)
    for r in range(rows_here):
        offset = token - r * tokens
        inside = (item // steps == r) & (offset >= 0) & (offset < lengths_ref[r] + item % steps)
        seen = jnp.where(inside, 1.0, seen)
    seen = jnp.concatenate([seen] * group_size, axis=0)
    logs = [jnp.zeros((items, LANES), jnp.float32)] * 2
    for g in range(kv_here):
        columns = slice(g * group_size * HD, (g + 1) * group_size * HD)
        q_all = flat(q_ref[:, :, columns]).astype(jnp.bfloat16)
        q = stack([q_all[:, n * HD : (n + 1) * HD] for n in range(group_size)])
        keys = k_ref[:, :, g * HD : (g + 1) * HD].reshape(span, HD)
        values = v_ref[:, :, g * HD : (g + 1) * HD].reshape(span, HD)
        s = jnp.where(seen > 0.0, dot_nt(q, keys), NONE)
        highest = jnp.max(s, axis=1, keepdims=True)
        p = jnp.exp2((s - highest) * (SCALE * LOG2E))
        p = jnp.where(seen > 0.0, p, 0.0)
        total = jnp.sum(p, axis=1, keepdims=True)
        out = jnp.dot(p.astype(jnp.bfloat16), values, preferred_element_type=jnp.float32) / total
        log = highest * SCALE + jnp.log(total)
        for n in range(group_size):
            h = g * group_size + n
            out_ref[:, h * HD : (h + 1) * HD] = out[n * items : (n + 1) * items]
            side = h // half
            logs[side] = jnp.where(lane == h % half, log[n * items : (n + 1) * items], logs[side])
    for side in range(2):
        log_ref[side] = logs[side]


def attend_suffix(lengths, queries, suffix_k, suffix_v):
    rows, steps, width = queries.shape
    _, tokens, kv_width = suffix_k.shape
    items = rows * steps
    whole = lambda i, n: (0, 0, 0)
    return pl.pallas_call(
        functools.partial(suffix_kernel, width // kv_width),
        grid_spec=pltpu.PrefetchScalarGridSpec(
            num_scalar_prefetch=1,
            grid=(1,),
            in_specs=[pl.BlockSpec(x.shape, whole) for x in (queries, suffix_k, suffix_v)],
            out_specs=[
                pl.BlockSpec((items, width), lambda i, n: (0, 0)),
                pl.BlockSpec((2, items, LANES), whole),
            ],
        ),
        out_shape=(
            jax.ShapeDtypeStruct((items, width), jnp.float32),
            jax.ShapeDtypeStruct((2, items, LANES), jnp.float32),
        ),
        compiler_params=params(),
        cost_estimate=pl.CostEstimate(
            flops=16 * items * rows * tokens * width,
            bytes_accessed=4 * suffix_k.size + 6 * items * width,
            transcendentals=items * rows * tokens * width // HD,
        ),
    )(lengths, queries, suffix_k, suffix_v)


def weigh(parts, items, heads):
    columns = heads * HD
    logs = []
    for ref, start in parts:
        x = ref[start : start + items, columns:].astype(jnp.float32)
        logs.append(x[:, :heads] + x[:, heads : 2 * heads] + x[:, 2 * heads : 3 * heads])
    return logs


def shares(logs):
    top = logs[0]
    for log in logs[1:]:
        top = jnp.maximum(top, log)
    factors = [jnp.exp(log - top) for log in logs]
    total = factors[0]
    for factor in factors[1:]:
        total += factor
    inverse = 1.0 / total
    return [factor * inverse for factor in factors], top + jnp.log(total)


def finish_kernel(sides, *refs):
    out_s_ref, log_s_ref, out_ref = refs[-3:]
    rows, steps, width = out_ref.shape
    items = rows * steps
    columns = width // 2
    heads = columns // HD
    core = lax.axis_index("ctx") % 2
    taken = 0
    for count, which in zip(sides, (core, 1 - core)):
        back_refs = refs[taken : taken + count]
        taken += count
        parts = [(ref, start) for ref in back_refs for start in range(0, ref.shape[0], items)]
        factors, _ = shares([log_s_ref[which][:, :heads]] + weigh(parts, items, heads))
        for h in range(heads):
            here = slice(h * HD, (h + 1) * HD)
            span = pl.ds(pl.multiple_of(which * columns + h * HD, HD), HD)
            acc = factors[0][:, h : h + 1] * out_s_ref[:, span]
            for factor, (ref, start) in zip(factors[1:], parts):
                acc += factor[:, h : h + 1] * ref[start : start + items, here].astype(jnp.float32)
            for row in range(rows):
                out_ref[row, :, span] = acc[row * steps : (row + 1) * steps].astype(jnp.bfloat16)


def finish(sides, out_s, log_s, shape):
    return pl.pallas_call(
        functools.partial(finish_kernel, [len(side) for side in sides]),
        out_shape=jax.ShapeDtypeStruct(shape, jnp.bfloat16),
        compiler_params=params(SMALL),
    )(*sides[0], *sides[1], out_s, log_s)


def join_kernel(a_ref, b_ref, after_ref, out_ref):
    rows = a_ref.shape[0]
    out_ref[:rows] = a_ref[...]
    out_ref[rows:] = b_ref[...]


def join(a, b, after):
    whole = pl.BlockSpec(memory_space=pltpu.VMEM)
    return pl.pallas_call(
        join_kernel,
        in_specs=[whole, whole, ANY],
        out_shape=jax.ShapeDtypeStruct((2 * a.shape[0], a.shape[1]), a.dtype),
        compiler_params=params(),
    )(a, b, after)


def local(queries, selected, placement, lengths, cache_k, cache_v, suffix_k, suffix_v):
    rows_here, steps, width = queries.shape
    size = lax.axis_size("ctx")
    blocks_here, _, kv_width = cache_k.shape
    group_size = width // kv_width
    items = rows_here * steps
    chips = size // 2

    def swap(x, bits):
        return lax.ppermute(x, "ctx", [(i, i ^ bits) for i in range(size)]) if bits else x

    own = lax.axis_index("ctx")
    where = jnp.stack([own * blocks_here, (own ^ 1) * blocks_here, own & 1]).astype(jnp.int32)
    place = placement.reshape(1, -1)
    caches = [cache_k, cache_v, swap(cache_k, 1), swap(cache_v, 1)]
    packed = pack(queries, selected)
    out_s, log_s = attend_suffix(lengths, queries, suffix_k, suffix_v)
    chip = join(packed[0], swap(packed[1], 1), log_s)
    attend = functools.partial(attend_blocks, where, place, caches, group_size)
    if chips == 4:
        far, near = swap(chip, 4), swap(chip, 2)
        farthest = swap(far, 2)
        partial = attend([chip, near, far, farthest], size, [])
        back = {n: swap(partial[n], n) for n in (3, 4, 5, 6, 7, 2, 1, 0)}
        sides = [[back[n] for n in range(side, size, 2)] for side in range(2)]
    else:
        same = [[2 * z + core for z in range(chips)] for core in range(2)]
        every = lax.all_gather(chip, "ctx", axis=0, tiled=True, axis_index_groups=same)
        (partial,) = attend([every], 1, [])
        back = lax.all_to_all(
            partial, "ctx", split_axis=0, concat_axis=0, tiled=True, axis_index_groups=same
        ).reshape(chips, 2, items, -1)
        sides = [[swap(back[:, n].reshape(chips * items, -1), n)] for n in range(2)]
    return finish(sides, out_s, log_s, queries.shape)


def solution(mesh):
    rows = P(("groups", "ctx"), None, "rows")
    in_specs = (
        rows,
        P(("groups", "ctx"), None, None),
        P("groups"),
        P(("groups", "ctx")),
        rows,
        rows,
        rows,
        rows,
    )
    return jax.shard_map(local, mesh=mesh, in_specs=in_specs, out_specs=rows, check_vma=False)
```

```python
import functools
import math

import jax
import jax.numpy as jnp
from jax import lax
from jax.experimental import pallas as pl
from jax.experimental.pallas import tpu as pltpu
from jax.sharding import PartitionSpec as P

HD = 128
LANES = 128
SCALE = 1.0 / math.sqrt(HD)
LOG2E = math.log2(math.e)
NONE = -1e30
LOW, HIGH = 2.0**-80, 2.0**100
VMEM = 121 * 1024 * 1024 // 2
SMALL = 16 * 1024 * 1024
ROWS_STEP = 1024


def split3(x):
    high = x.astype(jnp.bfloat16)
    rest = x - high.astype(jnp.float32)
    middle = rest.astype(jnp.bfloat16)
    low = (rest - middle.astype(jnp.float32)).astype(jnp.bfloat16)
    return high, middle, low


def dot_nt(a, b):
    return lax.dot_general(a, b, (((1,), (1,)), ((), ())), preferred_element_type=jnp.float32)


def dot_tn(a, b):
    return lax.dot_general(a, b, (((0,), (0,)), ((), ())), preferred_element_type=jnp.float32)


def stack(arrays):
    return arrays[0] if len(arrays) == 1 else jnp.concatenate(arrays, axis=0)


def params(limit=VMEM):
    return pltpu.CompilerParams(vmem_limit_bytes=limit)


def flat(x):
    return x.astype(jnp.float32).reshape(x.shape[0] * x.shape[1], x.shape[2])


ANY = pl.BlockSpec(memory_space=pl.ANY)


def pack_kernel(q_ref, selected_ref, mine_ref, other_ref):
    half = q_ref.shape[2] // 2
    core = lax.axis_index("ctx") % 2
    ids = flat(selected_ref[...])
    pad = jnp.full((ids.shape[0], LANES - ids.shape[1]), -1.0, jnp.float32)
    ids = jnp.concatenate([ids, pad], axis=1).astype(jnp.bfloat16)
    for ref, which in ((mine_ref, core), (other_ref, 1 - core)):
        start = pl.multiple_of(which * half, LANES)
        ref[:, :half] = flat(q_ref[:, :, pl.ds(start, half)]).astype(jnp.bfloat16)
        ref[:, half:] = ids


def pack(queries, selected):
    rows, steps, width = queries.shape
    shape = jax.ShapeDtypeStruct((rows * steps, width // 2 + LANES), jnp.bfloat16)
    return pl.pallas_call(pack_kernel, out_shape=[shape, shape], compiler_params=params())(
        queries, selected
    )


def block_kernel(pieces, outs, group_size, step, where_ref, place_ref, *refs):
    q_refs = refs[:pieces]
    id_refs = refs[pieces : 2 * pieces]
    own_k, own_v, next_k, next_v = refs[2 * pieces : 2 * pieces + 4]
    out_refs = refs[-2 - outs : -2]
    logs_ref, s_ref = refs[-2:]
    kv = pl.program_id(1)
    share = q_refs[0].shape[0]
    items = share * pieces
    kept = items // outs
    blocks, tokens, _ = own_k.shape
    lane = lax.broadcasted_iota(jnp.int32, (items, LANES), 1)
    first_head = kv * group_size
    mine = (lane >= first_head) & (lane < first_head + group_size)
    ids = stack([ref[...].astype(jnp.float32) for ref in id_refs])
    place = place_ref[...]
    block_ids = lax.broadcasted_iota(jnp.int32, place.shape, 1)
    keys = [ref.at[b] for ref in (own_k, next_k) for b in range(blocks)]
    values = [ref.at[b] for ref in (own_v, next_v) for b in range(blocks)]
    hits = []
    for base in (where_ref[0], where_ref[1]):
        for b in range(blocks):
            target = jnp.sum(
                jnp.where(place == base + b, block_ids, 0).astype(jnp.float32), axis=1, keepdims=True
            )
            hits.append(jnp.max(jnp.where(ids == target, 1.0, 0.0), axis=1, keepdims=True))
    some = hits[0]
    for hit in hits[1:]:
        some = jnp.maximum(some, hit)

    def write(head, out):
        start = pl.multiple_of((first_head + head) * HD, HD)
        out = out.astype(jnp.bfloat16)
        for n, ref in enumerate(out_refs):
            ref[:, pl.ds(start, HD)] = out[n * kept : (n + 1) * kept]

    listed = jnp.zeros((items, LANES), jnp.float32)
    for n, hit in enumerate(hits):
        listed = jnp.where(lane == n, hit, listed)
    wide = (items, step * items)
    column = lax.broadcasted_iota(jnp.int32, wide, 1) % items
    spread = jnp.where(column == lax.broadcasted_iota(jnp.int32, wide, 0), 1.0, 0.0)
    listed = dot_tn(listed, spread)
    totals = jnp.ones((items, LANES), jnp.float32)
    for first in range(0, group_size, step):
        q = stack(
            [ref[:, h * HD : (h + 1) * HD] for h in range(first, first + step) for ref in q_refs]
        )
        acc = jnp.zeros((HD, step * items), jnp.float32)
        total = jnp.zeros((1, step * items), jnp.float32)
        for n, (key, value) in enumerate(zip(keys, values)):
            p = jnp.exp2(dot_nt(key[...], q) * (SCALE * LOG2E))
            here = dot_tn(value[...], p.astype(jnp.bfloat16))
            hit = listed[n : n + 1] > 0.0
            acc = jnp.where(hit, acc + here, acc)
            total = jnp.where(hit, total + jnp.sum(p, axis=0, keepdims=True), total)
        out = (acc / jnp.where(total > 0.0, total, 1.0)).T
        total = jnp.broadcast_to(total, (8, step * items)).T
        for n in range(step):
            rows = slice(n * items, (n + 1) * items)
            write(first + n, out[rows])
            totals = jnp.where(lane == first_head + first + n, total[rows, :1], totals)
    good = (totals > LOW) & (totals < HIGH)
    bad = jnp.max(jnp.where(good | (some == 0.0), 0.0, 1.0))
    logs = jnp.where((some > 0.0) & good, jnp.log(jnp.where(good, totals, 1.0)), NONE)
    logs_ref[...] = jnp.where(mine, logs, logs_ref[...])

    @pl.when(bad > 0.0)
    def _():
        @pl.loop(0, group_size)
        def _(head):
            start = pl.multiple_of(head * HD, HD)
            q = stack([ref[:, pl.ds(start, HD)] for ref in q_refs])
            top = jnp.full((items, 1), NONE, jnp.float32)
            for n, (hit, key) in enumerate(zip(hits, keys)):
                s = dot_nt(q, key[...])
                s_ref[n] = s
                here = jnp.max(s, axis=1, keepdims=True)
                top = jnp.where(hit > 0.0, jnp.maximum(top, here), top)
            acc = jnp.zeros((items, HD), jnp.float32)
            total = jnp.zeros((items, 1), jnp.float32)
            for n, (hit, value) in enumerate(zip(hits, values)):
                p = jnp.exp2((s_ref[n] - top) * (SCALE * LOG2E))
                p = jnp.where(hit > 0.0, p, 0.0)
                total += jnp.sum(p, axis=1, keepdims=True)
                acc += jnp.dot(p.astype(jnp.bfloat16), value[...], preferred_element_type=jnp.float32)
            safe = jnp.where(some > 0.0, total, 1.0)
            write(head, jnp.where(some > 0.0, acc / safe, 0.0))
            log = jnp.where(some > 0.0, top * SCALE + jnp.log(safe), NONE)
            logs_ref[...] = jnp.where(lane == first_head + head, log, logs_ref[...])

    @pl.when(kv == pl.num_programs(1) - 1)
    def _():
        heads = (out_refs[0].shape[1] - LANES) // HD
        parts = jnp.concatenate([x[:, :heads] for x in split3(logs_ref[...])], axis=1)
        pad = jnp.zeros((items, LANES - 3 * heads), jnp.bfloat16)
        parts = jnp.concatenate([parts, pad], axis=1)
        for n, ref in enumerate(out_refs):
            ref[:, heads * HD :] = parts[n * kept : (n + 1) * kept]


def attend_blocks(where, place, caches, group_size, queries, outs, after):
    pieces = len(queries)
    rows, columns = queries[0].shape
    blocks, tokens, kv_width = caches[0].shape
    kv_half = kv_width // HD // 2
    share = min(rows, 64)
    items = share * pieces
    cache_block = pl.BlockSpec((blocks, tokens, HD), lambda i, g, w: (0, 0, w[2] * kv_half + g))
    queries_block = pl.BlockSpec((share, group_size * HD), lambda i, g, w: (i, g))
    ids_block = pl.BlockSpec((share, LANES), lambda i, g, w: (i, columns // LANES - 1))
    return pl.pallas_call(
        functools.partial(block_kernel, pieces, outs, group_size, min(group_size, max(1, ROWS_STEP // items))),
        grid_spec=pltpu.PrefetchScalarGridSpec(
            num_scalar_prefetch=1,
            grid=(rows // share, kv_half),
            in_specs=[pl.BlockSpec(place.shape, lambda i, g, w: (0, 0))]
            + [queries_block] * pieces
            + [ids_block] * pieces
            + [cache_block] * 4
            + [pl.BlockSpec(memory_space=pl.ANY)] * len(after),
            out_specs=[pl.BlockSpec((items // outs, columns), lambda i, g, w: (i, 0))] * outs,
            scratch_shapes=[
                pltpu.VMEM((items, LANES), jnp.float32),
                pltpu.VMEM((2 * blocks, items, tokens), jnp.float32),
            ],
        ),
        out_shape=[jax.ShapeDtypeStruct((rows * pieces // outs, columns), jnp.bfloat16)] * outs,
        compiler_params=params(),
        cost_estimate=pl.CostEstimate(
            flops=rows * pieces * tokens * columns,
            bytes_accessed=4 * rows * pieces * columns,
            transcendentals=rows * pieces * columns,
        ),
    )(where, place, *queries, *queries, *caches, *after)


def suffix_kernel(group_size, lengths_ref, q_ref, k_ref, v_ref, out_ref, log_ref):
    rows_here, steps, width = q_ref.shape
    tokens = k_ref.shape[1]
    kv_here = k_ref.shape[2] // HD
    items = rows_here * steps
    span = rows_here * tokens
    half = width // HD // 2
    lane = lax.broadcasted_iota(jnp.int32, (items, LANES), 1)
    token = lax.broadcasted_iota(jnp.int32, (items, span), 1)
    item = lax.broadcasted_iota(jnp.int32, (items, span), 0)
    seen = jnp.zeros((items, span), jnp.float32)
    for r in range(rows_here):
        offset = token - r * tokens
        inside = (item // steps == r) & (offset >= 0) & (offset < lengths_ref[r] + item % steps)
        seen = jnp.where(inside, 1.0, seen)
    seen = jnp.concatenate([seen] * group_size, axis=0)
    logs = [jnp.zeros((items, LANES), jnp.float32)] * 2
    for g in range(kv_here):
        columns = slice(g * group_size * HD, (g + 1) * group_size * HD)
        q_all = flat(q_ref[:, :, columns]).astype(jnp.bfloat16)
        q = stack([q_all[:, n * HD : (n + 1) * HD] for n in range(group_size)])
        keys = k_ref[:, :, g * HD : (g + 1) * HD].reshape(span, HD)
        values = v_ref[:, :, g * HD : (g + 1) * HD].reshape(span, HD)
        s = jnp.where(seen > 0.0, dot_nt(q, keys), NONE)
        highest = jnp.max(s, axis=1, keepdims=True)
        p = jnp.exp2((s - highest) * (SCALE * LOG2E))
        p = jnp.where(seen > 0.0, p, 0.0)
        total = jnp.sum(p, axis=1, keepdims=True)
        out = jnp.dot(p.astype(jnp.bfloat16), values, preferred_element_type=jnp.float32) / total
        log = highest * SCALE + jnp.log(total)
        for n in range(group_size):
            h = g * group_size + n
            out_ref[:, h * HD : (h + 1) * HD] = out[n * items : (n + 1) * items]
            side = h // half
            logs[side] = jnp.where(lane == h % half, log[n * items : (n + 1) * items], logs[side])
    for side in range(2):
        log_ref[side] = logs[side]


def attend_suffix(lengths, queries, suffix_k, suffix_v):
    rows, steps, width = queries.shape
    _, tokens, kv_width = suffix_k.shape
    items = rows * steps
    whole = lambda i, n: (0, 0, 0)
    return pl.pallas_call(
        functools.partial(suffix_kernel, width // kv_width),
        grid_spec=pltpu.PrefetchScalarGridSpec(
            num_scalar_prefetch=1,
            grid=(1,),
            in_specs=[pl.BlockSpec(x.shape, whole) for x in (queries, suffix_k, suffix_v)],
            out_specs=[
                pl.BlockSpec((items, width), lambda i, n: (0, 0)),
                pl.BlockSpec((2, items, LANES), whole),
            ],
        ),
        out_shape=(
            jax.ShapeDtypeStruct((items, width), jnp.float32),
            jax.ShapeDtypeStruct((2, items, LANES), jnp.float32),
        ),
        compiler_params=params(),
        cost_estimate=pl.CostEstimate(
            flops=16 * items * rows * tokens * width,
            bytes_accessed=4 * suffix_k.size + 6 * items * width,
            transcendentals=items * rows * tokens * width // HD,
        ),
    )(lengths, queries, suffix_k, suffix_v)


def weigh(parts, items, heads):
    columns = heads * HD
    logs = []
    for ref, start in parts:
        x = ref[start : start + items, columns:].astype(jnp.float32)
        logs.append(x[:, :heads] + x[:, heads : 2 * heads] + x[:, 2 * heads : 3 * heads])
    return logs


def shares(logs):
    top = logs[0]
    for log in logs[1:]:
        top = jnp.maximum(top, log)
    factors = [jnp.exp(log - top) for log in logs]
    total = factors[0]
    for factor in factors[1:]:
        total += factor
    inverse = 1.0 / total
    return [factor * inverse for factor in factors], top + jnp.log(total)


def finish_kernel(sides, *refs):
    out_s_ref, log_s_ref, out_ref = refs[-3:]
    rows, steps, width = out_ref.shape
    items = rows * steps
    columns = width // 2
    heads = columns // HD
    core = lax.axis_index("ctx") % 2
    taken = 0
    for count, which in zip(sides, (core, 1 - core)):
        back_refs = refs[taken : taken + count]
        taken += count
        parts = [(ref, start) for ref in back_refs for start in range(0, ref.shape[0], items)]
        factors, _ = shares([log_s_ref[which][:, :heads]] + weigh(parts, items, heads))
        for h in range(heads):
            here = slice(h * HD, (h + 1) * HD)
            span = pl.ds(pl.multiple_of(which * columns + h * HD, HD), HD)
            acc = factors[0][:, h : h + 1] * out_s_ref[:, span]
            for factor, (ref, start) in zip(factors[1:], parts):
                acc += factor[:, h : h + 1] * ref[start : start + items, here].astype(jnp.float32)
            for row in range(rows):
                out_ref[row, :, span] = acc[row * steps : (row + 1) * steps].astype(jnp.bfloat16)


def finish(sides, out_s, log_s, shape):
    return pl.pallas_call(
        functools.partial(finish_kernel, [len(side) for side in sides]),
        out_shape=jax.ShapeDtypeStruct(shape, jnp.bfloat16),
        compiler_params=params(SMALL),
    )(*sides[0], *sides[1], out_s, log_s)


def local(queries, selected, placement, lengths, cache_k, cache_v, suffix_k, suffix_v):
    rows_here, steps, width = queries.shape
    size = lax.axis_size("ctx")
    blocks_here, _, kv_width = cache_k.shape
    group_size = width // kv_width
    items = rows_here * steps
    chips = size // 2

    def swap(x, bits):
        return lax.ppermute(x, "ctx", [(i, i ^ bits) for i in range(size)]) if bits else x

    own = lax.axis_index("ctx")
    where = jnp.stack([own * blocks_here, (own ^ 1) * blocks_here, own & 1]).astype(jnp.int32)
    place = placement.reshape(1, -1)
    caches = [cache_k, cache_v, swap(cache_k, 1), swap(cache_v, 1)]
    packed = pack(queries, selected)
    out_s, log_s = attend_suffix(lengths, queries, suffix_k, suffix_v)
    attend = functools.partial(attend_blocks, where, place, caches, group_size)
    if chips == 4:
        arrived = {n: swap(packed[n % 2], n) for n in (4, 5, 2, 3, 0, 1)}
        arrived.update({n: swap(arrived[n - 2], 2) for n in (6, 7)})
        partial = attend([arrived[n] for n in range(size)], size, [log_s])
        back = {n: swap(partial[n], n) for n in (3, 4, 5, 6, 7, 2, 1, 0)}
        sides = [[back[n] for n in range(side, size, 2)] for side in range(2)]
    else:
        same = [[2 * z + core for z in range(chips)] for core in range(2)]
        chip = jnp.concatenate([packed[0], swap(packed[1], 1)], axis=0)
        every = lax.all_gather(chip, "ctx", axis=0, tiled=True, axis_index_groups=same)
        (partial,) = attend([every], 1, [log_s])
        back = lax.all_to_all(
            partial, "ctx", split_axis=0, concat_axis=0, tiled=True, axis_index_groups=same
        ).reshape(chips, 2, items, -1)
        sides = [[swap(back[:, n].reshape(chips * items, -1), n)] for n in range(2)]
    return finish(sides, out_s, log_s, queries.shape)


def solution(mesh):
    rows = P(("groups", "ctx"), None, "rows")
    in_specs = (
        rows,
        P(("groups", "ctx"), None, None),
        P("groups"),
        P(("groups", "ctx")),
        rows,
        rows,
        rows,
        rows,
    )
    return jax.shard_map(local, mesh=mesh, in_specs=in_specs, out_specs=rows, check_vma=False)
```

```python
import functools
import math

import jax
import jax.numpy as jnp
from jax import lax
from jax.experimental import pallas as pl
from jax.experimental.pallas import tpu as pltpu
from jax.sharding import PartitionSpec as P

HD = 128
LANES = 128
SCALE = 1.0 / math.sqrt(HD)
LOG2E = math.log2(math.e)
NONE = -1e30
LOW, HIGH = 2.0**-80, 2.0**100
VMEM = 121 * 1024 * 1024 // 2
SMALL = 16 * 1024 * 1024
ROWS_STEP = 1024


def split3(x):
    high = x.astype(jnp.bfloat16)
    rest = x - high.astype(jnp.float32)
    middle = rest.astype(jnp.bfloat16)
    low = (rest - middle.astype(jnp.float32)).astype(jnp.bfloat16)
    return high, middle, low


def dot_nt(a, b):
    return lax.dot_general(a, b, (((1,), (1,)), ((), ())), preferred_element_type=jnp.float32)


def dot_tn(a, b):
    return lax.dot_general(a, b, (((0,), (0,)), ((), ())), preferred_element_type=jnp.float32)


def stack(arrays):
    return arrays[0] if len(arrays) == 1 else jnp.concatenate(arrays, axis=0)


def params(limit=VMEM):
    return pltpu.CompilerParams(vmem_limit_bytes=limit)


def flat(x):
    return x.astype(jnp.float32).reshape(x.shape[0] * x.shape[1], x.shape[2])


ANY = pl.BlockSpec(memory_space=pl.ANY)


def pack_kernel(q_ref, selected_ref, mine_ref, other_ref):
    half = q_ref.shape[2] // 2
    core = lax.axis_index("ctx") % 2
    ids = flat(selected_ref[...])
    pad = jnp.full((ids.shape[0], LANES - ids.shape[1]), -1.0, jnp.float32)
    ids = jnp.concatenate([ids, pad], axis=1).astype(jnp.bfloat16)
    for ref, which in ((mine_ref, core), (other_ref, 1 - core)):
        start = pl.multiple_of(which * half, LANES)
        ref[:, :half] = flat(q_ref[:, :, pl.ds(start, half)]).astype(jnp.bfloat16)
        ref[:, half:] = ids


def pack(queries, selected):
    rows, steps, width = queries.shape
    shape = jax.ShapeDtypeStruct((rows * steps, width // 2 + LANES), jnp.bfloat16)
    return pl.pallas_call(pack_kernel, out_shape=[shape, shape], compiler_params=params())(
        queries, selected
    )


def block_kernel(pieces, outs, group_size, step, where_ref, place_ref, *refs):
    q_refs = refs[:pieces]
    id_refs = refs[pieces : 2 * pieces]
    own_k, own_v, next_k, next_v = refs[2 * pieces : 2 * pieces + 4]
    out_refs = refs[-2 - outs : -2]
    logs_ref, s_ref = refs[-2:]
    kv = pl.program_id(1)
    share = q_refs[0].shape[0]
    items = share * pieces
    kept = items // outs
    blocks, tokens, _ = own_k.shape
    lane = lax.broadcasted_iota(jnp.int32, (items, LANES), 1)
    first_head = kv * group_size
    mine = (lane >= first_head) & (lane < first_head + group_size)
    ids = stack([ref[...].astype(jnp.float32) for ref in id_refs])
    place = place_ref[...]
    block_ids = lax.broadcasted_iota(jnp.int32, place.shape, 1)
    keys = [ref.at[b] for ref in (own_k, next_k) for b in range(blocks)]
    values = [ref.at[b] for ref in (own_v, next_v) for b in range(blocks)]
    hits = []
    for base in (where_ref[0], where_ref[1]):
        for b in range(blocks):
            target = jnp.sum(
                jnp.where(place == base + b, block_ids, 0).astype(jnp.float32), axis=1, keepdims=True
            )
            hits.append(jnp.max(jnp.where(ids == target, 1.0, 0.0), axis=1, keepdims=True))
    some = hits[0]
    for hit in hits[1:]:
        some = jnp.maximum(some, hit)

    def write(head, out):
        start = pl.multiple_of((first_head + head) * HD, HD)
        out = out.astype(jnp.bfloat16)
        for n, ref in enumerate(out_refs):
            ref[:, pl.ds(start, HD)] = out[n * kept : (n + 1) * kept]

    listed = jnp.zeros((items, LANES), jnp.float32)
    for n, hit in enumerate(hits):
        listed = jnp.where(lane == n, hit, listed)
    wide = (items, step * items)
    column = lax.broadcasted_iota(jnp.int32, wide, 1) % items
    spread = jnp.where(column == lax.broadcasted_iota(jnp.int32, wide, 0), 1.0, 0.0)
    listed = dot_tn(listed, spread)
    totals = jnp.ones((items, LANES), jnp.float32)
    for first in range(0, group_size, step):
        q = stack(
            [ref[:, h * HD : (h + 1) * HD] for h in range(first, first + step) for ref in q_refs]
        )
        acc = jnp.zeros((HD, step * items), jnp.float32)
        total = jnp.zeros((1, step * items), jnp.float32)
        for n, (key, value) in enumerate(zip(keys, values)):
            p = jnp.exp2(dot_nt(key[...], q) * (SCALE * LOG2E))
            here = dot_tn(value[...], p.astype(jnp.bfloat16))
            hit = listed[n : n + 1] > 0.0
            acc = jnp.where(hit, acc + here, acc)
            total = jnp.where(hit, total + jnp.sum(p, axis=0, keepdims=True), total)
        out = (acc / jnp.where(total > 0.0, total, 1.0)).T
        total = jnp.broadcast_to(total, (8, step * items)).T
        for n in range(step):
            rows = slice(n * items, (n + 1) * items)
            write(first + n, out[rows])
            totals = jnp.where(lane == first_head + first + n, total[rows, :1], totals)
    good = (totals > LOW) & (totals < HIGH)
    bad = jnp.max(jnp.where(good | (some == 0.0), 0.0, 1.0))
    logs = jnp.where((some > 0.0) & good, jnp.log(jnp.where(good, totals, 1.0)), NONE)
    logs_ref[...] = jnp.where(mine, logs, logs_ref[...])

    @pl.when(bad > 0.0)
    def _():
        @pl.loop(0, group_size)
        def _(head):
            start = pl.multiple_of(head * HD, HD)
            q = stack([ref[:, pl.ds(start, HD)] for ref in q_refs])
            top = jnp.full((items, 1), NONE, jnp.float32)
            for n, (hit, key) in enumerate(zip(hits, keys)):
                s = dot_nt(q, key[...])
                s_ref[n] = s
                here = jnp.max(s, axis=1, keepdims=True)
                top = jnp.where(hit > 0.0, jnp.maximum(top, here), top)
            acc = jnp.zeros((items, HD), jnp.float32)
            total = jnp.zeros((items, 1), jnp.float32)
            for n, (hit, value) in enumerate(zip(hits, values)):
                p = jnp.exp2((s_ref[n] - top) * (SCALE * LOG2E))
                p = jnp.where(hit > 0.0, p, 0.0)
                total += jnp.sum(p, axis=1, keepdims=True)
                acc += jnp.dot(p.astype(jnp.bfloat16), value[...], preferred_element_type=jnp.float32)
            safe = jnp.where(some > 0.0, total, 1.0)
            write(head, jnp.where(some > 0.0, acc / safe, 0.0))
            log = jnp.where(some > 0.0, top * SCALE + jnp.log(safe), NONE)
            logs_ref[...] = jnp.where(lane == first_head + head, log, logs_ref[...])

    @pl.when(kv == pl.num_programs(1) - 1)
    def _():
        heads = (out_refs[0].shape[1] - LANES) // HD
        parts = jnp.concatenate([x[:, :heads] for x in split3(logs_ref[...])], axis=1)
        pad = jnp.zeros((items, LANES - 3 * heads), jnp.bfloat16)
        parts = jnp.concatenate([parts, pad], axis=1)
        for n, ref in enumerate(out_refs):
            ref[:, heads * HD :] = parts[n * kept : (n + 1) * kept]


def attend_blocks(where, place, caches, group_size, queries, outs, after):
    pieces = len(queries)
    rows, columns = queries[0].shape
    blocks, tokens, kv_width = caches[0].shape
    kv_half = kv_width // HD // 2
    share = min(rows, 64)
    items = share * pieces
    cache_block = pl.BlockSpec((blocks, tokens, HD), lambda i, g, w: (0, 0, w[2] * kv_half + g))
    queries_block = pl.BlockSpec((share, group_size * HD), lambda i, g, w: (i, g))
    ids_block = pl.BlockSpec((share, LANES), lambda i, g, w: (i, columns // LANES - 1))
    return pl.pallas_call(
        functools.partial(block_kernel, pieces, outs, group_size, min(group_size, max(1, ROWS_STEP // items))),
        grid_spec=pltpu.PrefetchScalarGridSpec(
            num_scalar_prefetch=1,
            grid=(rows // share, kv_half),
            in_specs=[pl.BlockSpec(place.shape, lambda i, g, w: (0, 0))]
            + [queries_block] * pieces
            + [ids_block] * pieces
            + [cache_block] * 4
            + [pl.BlockSpec(memory_space=pl.ANY)] * len(after),
            out_specs=[pl.BlockSpec((items // outs, columns), lambda i, g, w: (i, 0))] * outs,
            scratch_shapes=[
                pltpu.VMEM((items, LANES), jnp.float32),
                pltpu.VMEM((2 * blocks, items, tokens), jnp.float32),
            ],
        ),
        out_shape=[jax.ShapeDtypeStruct((rows * pieces // outs, columns), jnp.bfloat16)] * outs,
        compiler_params=params(),
        cost_estimate=pl.CostEstimate(
            flops=rows * pieces * tokens * columns,
            bytes_accessed=4 * rows * pieces * columns,
            transcendentals=rows * pieces * columns,
        ),
    )(where, place, *queries, *queries, *caches, *after)


def suffix_kernel(group_size, lengths_ref, q_ref, k_ref, v_ref, pass_ref, where_ref, out_ref, log_ref, passed_ref):
    passed_ref[...] = pass_ref[...]
    rows_here, steps, width = q_ref.shape
    tokens = k_ref.shape[1]
    kv_here = k_ref.shape[2] // HD
    items = rows_here * steps
    span = rows_here * tokens
    half = width // HD // 2
    lane = lax.broadcasted_iota(jnp.int32, (items, LANES), 1)
    token = lax.broadcasted_iota(jnp.int32, (items, span), 1)
    item = lax.broadcasted_iota(jnp.int32, (items, span), 0)
    seen = jnp.zeros((items, span), jnp.float32)
    for r in range(rows_here):
        offset = token - r * tokens
        inside = (item // steps == r) & (offset >= 0) & (offset < lengths_ref[r] + item % steps)
        seen = jnp.where(inside, 1.0, seen)
    seen = jnp.concatenate([seen] * group_size, axis=0)
    logs = [jnp.zeros((items, LANES), jnp.float32)] * 2
    for g in range(kv_here):
        columns = slice(g * group_size * HD, (g + 1) * group_size * HD)
        q_all = flat(q_ref[:, :, columns]).astype(jnp.bfloat16)
        q = stack([q_all[:, n * HD : (n + 1) * HD] for n in range(group_size)])
        keys = k_ref[:, :, g * HD : (g + 1) * HD].reshape(span, HD)
        values = v_ref[:, :, g * HD : (g + 1) * HD].reshape(span, HD)
        s = jnp.where(seen > 0.0, dot_nt(q, keys), NONE)
        highest = jnp.max(s, axis=1, keepdims=True)
        p = jnp.exp2((s - highest) * (SCALE * LOG2E))
        p = jnp.where(seen > 0.0, p, 0.0)
        total = jnp.sum(p, axis=1, keepdims=True)
        out = jnp.dot(p.astype(jnp.bfloat16), values, preferred_element_type=jnp.float32) / total
        log = highest * SCALE + jnp.log(total)
        for n in range(group_size):
            h = g * group_size + n
            out_ref[:, h * HD : (h + 1) * HD] = out[n * items : (n + 1) * items]
            side = h // half
            logs[side] = jnp.where(lane == h % half, log[n * items : (n + 1) * items], logs[side])
    for side in range(2):
        log_ref[side] = logs[side]


def attend_suffix(lengths, queries, suffix_k, suffix_v, passing, where):
    rows, steps, width = queries.shape
    _, tokens, kv_width = suffix_k.shape
    items = rows * steps
    whole = lambda i, n: (0, 0, 0)
    return pl.pallas_call(
        functools.partial(suffix_kernel, width // kv_width),
        grid_spec=pltpu.PrefetchScalarGridSpec(
            num_scalar_prefetch=1,
            grid=(1,),
            in_specs=[pl.BlockSpec(x.shape, whole) for x in (queries, suffix_k, suffix_v)]
            + [pl.BlockSpec(passing.shape, lambda i, n: (0, 0)), ANY],
            out_specs=[
                pl.BlockSpec((items, width), lambda i, n: (0, 0)),
                pl.BlockSpec((2, items, LANES), whole),
                pl.BlockSpec(passing.shape, lambda i, n: (0, 0)),
            ],
        ),
        out_shape=(
            jax.ShapeDtypeStruct((items, width), jnp.float32),
            jax.ShapeDtypeStruct((2, items, LANES), jnp.float32),
            jax.ShapeDtypeStruct(passing.shape, passing.dtype),
        ),
        compiler_params=params(),
        cost_estimate=pl.CostEstimate(
            flops=16 * items * rows * tokens * width,
            bytes_accessed=4 * suffix_k.size + 6 * items * width,
            transcendentals=items * rows * tokens * width // HD,
        ),
    )(lengths, queries, suffix_k, suffix_v, passing, where)


def weigh(parts, items, heads):
    columns = heads * HD
    logs = []
    for ref, start in parts:
        x = ref[start : start + items, columns:].astype(jnp.float32)
        logs.append(x[:, :heads] + x[:, heads : 2 * heads] + x[:, 2 * heads : 3 * heads])
    return logs


def shares(logs):
    top = logs[0]
    for log in logs[1:]:
        top = jnp.maximum(top, log)
    factors = [jnp.exp(log - top) for log in logs]
    total = factors[0]
    for factor in factors[1:]:
        total += factor
    inverse = 1.0 / total
    return [factor * inverse for factor in factors], top + jnp.log(total)


def finish_kernel(sides, *refs):
    out_s_ref, log_s_ref, out_ref = refs[-3:]
    rows, steps, width = out_ref.shape
    items = rows * steps
    columns = width // 2
    heads = columns // HD
    core = lax.axis_index("ctx") % 2
    taken = 0
    for count, which in zip(sides, (core, 1 - core)):
        back_refs = refs[taken : taken + count]
        taken += count
        parts = [(ref, start) for ref in back_refs for start in range(0, ref.shape[0], items)]
        factors, _ = shares([log_s_ref[which][:, :heads]] + weigh(parts, items, heads))
        for h in range(heads):
            here = slice(h * HD, (h + 1) * HD)
            span = pl.ds(pl.multiple_of(which * columns + h * HD, HD), HD)
            acc = factors[0][:, h : h + 1] * out_s_ref[:, span]
            for factor, (ref, start) in zip(factors[1:], parts):
                acc += factor[:, h : h + 1] * ref[start : start + items, here].astype(jnp.float32)
            for row in range(rows):
                out_ref[row, :, span] = acc[row * steps : (row + 1) * steps].astype(jnp.bfloat16)


def finish(sides, out_s, log_s, shape):
    return pl.pallas_call(
        functools.partial(finish_kernel, [len(side) for side in sides]),
        out_shape=jax.ShapeDtypeStruct(shape, jnp.bfloat16),
        compiler_params=params(SMALL),
    )(*sides[0], *sides[1], out_s, log_s)


def local(queries, selected, placement, lengths, cache_k, cache_v, suffix_k, suffix_v):
    rows_here, steps, width = queries.shape
    size = lax.axis_size("ctx")
    blocks_here, _, kv_width = cache_k.shape
    group_size = width // kv_width
    items = rows_here * steps
    chips = size // 2

    def swap(x, bits):
        return lax.ppermute(x, "ctx", [(i, i ^ bits) for i in range(size)]) if bits else x

    own = lax.axis_index("ctx")
    where = jnp.stack([own * blocks_here, (own ^ 1) * blocks_here, own & 1]).astype(jnp.int32)
    place = placement.reshape(1, -1)
    caches = [cache_k, cache_v, swap(cache_k, 1), swap(cache_v, 1)]
    packed = pack(queries, selected)
    out_s, log_s, passed = attend_suffix(
        lengths, queries, suffix_k, suffix_v, packed[1], where
    )
    attend = functools.partial(attend_blocks, where, place, caches, group_size)
    if chips == 4:
        arrived = {n: swap(packed[n % 2], n) for n in (4, 5, 2, 0)}
        arrived.update({n: swap(passed, n) for n in (3, 1)})
        arrived.update({n: swap(arrived[n - 2], 2) for n in (6, 7)})
        partial = attend([arrived[n] for n in range(size)], size, [log_s])
        back = {n: swap(partial[n], n) for n in (1, 3, 4, 5, 6, 7, 2, 0)}
        sides = [[back[n] for n in range(side, size, 2)] for side in range(2)]
    else:
        same = [[2 * z + core for z in range(chips)] for core in range(2)]
        chip = jnp.concatenate([packed[0], swap(passed, 1)], axis=0)
        every = lax.all_gather(chip, "ctx", axis=0, tiled=True, axis_index_groups=same)
        (partial,) = attend([every], 1, [log_s])
        back = lax.all_to_all(
            partial, "ctx", split_axis=0, concat_axis=0, tiled=True, axis_index_groups=same
        ).reshape(chips, 2, items, -1)
        sides = [[swap(back[:, n].reshape(chips * items, -1), n)] for n in range(2)]
    return finish(sides, out_s, log_s, queries.shape)


def solution(mesh):
    rows = P(("groups", "ctx"), None, "rows")
    in_specs = (
        rows,
        P(("groups", "ctx"), None, None),
        P("groups"),
        P(("groups", "ctx")),
        rows,
        rows,
        rows,
        rows,
    )
    return jax.shard_map(local, mesh=mesh, in_specs=in_specs, out_specs=rows, check_vma=False)
```

```python
import functools
import math

import jax
import jax.numpy as jnp
from jax import lax
from jax.experimental import pallas as pl
from jax.experimental.pallas import tpu as pltpu
from jax.sharding import PartitionSpec as P

HD = 128
LANES = 128
SCALE = 1.0 / math.sqrt(HD)
LOG2E = math.log2(math.e)
NONE = -1e30
LOW, HIGH = 2.0**-80, 2.0**100
VMEM = 121 * 1024 * 1024 // 2
SMALL = 16 * 1024 * 1024
ROWS_STEP = 1024


def split3(x):
    high = x.astype(jnp.bfloat16)
    rest = x - high.astype(jnp.float32)
    middle = rest.astype(jnp.bfloat16)
    low = (rest - middle.astype(jnp.float32)).astype(jnp.bfloat16)
    return high, middle, low


def dot_nt(a, b):
    return lax.dot_general(a, b, (((1,), (1,)), ((), ())), preferred_element_type=jnp.float32)


def dot_tn(a, b):
    return lax.dot_general(a, b, (((0,), (0,)), ((), ())), preferred_element_type=jnp.float32)


def stack(arrays):
    return arrays[0] if len(arrays) == 1 else jnp.concatenate(arrays, axis=0)


def params(limit=VMEM):
    return pltpu.CompilerParams(vmem_limit_bytes=limit)


def flat(x):
    return x.astype(jnp.float32).reshape(x.shape[0] * x.shape[1], x.shape[2])


ANY = pl.BlockSpec(memory_space=pl.ANY)


def pack_kernel(q_ref, selected_ref, mine_ref, other_ref):
    half = q_ref.shape[2] // 2
    core = lax.axis_index("ctx") % 2
    ids = flat(selected_ref[...])
    pad = jnp.full((ids.shape[0], LANES - ids.shape[1]), -1.0, jnp.float32)
    ids = jnp.concatenate([ids, pad], axis=1).astype(jnp.bfloat16)
    for ref, which in ((mine_ref, core), (other_ref, 1 - core)):
        start = pl.multiple_of(which * half, LANES)
        ref[:, :half] = flat(q_ref[:, :, pl.ds(start, half)]).astype(jnp.bfloat16)
        ref[:, half:] = ids


def pack(queries, selected):
    rows, steps, width = queries.shape
    shape = jax.ShapeDtypeStruct((rows * steps, width // 2 + LANES), jnp.bfloat16)
    return pl.pallas_call(pack_kernel, out_shape=[shape, shape], compiler_params=params())(
        queries, selected
    )


def block_kernel(pieces, outs, group_size, step, where_ref, place_ref, *refs):
    q_refs = refs[:pieces]
    id_refs = refs[pieces : 2 * pieces]
    own_k, own_v, next_k, next_v = refs[2 * pieces : 2 * pieces + 4]
    out_refs = refs[-2 - outs : -2]
    logs_ref, s_ref = refs[-2:]
    kv = pl.program_id(1)
    share = q_refs[0].shape[0]
    items = share * pieces
    kept = items // outs
    blocks, tokens, _ = own_k.shape
    lane = lax.broadcasted_iota(jnp.int32, (items, LANES), 1)
    first_head = kv * group_size
    mine = (lane >= first_head) & (lane < first_head + group_size)
    ids = stack([ref[...].astype(jnp.float32) for ref in id_refs])
    place = place_ref[...]
    block_ids = lax.broadcasted_iota(jnp.int32, place.shape, 1)
    keys = [ref.at[b] for ref in (own_k, next_k) for b in range(blocks)]
    values = [ref.at[b] for ref in (own_v, next_v) for b in range(blocks)]
    hits = []
    for base in (where_ref[0], where_ref[1]):
        for b in range(blocks):
            target = jnp.sum(
                jnp.where(place == base + b, block_ids, 0).astype(jnp.float32), axis=1, keepdims=True
            )
            hits.append(jnp.max(jnp.where(ids == target, 1.0, 0.0), axis=1, keepdims=True))
    some = hits[0]
    for hit in hits[1:]:
        some = jnp.maximum(some, hit)

    def write(head, out):
        start = pl.multiple_of((first_head + head) * HD, HD)
        out = out.astype(jnp.bfloat16)
        for n, ref in enumerate(out_refs):
            ref[:, pl.ds(start, HD)] = out[n * kept : (n + 1) * kept]

    listed = jnp.zeros((items, LANES), jnp.float32)
    for n, hit in enumerate(hits):
        listed = jnp.where(lane == n, hit, listed)
    wide = (items, step * items)
    column = lax.broadcasted_iota(jnp.int32, wide, 1) % items
    spread = jnp.where(column == lax.broadcasted_iota(jnp.int32, wide, 0), 1.0, 0.0)
    listed = dot_tn(listed, spread)
    totals = jnp.ones((items, LANES), jnp.float32)
    for first in range(0, group_size, step):
        q = stack(
            [ref[:, h * HD : (h + 1) * HD] for h in range(first, first + step) for ref in q_refs]
        )
        acc = jnp.zeros((HD, step * items), jnp.float32)
        total = jnp.zeros((1, step * items), jnp.float32)
        for n, (key, value) in enumerate(zip(keys, values)):
            p = jnp.exp2(dot_nt(key[...], q) * (SCALE * LOG2E))
            here = dot_tn(value[...], p.astype(jnp.bfloat16))
            hit = listed[n : n + 1] > 0.0
            acc = jnp.where(hit, acc + here, acc)
            total = jnp.where(hit, total + jnp.sum(p, axis=0, keepdims=True), total)
        out = (acc / jnp.where(total > 0.0, total, 1.0)).T
        total = jnp.broadcast_to(total, (8, step * items)).T
        for n in range(step):
            rows = slice(n * items, (n + 1) * items)
            write(first + n, out[rows])
            totals = jnp.where(lane == first_head + first + n, total[rows, :1], totals)
    good = (totals > LOW) & (totals < HIGH)
    bad = jnp.max(jnp.where(good | (some == 0.0), 0.0, 1.0))
    logs = jnp.where((some > 0.0) & good, jnp.log(jnp.where(good, totals, 1.0)), NONE)
    logs_ref[...] = jnp.where(mine, logs, logs_ref[...])

    @pl.when(bad > 0.0)
    def _():
        @pl.loop(0, group_size)
        def _(head):
            start = pl.multiple_of(head * HD, HD)
            q = stack([ref[:, pl.ds(start, HD)] for ref in q_refs])
            top = jnp.full((items, 1), NONE, jnp.float32)
            for n, (hit, key) in enumerate(zip(hits, keys)):
                s = dot_nt(q, key[...])
                s_ref[n] = s
                here = jnp.max(s, axis=1, keepdims=True)
                top = jnp.where(hit > 0.0, jnp.maximum(top, here), top)
            acc = jnp.zeros((items, HD), jnp.float32)
            total = jnp.zeros((items, 1), jnp.float32)
            for n, (hit, value) in enumerate(zip(hits, values)):
                p = jnp.exp2((s_ref[n] - top) * (SCALE * LOG2E))
                p = jnp.where(hit > 0.0, p, 0.0)
                total += jnp.sum(p, axis=1, keepdims=True)
                acc += jnp.dot(p.astype(jnp.bfloat16), value[...], preferred_element_type=jnp.float32)
            safe = jnp.where(some > 0.0, total, 1.0)
            write(head, jnp.where(some > 0.0, acc / safe, 0.0))
            log = jnp.where(some > 0.0, top * SCALE + jnp.log(safe), NONE)
            logs_ref[...] = jnp.where(lane == first_head + head, log, logs_ref[...])

    @pl.when(kv == pl.num_programs(1) - 1)
    def _():
        heads = (out_refs[0].shape[1] - LANES) // HD
        parts = jnp.concatenate([x[:, :heads] for x in split3(logs_ref[...])], axis=1)
        pad = jnp.zeros((items, LANES - 3 * heads), jnp.bfloat16)
        parts = jnp.concatenate([parts, pad], axis=1)
        for n, ref in enumerate(out_refs):
            ref[:, heads * HD :] = parts[n * kept : (n + 1) * kept]


def attend_blocks(where, place, caches, group_size, queries, outs, after):
    pieces = len(queries)
    rows, columns = queries[0].shape
    blocks, tokens, kv_width = caches[0].shape
    kv_half = kv_width // HD // 2
    share = min(rows, 64)
    items = share * pieces
    cache_block = pl.BlockSpec((blocks, tokens, HD), lambda i, g, w: (0, 0, w[2] * kv_half + g))
    queries_block = pl.BlockSpec((share, group_size * HD), lambda i, g, w: (i, g))
    ids_block = pl.BlockSpec((share, LANES), lambda i, g, w: (i, columns // LANES - 1))
    return pl.pallas_call(
        functools.partial(block_kernel, pieces, outs, group_size, min(group_size, max(1, ROWS_STEP // items))),
        grid_spec=pltpu.PrefetchScalarGridSpec(
            num_scalar_prefetch=1,
            grid=(rows // share, kv_half),
            in_specs=[pl.BlockSpec(place.shape, lambda i, g, w: (0, 0))]
            + [queries_block] * pieces
            + [ids_block] * pieces
            + [cache_block] * 4
            + [pl.BlockSpec(memory_space=pl.ANY)] * len(after),
            out_specs=[pl.BlockSpec((items // outs, columns), lambda i, g, w: (i, 0))] * outs,
            scratch_shapes=[
                pltpu.VMEM((items, LANES), jnp.float32),
                pltpu.VMEM((2 * blocks, items, tokens), jnp.float32),
            ],
        ),
        out_shape=[jax.ShapeDtypeStruct((rows * pieces // outs, columns), jnp.bfloat16)] * outs,
        compiler_params=params(),
        cost_estimate=pl.CostEstimate(
            flops=rows * pieces * tokens * columns,
            bytes_accessed=4 * rows * pieces * columns,
            transcendentals=rows * pieces * columns,
        ),
    )(where, place, *queries, *queries, *caches, *after)


def suffix_kernel(group_size, lengths_ref, q_ref, k_ref, v_ref, pass_ref, where_ref, out_ref, log_ref, passed_ref):
    passed_ref[...] = pass_ref[...]
    rows_here, steps, width = q_ref.shape
    tokens = k_ref.shape[1]
    kv_here = k_ref.shape[2] // HD
    items = rows_here * steps
    span = rows_here * tokens
    half = width // HD // 2
    lane = lax.broadcasted_iota(jnp.int32, (items, LANES), 1)
    token = lax.broadcasted_iota(jnp.int32, (items, span), 1)
    item = lax.broadcasted_iota(jnp.int32, (items, span), 0)
    seen = jnp.zeros((items, span), jnp.float32)
    for r in range(rows_here):
        offset = token - r * tokens
        inside = (item // steps == r) & (offset >= 0) & (offset < lengths_ref[r] + item % steps)
        seen = jnp.where(inside, 1.0, seen)
    seen = jnp.concatenate([seen] * group_size, axis=0)
    logs = [jnp.zeros((items, LANES), jnp.float32)] * 2
    for g in range(kv_here):
        columns = slice(g * group_size * HD, (g + 1) * group_size * HD)
        q_all = flat(q_ref[:, :, columns]).astype(jnp.bfloat16)
        q = stack([q_all[:, n * HD : (n + 1) * HD] for n in range(group_size)])
        keys = k_ref[:, :, g * HD : (g + 1) * HD].reshape(span, HD)
        values = v_ref[:, :, g * HD : (g + 1) * HD].reshape(span, HD)
        s = jnp.where(seen > 0.0, dot_nt(q, keys), NONE)
        highest = jnp.max(s, axis=1, keepdims=True)
        p = jnp.exp2((s - highest) * (SCALE * LOG2E))
        p = jnp.where(seen > 0.0, p, 0.0)
        total = jnp.sum(p, axis=1, keepdims=True)
        out = jnp.dot(p.astype(jnp.bfloat16), values, preferred_element_type=jnp.float32) / total
        log = highest * SCALE + jnp.log(total)
        for n in range(group_size):
            h = g * group_size + n
            out_ref[:, h * HD : (h + 1) * HD] = out[n * items : (n + 1) * items]
            side = h // half
            logs[side] = jnp.where(lane == h % half, log[n * items : (n + 1) * items], logs[side])
    for side in range(2):
        log_ref[side] = logs[side]


def attend_suffix(lengths, queries, suffix_k, suffix_v, passing, where):
    rows, steps, width = queries.shape
    _, tokens, kv_width = suffix_k.shape
    items = rows * steps
    whole = lambda i, n: (0, 0, 0)
    return pl.pallas_call(
        functools.partial(suffix_kernel, width // kv_width),
        grid_spec=pltpu.PrefetchScalarGridSpec(
            num_scalar_prefetch=1,
            grid=(1,),
            in_specs=[pl.BlockSpec(x.shape, whole) for x in (queries, suffix_k, suffix_v)]
            + [pl.BlockSpec(passing.shape, lambda i, n: (0, 0)), ANY],
            out_specs=[
                pl.BlockSpec((items, width), lambda i, n: (0, 0)),
                pl.BlockSpec((2, items, LANES), whole),
                pl.BlockSpec(passing.shape, lambda i, n: (0, 0)),
            ],
        ),
        out_shape=(
            jax.ShapeDtypeStruct((items, width), jnp.float32),
            jax.ShapeDtypeStruct((2, items, LANES), jnp.float32),
            jax.ShapeDtypeStruct(passing.shape, passing.dtype),
        ),
        compiler_params=params(),
        cost_estimate=pl.CostEstimate(
            flops=16 * items * rows * tokens * width,
            bytes_accessed=4 * suffix_k.size + 6 * items * width,
            transcendentals=items * rows * tokens * width // HD,
        ),
    )(lengths, queries, suffix_k, suffix_v, passing, where)


def weigh(parts, items, heads):
    columns = heads * HD
    logs = []
    for ref, start in parts:
        x = ref[start : start + items, columns:].astype(jnp.float32)
        logs.append(x[:, :heads] + x[:, heads : 2 * heads] + x[:, 2 * heads : 3 * heads])
    return logs


def shares(logs):
    top = logs[0]
    for log in logs[1:]:
        top = jnp.maximum(top, log)
    factors = [jnp.exp(log - top) for log in logs]
    total = factors[0]
    for factor in factors[1:]:
        total += factor
    inverse = 1.0 / total
    return [factor * inverse for factor in factors], top + jnp.log(total)


def finish_kernel(sides, *refs):
    out_s_ref, log_s_ref, out_ref = refs[-3:]
    rows, steps, width = out_ref.shape
    items = rows * steps
    columns = width // 2
    heads = columns // HD
    core = lax.axis_index("ctx") % 2
    taken = 0
    for count, which in zip(sides, (core, 1 - core)):
        back_refs = refs[taken : taken + count]
        taken += count
        parts = [(ref, start) for ref in back_refs for start in range(0, ref.shape[0], items)]
        factors, _ = shares([log_s_ref[which][:, :heads]] + weigh(parts, items, heads))
        for h in range(heads):
            here = slice(h * HD, (h + 1) * HD)
            span = pl.ds(pl.multiple_of(which * columns + h * HD, HD), HD)
            acc = factors[0][:, h : h + 1] * out_s_ref[:, span]
            for factor, (ref, start) in zip(factors[1:], parts):
                acc += factor[:, h : h + 1] * ref[start : start + items, here].astype(jnp.float32)
            for row in range(rows):
                out_ref[row, :, span] = acc[row * steps : (row + 1) * steps].astype(jnp.bfloat16)


def finish(sides, out_s, log_s, shape):
    return pl.pallas_call(
        functools.partial(finish_kernel, [len(side) for side in sides]),
        out_shape=jax.ShapeDtypeStruct(shape, jnp.bfloat16),
        compiler_params=params(SMALL),
    )(*sides[0], *sides[1], out_s, log_s)


def local(queries, selected, placement, lengths, cache_k, cache_v, suffix_k, suffix_v):
    rows_here, steps, width = queries.shape
    size = lax.axis_size("ctx")
    blocks_here, _, kv_width = cache_k.shape
    group_size = width // kv_width
    items = rows_here * steps
    chips = size // 2

    def swap(x, bits):
        return lax.ppermute(x, "ctx", [(i, i ^ bits) for i in range(size)]) if bits else x

    own = lax.axis_index("ctx")
    where = jnp.stack([own * blocks_here, (own ^ 1) * blocks_here, own & 1]).astype(jnp.int32)
    place = placement.reshape(1, -1)
    caches = [cache_k, cache_v, swap(cache_k, 1), swap(cache_v, 1)]
    packed = pack(queries, selected)
    out_s, log_s, passed = attend_suffix(
        lengths, queries, suffix_k, suffix_v, packed[1], where
    )
    attend = functools.partial(attend_blocks, where, place, caches, group_size)
    if chips == 4:
        arrived = {n: swap(packed[n % 2], n) for n in (4, 5, 2, 3, 0)}
        arrived[1] = swap(passed, 1)
        arrived.update({n: swap(arrived[n - 2], 2) for n in (6, 7)})
        partial = attend([arrived[n] for n in range(size)], size, [log_s])
        back = {n: swap(partial[n], n) for n in (1, 3, 4, 5, 6, 7, 2, 0)}
        sides = [[back[n] for n in range(side, size, 2)] for side in range(2)]
    else:
        same = [[2 * z + core for z in range(chips)] for core in range(2)]
        chip = jnp.concatenate([packed[0], swap(passed, 1)], axis=0)
        every = lax.all_gather(chip, "ctx", axis=0, tiled=True, axis_index_groups=same)
        (partial,) = attend([every], 1, [log_s])
        back = lax.all_to_all(
            partial, "ctx", split_axis=0, concat_axis=0, tiled=True, axis_index_groups=same
        ).reshape(chips, 2, items, -1)
        sides = [[swap(back[:, n].reshape(chips * items, -1), n)] for n in range(2)]
    return finish(sides, out_s, log_s, queries.shape)


def solution(mesh):
    rows = P(("groups", "ctx"), None, "rows")
    in_specs = (
        rows,
        P(("groups", "ctx"), None, None),
        P("groups"),
        P(("groups", "ctx")),
        rows,
        rows,
        rows,
        rows,
    )
    return jax.shard_map(local, mesh=mesh, in_specs=in_specs, out_specs=rows, check_vma=False)
```
